32 devices in a mesh: row: 2 (over core), col: 16 (over z, y, x).
Axes of the slice: x: 2, y: 2, z: 4, core: 2. Of those that a mesh axis runs over, the one named last changes fastest.
Arguments:
- image_emb: bfloat16 [2560, 1152], P(('row', 'col')), may hold values from -6 to 6
- text_emb: bfloat16 [2560, 1152], P('col', 'row'), may hold values from -6 to 6
- image_valid: int32 [2560], P(('row', 'col')), may hold values from 0 to 4
- text_valid: int32 [2560], P('col'), may hold values from 0 to 4
- sample_count: int32 [1], replicated, may hold values from 2560 to 5119
- logit_scale: float32 [1], replicated, may hold values from 0.029462783 to 0.088388346
- logit_bias: float32 [1], replicated, may hold values from -4 to -1
- loss_grad: float32 [1], replicated, may hold values from 256 to 1024
Outputs:
- image_grad: bfloat16 [2560, 1152], P(('row', 'col'))
- text_grad: bfloat16 [2560, 1152], P('col', 'row')
The draws below stay inside these ranges and needn't reach their ends.
All inputs are finite; a program needn't handle non-finite values.
Results may differ from the reference program's by a relative error of at most 0.0042.
Values may be sent and summed in bfloat16 or wider, within the bound.
No kernel may reach another device: no remote copies, remote signals or barrier semaphores. Data moves between devices by JAX's collectives and lax.ppermute only.
A program may use at most 64 MiB of HBM per device.

```python
import jax
import jax.numpy as jnp
from jax import lax

D = 1152
PAIRS = 2560
N_ROW = 2


def set_ends(array, rng, smallest, high):
    longest = array.shape.index(max(array.shape))
    spots = []
    for shift in (0, 1):
        where = [jax.random.randint(jax.random.fold_in(rng, axis), (), 0, length) for axis, length in enumerate(array.shape)]
        where[longest] = (where[longest] + shift) % array.shape[longest]
        spots.append(tuple(where))
    return array.at[spots[0]].set(smallest).at[spots[1]].set(high)


def block_levels(key, dims, cuts, smallest, largest):
    def one(dim, parts):
        draws = jax.random.uniform(jax.random.fold_in(jax.random.fold_in(key, 6), dim), (parts,), jnp.float32, smallest / len(cuts), largest / len(cuts))
        return jnp.repeat(jnp.exp(draws), dims[dim] // parts).reshape((-1,) + (1,) * (len(dims) - dim - 1))

    factor_of = one(*cuts[0])
    for cut in cuts[1:]:
        factor_of = factor_of * one(*cut)
    return factor_of


def gaussian(rng, extent, width, bound, cuts=(), held_as=jnp.bfloat16):
    entries = width * jax.random.normal(rng, extent, jnp.float32)
    if cuts:
        entries = entries * block_levels(rng, extent, cuts, -0.22, 0.18)
    return jnp.clip(entries, -bound, bound).astype(held_as)


def setup_inputs(seed: int = 0) -> dict:
    key_list = jax.random.split(jax.random.key(seed), 9)
    image_emb = gaussian(key_list[0], (PAIRS, D), 1.0, 6.0, ((0, 32),))
    text_emb = gaussian(key_list[1], (PAIRS, D), 1.0, 6.0, ((0, 16), (1, 2)))
    image_valid = set_ends(jax.random.randint(key_list[2], (PAIRS,), 0, 5), jax.random.fold_in(key_list[2], 1), 0, 4).astype(jnp.int32)
    text_valid = set_ends(jax.random.randint(key_list[3], (PAIRS,), 0, 5), jax.random.fold_in(key_list[3], 1), 0, 4).astype(jnp.int32)
    sample_count = jax.random.randint(key_list[4], (1,), PAIRS, 2 * PAIRS).astype(jnp.int32)
    logit_scale = jnp.clip(jax.random.uniform(key_list[5], (1,), jnp.float32, 0.029462783, 0.088388346), 0.029462783, 0.088388346)
    logit_bias = jnp.clip(jax.random.uniform(key_list[6], (1,), jnp.float32, -4.0, -1.0), -4.0, -1.0)
    loss_grad = jnp.clip(jax.random.uniform(key_list[7], (1,), jnp.float32, 256.0, 1024.0), 256.0, 1024.0)
    return {"image_emb": image_emb, "text_emb": text_emb, "image_valid": image_valid, "text_valid": text_valid, "sample_count": sample_count, "logit_scale": logit_scale, "logit_bias": logit_bias, "loss_grad": loss_grad}


def reference(image_emb, text_emb, image_valid, text_valid, sample_count, logit_scale, logit_bias, loss_grad):
    images = image_emb.astype(jnp.float32)
    texts = text_emb.astype(jnp.float32)
    weight_image = image_valid.astype(jnp.float32)
    weight_text = text_valid.astype(jnp.float32)
    factor = loss_grad[0] * logit_scale[0] / sample_count[0].astype(jnp.float32)
    block_size = PAIRS // N_ROW
    text_ids = jnp.arange(PAIRS, dtype=jnp.int32)

    def advance(text_total, index_now):
        first_row = (index_now * block_size).astype(jnp.int32)
        image_block = lax.dynamic_slice_in_dim(images, first_row, block_size, 0)
        weight_block = lax.dynamic_slice_in_dim(weight_image, first_row, block_size, 0)
        logits = jnp.dot(image_block, texts.T) * logit_scale[0] + logit_bias[0]
        row_ids = first_row + jnp.arange(block_size, dtype=jnp.int32)
        label_sign = jnp.where(row_ids[:, None] == text_ids[None, :], 1.0, -1.0).astype(jnp.float32)
        coefficient = (-factor * label_sign * jax.nn.sigmoid(-label_sign * logits)
                       * weight_block[:, None] * weight_text[None, :]).astype(jnp.bfloat16)
        coefficient = lax.optimization_barrier(coefficient).astype(jnp.float32)
        image_part = jnp.dot(coefficient, texts).astype(jnp.bfloat16)
        text_total = text_total + jnp.dot(coefficient.T, image_block)
        return text_total, image_part

    text_total, image_parts = lax.scan(advance, jnp.zeros((PAIRS, D), jnp.float32),
                                       jnp.arange(N_ROW, dtype=jnp.int32))
    return image_parts.reshape(PAIRS, D), text_total.astype(jnp.bfloat16)
```

```python
import functools

import jax
import jax.numpy as jnp
from jax import lax
from jax.experimental import pallas as pl
from jax.experimental.pallas import tpu as pltpu
from jax.sharding import PartitionSpec as P

SPARE = 8


def hop(block, image_bit, text_bit):
    count = lax.axis_size("col")
    route = [(c, c ^ image_bit) for c in range(count)]
    route += [(count + c, count + (c ^ text_bit)) for c in range(count)]
    return lax.ppermute(block, ("row", "col"), route)


def swap(block):
    return lax.ppermute(block, "row", [(0, 1), (1, 0)])


def pack_kernel(row_ref, image_ref, text_ref, other_image_ref, other_text_ref, image_valid_ref,
                other_valid_ref, text_valid_ref, out_ref):
    half, width = image_ref.shape
    count, part = text_ref.shape
    lanes = 256 if count <= 256 else width

    def put_valid(pieces):
        used = sum(piece.shape[1] for piece in pieces)
        pieces = pieces + [jnp.zeros((1, lanes - used), jnp.float32)]
        line = jnp.concatenate(pieces, axis=1)
        out_ref[count:, :lanes] = jnp.broadcast_to(line, (SPARE, lanes)).astype(out_ref.dtype)

    @pl.when(row_ref[0] == 0)
    def _():
        out_ref[:half] = image_ref[...]
        out_ref[half:count] = other_image_ref[...]
        put_valid([image_valid_ref[...].astype(jnp.float32), other_valid_ref[...].astype(jnp.float32)])

    @pl.when(row_ref[0] != 0)
    def _():
        out_ref[:count, :part] = other_text_ref[...]
        out_ref[:count, part:] = text_ref[...]
        put_valid([text_valid_ref[...].astype(jnp.float32)])


def partial_kernel(kinds, place_ref, scalar_ref, sample_ref, mine_ref, *refs):
    others, out_ref = refs[:-1], refs[-1]
    count = others[0].shape[0] - SPARE
    scale, bias = scalar_ref[0], scalar_ref[1]
    factor = scalar_ref[2] * scale / sample_ref[0].astype(jnp.float32)
    mine = mine_ref[...]
    line = mine[count:, :256].astype(jnp.float32)[:1, :count]
    at = lax.broadcasted_iota(jnp.int32, (count, count), 0)
    to = lax.broadcasted_iota(jnp.int32, (count, count), 1)
    weight = jnp.sum(jnp.where(at == to, line, 0.0), axis=1, keepdims=True)
    my_id = lax.broadcasted_iota(jnp.int32, (count, 1), 0)
    my_id = my_id + place_ref[0] + jnp.where(my_id >= count // 2, place_ref[1], 0)
    parts = []
    for n, ref in enumerate(others):
        other = ref[...]
        logits = lax.dot_general(mine[:count], other[:count], (((1,), (1,)), ((), ())),
                                 preferred_element_type=jnp.float32)
        logits = logits * scale + bias
        other_id = lax.broadcasted_iota(jnp.int32, (1, count), 1)
        other_id = other_id + place_ref[3 + n] + jnp.where(other_id >= count // 2, place_ref[2], 0)
        match = my_id == other_id
        rate = 1.0 / (1.0 + jnp.exp(jnp.where(match, logits, -logits)))
        signed = jnp.where(match, -factor, factor) * rate
        other_weight = other[count:, :256].astype(jnp.float32)[:1, :count]
        parts.append((signed * weight * other_weight).astype(jnp.bfloat16))
    coefficient = jnp.concatenate(parts, axis=1)
    block = jnp.concatenate([ref[:count] for ref in others], axis=0)
    total = jnp.dot(coefficient, block, preferred_element_type=jnp.float32)
    out_ref[...] = total.astype(out_ref.dtype)


def call(kernel, out_shape, smem, *arrays):
    return pl.pallas_call(
        kernel,
        out_shape=out_shape,
        in_specs=[pl.BlockSpec(memory_space=pltpu.SMEM)] * smem
        + [pl.BlockSpec(memory_space=pltpu.VMEM)] * (len(arrays) - smem),
        out_specs=pl.BlockSpec(memory_space=pltpu.VMEM),
        compiler_params=pltpu.CompilerParams(vmem_limit_bytes=24 * 1024 * 1024),
    )(*arrays)


def pair_body(
    image_emb, text_emb, image_valid, text_valid, sample_count, logit_scale, logit_bias, loss_grad
):
    half, width = image_emb.shape
    count, part = text_emb.shape
    col_count = lax.axis_size("col")
    col = lax.axis_index("col")
    row = lax.axis_index("row")
    top = col_count // 2
    near = (1, 2)
    far = (top, top // 2)
    near_mask = jnp.where(row == 0, *near)
    far_mask = jnp.where(row == 0, *far)
    near_other = jnp.where(row == 0, *near[::-1])
    far_other = jnp.where(row == 0, *far[::-1])

    other_image = lax.ppermute(image_emb, "row", [(1, 0)])
    other_text = lax.ppermute(text_emb, "row", [(0, 1)])
    other_valid = lax.ppermute(image_valid, "row", [(1, 0)])
    block_shape = jax.ShapeDtypeStruct((count + SPARE, width), jnp.bfloat16)
    own = call(pack_kernel, block_shape, 1, row[None], image_emb, text_emb, other_image, other_text,
               image_valid[None], other_valid[None], text_valid[None])
    far_block = hop(own, *far)
    near_block = hop(own, *near)
    both_block = hop(far_block, *near)
    own_b, near_b, far_b, both_b = swap(own), swap(near_block), swap(far_block), swap(both_block)
    others = (own_b, near_b, far_b, both_b)

    other_cols = jnp.stack([col, col ^ near_other, col ^ far_other, col ^ near_other ^ far_other])
    other_first = other_cols * jnp.where(row == 0, count, half)
    jump = (col_count - 1) * half
    my_jump, other_jump = jnp.where(row == 0, jump, 0), jnp.where(row == 0, 0, jump)
    scalars = jnp.concatenate([logit_scale, logit_bias, loss_grad])

    def partial(mine, mask, dtype):
        first = (col ^ mask) * jnp.where(row == 0, half, count)
        place = jnp.concatenate([jnp.stack([first, my_jump, other_jump]), other_first])
        return call(functools.partial(partial_kernel, None), jax.ShapeDtypeStruct((count, width), dtype), 3,
                    place, scalars, sample_count, mine, *others)

    both_sum = partial(both_block, near_mask ^ far_mask, jnp.bfloat16)
    both_in = hop(both_sum, *near)
    near_sum = partial(near_block, near_mask, jnp.bfloat16)
    far_sum = partial(far_block, far_mask, jnp.float32)
    far_out = (far_sum + both_in.astype(jnp.float32)).astype(jnp.bfloat16)
    far_in = hop(far_out, *far)
    near_in = hop(near_sum, *near)
    own_sum = partial(own, 0, jnp.float32)
    total = own_sum + near_in.astype(jnp.float32) + far_in.astype(jnp.float32)
    total = total.astype(jnp.bfloat16)
    image_back = lax.ppermute(total[half:], "row", [(0, 1)])
    text_back = lax.ppermute(total[:, :part], "row", [(1, 0)])
    image_grad = jnp.where(row == 0, total[:half], image_back)
    text_grad = jnp.where(row == 0, text_back, total[:, part:])
    return image_grad, text_grad


def partner(block, axis, distance):
    count = lax.axis_size(axis)
    route = []
    for low in range(count):
        high = low | 1 << distance
        if high != low and high < count:
            route += [(low, high), (high, low)]
    return lax.ppermute(block, axis, route)


def coefficients(
    image_rows, valid_rows, row_ids, texts, weight_text, text_ids, factor, logit_scale, logit_bias
):
    logits = lax.dot_general(
        image_rows, texts, (((1,), (1,)), ((), ())), preferred_element_type=jnp.float32
    )
    logits = logits * logit_scale[0] + logit_bias[0]
    label_sign = jnp.where(row_ids[:, None] == text_ids[None, :], 1.0, -1.0).astype(jnp.float32)
    weights = valid_rows.astype(jnp.float32)[:, None] * weight_text[None, :]
    return (-factor * label_sign * jax.nn.sigmoid(-label_sign * logits) * weights).astype(
        jnp.bfloat16
    )


def text_part(coefficient, image_rows):
    return lax.dot_general(
        coefficient, image_rows, (((0,), (0,)), ((), ())), preferred_element_type=jnp.float32
    )


def body(
    image_emb, text_emb, image_valid, text_valid, sample_count, logit_scale, logit_bias, loss_grad
):
    text_block = lax.all_gather(text_emb, "row", axis=1, tiled=True)
    per_device = image_emb.shape[0]
    col_count = lax.axis_size("col")
    col_index = lax.axis_index("col")
    row_index = lax.axis_index("row")
    text_count = text_block.shape[0]
    factor = loss_grad[0] * logit_scale[0] / sample_count[0].astype(jnp.float32)
    valid_wire = image_valid.astype(jnp.bfloat16)
    parity = col_index % 2
    bit_count = col_count.bit_length() - 1
    text_wire = text_valid.astype(jnp.bfloat16)
    other_texts, other_valid = partner((text_block, text_wire), "col", 0)
    own_first = parity == 0
    texts = jnp.where(
        own_first,
        jnp.concatenate([text_block, other_texts], 0),
        jnp.concatenate([other_texts, text_block], 0),
    )
    text_weights = jnp.where(
        own_first,
        jnp.concatenate([text_wire, other_valid], 0),
        jnp.concatenate([other_valid, text_wire], 0),
    ).astype(jnp.float32)
    text_ids = (col_index - parity) * text_count + jnp.arange(2 * text_count, dtype=jnp.int32)
    image_rows, valid_rows = (image_emb, valid_wire)
    for bit in range(1, bit_count):
        other_rows, other_counts = partner((image_rows, valid_rows), "col", bit)
        lower = col_index >> bit & 1 == 0
        image_rows = jnp.where(
            lower,
            jnp.concatenate([image_rows, other_rows], 0),
            jnp.concatenate([other_rows, image_rows], 0),
        )
        valid_rows = jnp.where(
            lower,
            jnp.concatenate([valid_rows, other_counts], 0),
            jnp.concatenate([other_counts, valid_rows], 0),
        )
    positions = jnp.arange(image_rows.shape[0], dtype=jnp.int32)
    row_ids = (
        row_index * col_count + 2 * (positions // per_device) + parity
    ) * per_device + positions % per_device
    coefficient = coefficients(
        image_rows,
        valid_rows,
        row_ids,
        texts,
        text_weights,
        text_ids,
        factor,
        logit_scale,
        logit_bias,
    )
    partial_image = jnp.dot(coefficient, texts, preferred_element_type=jnp.float32)
    for bit in range(bit_count - 1, 0, -1):
        half = partial_image.shape[0] // 2
        upper = col_index >> bit & 1 == 1
        send = jnp.where(upper, partial_image[:half], partial_image[half:])
        keep = jnp.where(upper, partial_image[half:], partial_image[:half])
        partial_image = keep + partner(send, "col", bit)
    partial_text = text_part(coefficient, image_rows)
    odd = parity == 1
    send_text = jnp.where(odd, partial_text[:text_count], partial_text[text_count:])
    keep_text = jnp.where(odd, partial_text[text_count:], partial_text[:text_count])
    text_partial = keep_text + partner(send_text, "col", 0)
    text_grad = lax.psum_scatter(text_partial, "row", scatter_dimension=1, tiled=True)
    return (partial_image.astype(jnp.bfloat16), text_grad.astype(jnp.bfloat16))


def solution(mesh):
    in_specs = (
        P(("row", "col"), None),
        P("col", "row"),
        P(("row", "col")),
        P("col"),
        P(),
        P(),
        P(),
        P(),
    )
    out_specs = (P(("row", "col"), None), P("col", "row"))
    paired = mesh.shape["row"] == 2 and mesh.shape["col"] == 16
    run = pair_body if paired else body
    return jax.shard_map(run, mesh=mesh, in_specs=in_specs, out_specs=out_specs, check_vma=False)
```

```python
import functools

import jax
import jax.numpy as jnp
from jax import lax
from jax.experimental import pallas as pl
from jax.experimental.pallas import tpu as pltpu
from jax.sharding import PartitionSpec as P

SPARE = 8
LINE = 256


def hop(block, image_bit, text_bit, across=False):
    count = lax.axis_size("col")
    turn = count if across else 0
    route = [(c, turn + (c ^ image_bit)) for c in range(count)]
    route += [(count + c, count - turn + (c ^ text_bit)) for c in range(count)]
    return lax.ppermute(block, ("row", "col"), route)


def swap(block):
    return lax.ppermute(block, "row", [(0, 1), (1, 0)])


def masks(count, row):
    top = count // 2
    near, far = (1, 2), (top, top // 2)
    if row is None:
        return near, far
    return tuple(jnp.where(row == 0, *pair) for pair in (near, far, near[::-1], far[::-1]))


def put_line(ref, *pieces):
    pieces = [piece.astype(jnp.float32) for piece in pieces]
    pieces += [jnp.zeros((1, LINE - sum(piece.shape[1] for piece in pieces)), jnp.float32)]
    line = jnp.broadcast_to(jnp.concatenate(pieces, axis=1), (SPARE, LINE))
    ref[ref.shape[0] - SPARE :, :LINE] = line.astype(ref.dtype)


def put_texts(ref, text_ref):
    half, part = text_ref.shape[0] // 2, text_ref.shape[1]
    ref[:half, :part] = text_ref[:half]
    ref[:half, part:] = text_ref[half:]


def first_kernel(spot_ref, image_ref, text_ref, image_valid_ref, text_valid_ref, mine_ref, give_ref):
    half = image_ref.shape[0]

    def fill(image_to, text_to):
        image_to[:half] = image_ref[...]
        put_line(image_to, image_valid_ref[...])
        put_texts(text_to, text_ref)
        put_line(text_to, text_valid_ref[...])

    @pl.when(spot_ref[0] == 0)
    def _():
        fill(mine_ref, give_ref)

    @pl.when(spot_ref[0] != 0)
    def _():
        fill(give_ref, mine_ref)


def unpack(pair, texts, out_ref, start):
    one, two = pair
    half, part = one.shape[0] - SPARE, one.shape[1] // 2

    @pl.when(texts)
    def _():
        out_ref[start : start + half, :part] = two[:half, :part]
        out_ref[start : start + half, part:] = one[:half, :part]
        out_ref[start + half : start + 2 * half, :part] = two[:half, part:]
        out_ref[start + half : start + 2 * half, part:] = one[:half, part:]

    @pl.when(jnp.logical_not(texts))
    def _():
        out_ref[start : start + half] = one[:half]
        out_ref[start + half : start + 2 * half] = two[:half]


def counts(pair, texts):
    one, two = pair
    half = one.shape[0] - SPARE
    line_one = one[half:, :LINE].astype(jnp.float32)[:1]
    line_two = two[half:, :LINE].astype(jnp.float32)[:1]
    images = jnp.concatenate([line_one[:, :half], line_two[:, :half]], axis=1)
    return jnp.where(texts, line_one[:, : 2 * half], images)


def upright(line):
    size = line.shape[1]
    at = lax.broadcasted_iota(jnp.int32, (size, size), 0)
    to = lax.broadcasted_iota(jnp.int32, (size, size), 1)
    return jnp.sum(jnp.where(at == to, line, 0.0), axis=1, keepdims=True)


def sample_ids(col, texts, half, cols, axis):
    shape = (2 * half, 1) if axis == 0 else (1, 2 * half)
    at = lax.broadcasted_iota(jnp.int32, shape, axis)
    jump = jnp.where(texts, 0, (cols - 1) * half)
    first = col * jnp.where(texts, 2 * half, half)
    return at + first + jnp.where(at >= half, jump, 0)


def coefficients_of(cols, spot_ref, scale_ref, bias_ref, grad_ref, sample_ref, mine, others, my_sets, other_sets):
    row, col = spot_ref[0], spot_ref[1]
    my_texts, other_texts = row != 0, row == 0
    near, far, other_near, other_far = masks(cols, row)
    my_masks = {"own": 0, "near": near, "far": far, "both": near ^ far}
    other_masks = {"own": 0, "near": other_near, "far": other_far, "both": other_near ^ other_far}
    half = my_sets[0][1][0].shape[0] - SPARE
    scale, bias = scale_ref[0], bias_ref[0]
    factor = grad_ref[0] * scale / sample_ref[0].astype(jnp.float32)
    my_ids = jnp.concatenate([sample_ids(col ^ my_masks[k], my_texts, half, cols, 0) for k, _ in my_sets], axis=0)
    other_ids = jnp.concatenate(
        [sample_ids(col ^ other_masks[k], other_texts, half, cols, 1) for k, _ in other_sets], axis=1)
    my_weights = jnp.concatenate([upright(counts(pair, my_texts)) for _, pair in my_sets], axis=0)
    other_weights = factor * jnp.concatenate([counts(pair, other_texts) for _, pair in other_sets], axis=1)
    logits = lax.dot_general(mine, others, (((1,), (1,)), ((), ())), preferred_element_type=jnp.float32)
    logits = logits * scale + bias
    match = my_ids == other_ids
    rate = 1.0 / (1.0 + jnp.exp(jnp.where(match, logits, -logits)))
    return (jnp.where(match, -rate, rate) * my_weights * other_weights).astype(jnp.bfloat16)


def pairs(refs):
    return [refs[n : n + 2] for n in range(0, len(refs), 2)]


THREE = ("own", "near", "far")


def early_kernel(cols, spot_ref, scale_ref, bias_ref, grad_ref, sample_ref, *refs):
    mine_pairs, other_pairs = pairs(refs[:6]), pairs(refs[6:12])
    mine_ref, others_ref, total_ref = refs[12:]
    texts = spot_ref[0] != 0
    size = 2 * (refs[0].shape[0] - SPARE)
    for n in range(3):
        unpack(mine_pairs[n], texts, mine_ref, n * size)
        unpack(other_pairs[n], jnp.logical_not(texts), others_ref, n * size)
    others = others_ref[...]
    coefficient = coefficients_of(cols, spot_ref, scale_ref, bias_ref, grad_ref, sample_ref, mine_ref[...], others,
                                  list(zip(THREE, mine_pairs)), list(zip(THREE, other_pairs)))
    total_ref[...] = jnp.dot(coefficient, others, preferred_element_type=jnp.float32)


def both_kernel(cols, spot_ref, scale_ref, bias_ref, grad_ref, sample_ref, *refs):
    mine_pair, other_pairs = refs[:2], pairs(refs[2:8])
    others_ref, mine_ref, total_ref = refs[8:]
    unpack(mine_pair, spot_ref[0] != 0, mine_ref, 0)
    others = others_ref[...]
    coefficient = coefficients_of(cols, spot_ref, scale_ref, bias_ref, grad_ref, sample_ref, mine_ref[...], others,
                                  [("both", mine_pair)], list(zip(THREE, other_pairs)))
    total_ref[...] = jnp.dot(coefficient, others, preferred_element_type=jnp.float32)


def pack_sum(total, texts, stay_ref, cross_ref, start=0):
    half, part = total.shape[0] // 2, total.shape[1] // 2
    rows = slice(start, start + half)

    @pl.when(texts)
    def _():
        stay_ref[rows, :part] = total[:half, part:].astype(stay_ref.dtype)
        stay_ref[rows, part:] = total[half:, part:].astype(stay_ref.dtype)
        cross_ref[:half, :part] = total[:half, :part].astype(cross_ref.dtype)
        cross_ref[:half, part:] = total[half:, :part].astype(cross_ref.dtype)

    @pl.when(jnp.logical_not(texts))
    def _():
        stay_ref[rows] = total[:half].astype(stay_ref.dtype)
        cross_ref[:half] = total[half:].astype(cross_ref.dtype)


def late_kernel(cols, spot_ref, scale_ref, bias_ref, grad_ref, sample_ref, *refs):
    mine_pair, other_pair = refs[:2], refs[2:4]
    mine_ref, total_ref = refs[4:6]
    others_ref, stay_ref, cross_ref = refs[6:]
    texts = spot_ref[0] != 0
    unpack(other_pair, jnp.logical_not(texts), others_ref, 0)
    others = others_ref[...]
    coefficient = coefficients_of(cols, spot_ref, scale_ref, bias_ref, grad_ref, sample_ref, mine_ref[...], others,
                                  [("both", mine_pair)], [("both", other_pair)])
    total = total_ref[...] + jnp.dot(coefficient, others, preferred_element_type=jnp.float32)
    pack_sum(total, texts, stay_ref, cross_ref)


def rest_kernel(cols, spot_ref, scale_ref, bias_ref, grad_ref, sample_ref, *refs):
    mine_pairs, other_pair = pairs(refs[:6]), refs[6:8]
    mine_ref, others_ref, total_ref = refs[8:11]
    own_stay, own_cross, near_ref, far_stay, far_cross = refs[11:]
    texts = spot_ref[0] != 0
    others = others_ref[...]
    coefficient = coefficients_of(cols, spot_ref, scale_ref, bias_ref, grad_ref, sample_ref, mine_ref[...], others,
                                  list(zip(THREE, mine_pairs)), [("both", other_pair)])
    total = total_ref[...] + jnp.dot(coefficient, others, preferred_element_type=jnp.float32)
    size = total.shape[0] // 3
    pack_sum(total[2 * size :], texts, far_stay, far_cross)
    pack_sum(total[size : 2 * size], texts, near_ref, near_ref, size // 2)
    pack_sum(total[:size], texts, own_stay, own_cross)


def last_kernel(spot_ref, stay_ref, crossed_ref, stay_in_ref, cross_in_ref, image_ref, text_ref):
    half, part = text_ref.shape[0] // 2, text_ref.shape[1]
    stay = (stay_ref[...] + stay_in_ref[...].astype(jnp.float32)).astype(image_ref.dtype)
    crossed = (crossed_ref[...] + cross_in_ref[...].astype(jnp.float32)).astype(image_ref.dtype)

    def put(images, texts):
        image_ref[...] = images
        text_ref[:half] = texts[:, :part]
        text_ref[half:] = texts[:, part:]

    @pl.when(spot_ref[0] == 0)
    def _():
        put(stay, crossed)

    @pl.when(spot_ref[0] != 0)
    def _():
        put(crossed, stay)


def call(kernel, out_shape, smem, *arrays, flops=0):
    size = sum(a.size * a.dtype.itemsize for a in (*arrays, *jax.tree.leaves(out_shape)))
    return pl.pallas_call(
        kernel,
        out_shape=out_shape,
        in_specs=[pl.BlockSpec(memory_space=pltpu.SMEM)] * smem
        + [pl.BlockSpec(memory_space=pltpu.VMEM)] * (len(arrays) - smem),
        out_specs=jax.tree.map(lambda _: pl.BlockSpec(memory_space=pltpu.VMEM), out_shape),
        compiler_params=pltpu.CompilerParams(vmem_limit_bytes=24 * 1024 * 1024),
        cost_estimate=pl.CostEstimate(flops=flops, bytes_accessed=size, transcendentals=0),
    )(*arrays)


def pair_body(
    image_emb, text_emb, image_valid, text_valid, sample_count, logit_scale, logit_bias, loss_grad
):
    half, width = image_emb.shape
    size = 2 * half
    cols = lax.axis_size("col")
    spot = jnp.stack([lax.axis_index("row"), lax.axis_index("col")]).astype(jnp.int32)
    near, far = masks(cols, None)
    scalars = (spot, logit_scale, logit_bias, loss_grad, sample_count)

    def shape(rows, dtype):
        return jax.ShapeDtypeStruct((rows, width), dtype)

    bf16, f32 = jnp.bfloat16, jnp.float32
    sent = shape(half + SPARE, bf16)
    own_a, give = call(first_kernel, (sent, sent), 1, spot, image_emb, text_emb, image_valid[None],
                       text_valid[None])
    far_a = hop(own_a, *far)
    own_b = swap(give)
    far_b = hop(own_b, *far)
    near_a = hop(own_a, *near)
    near_b = hop(own_b, *near)
    both_a = hop(far_a, *near)
    both_b = hop(far_b, *near)
    mine = (own_a, own_b, near_a, near_b, far_a, far_b)
    others = (swap(own_a), give, swap(near_a), swap(near_b), swap(far_a), swap(far_b))
    both = (both_a, both_b)
    other_both = (swap(both_a), swap(both_b))

    pair_flops = 4 * size * size * width
    mine_rows, other_rows, early = call(
        functools.partial(early_kernel, cols), (shape(3 * size, bf16), shape(3 * size, bf16), shape(3 * size, f32)),
        5, *scalars, *mine, *others, flops=9 * pair_flops)
    both_rows, both_early = call(
        functools.partial(both_kernel, cols), (shape(size, bf16), shape(size, f32)), 5, *scalars, *both, *others,
        other_rows, flops=3 * pair_flops)
    other_late, late_stay, late_cross = call(
        functools.partial(late_kernel, cols), (shape(size, bf16), shape(half, bf16), shape(half, bf16)), 5, *scalars,
        *both, *other_both, both_rows, both_early, flops=pair_flops)
    in_cross = hop(late_cross, *near)
    in_stay = hop(late_stay, *near)
    own_stay, own_cross, near_out, far_stay, far_cross = call(
        functools.partial(rest_kernel, cols),
        (shape(half, f32), shape(half, f32), shape(size, bf16), shape(half, f32), shape(half, f32)), 5, *scalars,
        *mine, *other_both, mine_rows, other_late, early, flops=3 * pair_flops)
    far_cross = hop((far_cross + in_cross.astype(f32)).astype(bf16), *far, across=True)
    near_in = hop(near_out, *near)
    far_stay = hop((far_stay + in_stay.astype(f32)).astype(bf16), *far)
    crossed = swap(own_cross + near_in[:half].astype(f32))
    stay = own_stay + near_in[half:].astype(f32)
    return call(last_kernel, (shape(half, bf16), jax.ShapeDtypeStruct(text_emb.shape, bf16)), 1, spot, stay, crossed,
                far_stay, far_cross)


def partner(block, axis, distance):
    count = lax.axis_size(axis)
    route = []
    for low in range(count):
        high = low | 1 << distance
        if high != low and high < count:
            route += [(low, high), (high, low)]
    return lax.ppermute(block, axis, route)


def coefficients(
    image_rows, valid_rows, row_ids, texts, weight_text, text_ids, factor, logit_scale, logit_bias
):
    logits = lax.dot_general(
        image_rows, texts, (((1,), (1,)), ((), ())), preferred_element_type=jnp.float32
    )
    logits = logits * logit_scale[0] + logit_bias[0]
    label_sign = jnp.where(row_ids[:, None] == text_ids[None, :], 1.0, -1.0).astype(jnp.float32)
    weights = valid_rows.astype(jnp.float32)[:, None] * weight_text[None, :]
    return (-factor * label_sign * jax.nn.sigmoid(-label_sign * logits) * weights).astype(
        jnp.bfloat16
    )


def text_part(coefficient, image_rows):
    return lax.dot_general(
        coefficient, image_rows, (((0,), (0,)), ((), ())), preferred_element_type=jnp.float32
    )


def body(
    image_emb, text_emb, image_valid, text_valid, sample_count, logit_scale, logit_bias, loss_grad
):
    text_block = lax.all_gather(text_emb, "row", axis=1, tiled=True)
    per_device = image_emb.shape[0]
    col_count = lax.axis_size("col")
    col_index = lax.axis_index("col")
    row_index = lax.axis_index("row")
    text_count = text_block.shape[0]
    factor = loss_grad[0] * logit_scale[0] / sample_count[0].astype(jnp.float32)
    valid_wire = image_valid.astype(jnp.bfloat16)
    parity = col_index % 2
    bit_count = col_count.bit_length() - 1
    text_wire = text_valid.astype(jnp.bfloat16)
    other_texts, other_valid = partner((text_block, text_wire), "col", 0)
    own_first = parity == 0
    texts = jnp.where(
        own_first,
        jnp.concatenate([text_block, other_texts], 0),
        jnp.concatenate([other_texts, text_block], 0),
    )
    text_weights = jnp.where(
        own_first,
        jnp.concatenate([text_wire, other_valid], 0),
        jnp.concatenate([other_valid, text_wire], 0),
    ).astype(jnp.float32)
    text_ids = (col_index - parity) * text_count + jnp.arange(2 * text_count, dtype=jnp.int32)
    image_rows, valid_rows = (image_emb, valid_wire)
    for bit in range(1, bit_count):
        other_rows, other_counts = partner((image_rows, valid_rows), "col", bit)
        lower = col_index >> bit & 1 == 0
        image_rows = jnp.where(
            lower,
            jnp.concatenate([image_rows, other_rows], 0),
            jnp.concatenate([other_rows, image_rows], 0),
        )
        valid_rows = jnp.where(
            lower,
            jnp.concatenate([valid_rows, other_counts], 0),
            jnp.concatenate([other_counts, valid_rows], 0),
        )
    positions = jnp.arange(image_rows.shape[0], dtype=jnp.int32)
    row_ids = (
        row_index * col_count + 2 * (positions // per_device) + parity
    ) * per_device + positions % per_device
    coefficient = coefficients(
        image_rows,
        valid_rows,
        row_ids,
        texts,
        text_weights,
        text_ids,
        factor,
        logit_scale,
        logit_bias,
    )
    partial_image = jnp.dot(coefficient, texts, preferred_element_type=jnp.float32)
    for bit in range(bit_count - 1, 0, -1):
        half = partial_image.shape[0] // 2
        upper = col_index >> bit & 1 == 1
        send = jnp.where(upper, partial_image[:half], partial_image[half:])
        keep = jnp.where(upper, partial_image[half:], partial_image[:half])
        partial_image = keep + partner(send, "col", bit)
    partial_text = text_part(coefficient, image_rows)
    odd = parity == 1
    send_text = jnp.where(odd, partial_text[:text_count], partial_text[text_count:])
    keep_text = jnp.where(odd, partial_text[text_count:], partial_text[:text_count])
    text_partial = keep_text + partner(send_text, "col", 0)
    text_grad = lax.psum_scatter(text_partial, "row", scatter_dimension=1, tiled=True)
    return (partial_image.astype(jnp.bfloat16), text_grad.astype(jnp.bfloat16))


def solution(mesh):
    in_specs = (
        P(("row", "col"), None),
        P("col", "row"),
        P(("row", "col")),
        P("col"),
        P(),
        P(),
        P(),
        P(),
    )
    out_specs = (P(("row", "col"), None), P("col", "row"))
    paired = mesh.shape["row"] == 2 and mesh.shape["col"] == 16
    run = pair_body if paired else body
    return jax.shard_map(run, mesh=mesh, in_specs=in_specs, out_specs=out_specs, check_vma=False)
```

```python
import functools

import jax
import jax.numpy as jnp
from jax import lax
from jax.experimental import pallas as pl
from jax.experimental.pallas import tpu as pltpu
from jax.sharding import PartitionSpec as P

SPARE = 8
LINE = 256


def hop(block, image_bit, text_bit, across=False):
    count = lax.axis_size("col")
    turn = count if across else 0
    route = [(c, turn + (c ^ image_bit)) for c in range(count)]
    route += [(count + c, count - turn + (c ^ text_bit)) for c in range(count)]
    return lax.ppermute(block, ("row", "col"), route)


def swap(block):
    return lax.ppermute(block, "row", [(0, 1), (1, 0)])


def masks(count, row):
    top = count // 2
    near, far = (1, 2), (top, top // 2)
    if row is None:
        return near, far
    return tuple(jnp.where(row == 0, *pair) for pair in (near, far, near[::-1], far[::-1]))


def put_line(ref, *pieces):
    pieces = [piece.astype(jnp.float32) for piece in pieces]
    pieces += [jnp.zeros((1, LINE - sum(piece.shape[1] for piece in pieces)), jnp.float32)]
    line = jnp.broadcast_to(jnp.concatenate(pieces, axis=1), (SPARE, LINE))
    ref[ref.shape[0] - SPARE :, :LINE] = line.astype(ref.dtype)


def put_texts(ref, text_ref):
    half, part = text_ref.shape[0] // 2, text_ref.shape[1]
    ref[:half, :part] = text_ref[:half]
    ref[:half, part:] = text_ref[half:]


def first_kernel(spot_ref, image_ref, text_ref, image_valid_ref, text_valid_ref, mine_ref, give_ref, texts, image_line,
                 text_line, sems):
    half = image_ref.shape[0]

    def fill(image_to, text_to):
        copies = [
            pltpu.make_async_copy(source, target, sems.at[n])
            for n, (source, target) in enumerate((
                (text_ref, texts), (image_ref, image_to.at[pl.ds(0, half)]), (image_valid_ref, image_line),
                (text_valid_ref, text_line)))
        ]
        for copy in copies:
            copy.start()
        copies[0].wait()
        put_texts(text_to, texts)
        for copy in copies[1:]:
            copy.wait()
        put_line(image_to, image_line[...])
        put_line(text_to, text_line[...])

    @pl.when(spot_ref[0] == 0)
    def _():
        fill(mine_ref, give_ref)

    @pl.when(spot_ref[0] != 0)
    def _():
        fill(give_ref, mine_ref)


def unpack(pair, texts, out_ref, start):
    one, two = pair
    half, part = one.shape[0] - SPARE, one.shape[1] // 2

    @pl.when(texts)
    def _():
        out_ref[start : start + half, :part] = two[:half, :part]
        out_ref[start : start + half, part:] = one[:half, :part]
        out_ref[start + half : start + 2 * half, :part] = two[:half, part:]
        out_ref[start + half : start + 2 * half, part:] = one[:half, part:]

    @pl.when(jnp.logical_not(texts))
    def _():
        out_ref[start : start + half] = one[:half]
        out_ref[start + half : start + 2 * half] = two[:half]


def counts(pair, texts):
    one, two = pair
    half = one.shape[0] - SPARE
    line_one = one[half:, :LINE].astype(jnp.float32)[:1]
    line_two = two[half:, :LINE].astype(jnp.float32)[:1]
    images = jnp.concatenate([line_one[:, :half], line_two[:, :half]], axis=1)
    return jnp.where(texts, line_one[:, : 2 * half], images)


def upright(line):
    size = line.shape[1]
    at = lax.broadcasted_iota(jnp.int32, (size, size), 0)
    to = lax.broadcasted_iota(jnp.int32, (size, size), 1)
    return jnp.sum(jnp.where(at == to, line, 0.0), axis=1, keepdims=True)


def sample_ids(col, texts, half, cols, axis):
    shape = (2 * half, 1) if axis == 0 else (1, 2 * half)
    at = lax.broadcasted_iota(jnp.int32, shape, axis)
    jump = jnp.where(texts, 0, (cols - 1) * half)
    first = col * jnp.where(texts, 2 * half, half)
    return at + first + jnp.where(at >= half, jump, 0)


def coefficients_of(cols, spot_ref, scale_ref, bias_ref, grad_ref, sample_ref, mine, others, my_sets, other_sets):
    row, col = spot_ref[0], spot_ref[1]
    my_texts, other_texts = row != 0, row == 0
    near, far, other_near, other_far = masks(cols, row)
    my_masks = {"own": 0, "near": near, "far": far, "both": near ^ far}
    other_masks = {"own": 0, "near": other_near, "far": other_far, "both": other_near ^ other_far}
    half = my_sets[0][1][0].shape[0] - SPARE
    scale, bias = scale_ref[0], bias_ref[0]
    factor = grad_ref[0] * scale / sample_ref[0].astype(jnp.float32)
    my_ids = jnp.concatenate([sample_ids(col ^ my_masks[k], my_texts, half, cols, 0) for k, _ in my_sets], axis=0)
    other_ids = jnp.concatenate(
        [sample_ids(col ^ other_masks[k], other_texts, half, cols, 1) for k, _ in other_sets], axis=1)
    my_weights = jnp.concatenate([upright(counts(pair, my_texts)) for _, pair in my_sets], axis=0)
    other_weights = factor * jnp.concatenate([counts(pair, other_texts) for _, pair in other_sets], axis=1)
    logits = lax.dot_general(mine, others, (((1,), (1,)), ((), ())), preferred_element_type=jnp.float32)
    logits = logits * scale + bias
    match = my_ids == other_ids
    rate = 1.0 / (1.0 + jnp.exp(jnp.where(match, logits, -logits)))
    return (jnp.where(match, -rate, rate) * my_weights * other_weights).astype(jnp.bfloat16)


def pairs(refs):
    return [refs[n : n + 2] for n in range(0, len(refs), 2)]


THREE = ("own", "near", "far")


def early_kernel(cols, spot_ref, scale_ref, bias_ref, grad_ref, sample_ref, *refs):
    mine_pairs, other_pairs = pairs(refs[:6]), pairs(refs[6:12])
    mine_ref, others_ref, total_ref = refs[12:]
    texts = spot_ref[0] != 0
    size = 2 * (refs[0].shape[0] - SPARE)
    for n in range(3):
        unpack(mine_pairs[n], texts, mine_ref, n * size)
        unpack(other_pairs[n], jnp.logical_not(texts), others_ref, n * size)
    others = others_ref[...]
    coefficient = coefficients_of(cols, spot_ref, scale_ref, bias_ref, grad_ref, sample_ref, mine_ref[...], others,
                                  list(zip(THREE, mine_pairs)), list(zip(THREE, other_pairs)))
    total_ref[...] = jnp.dot(coefficient, others, preferred_element_type=jnp.float32)


def both_kernel(cols, spot_ref, scale_ref, bias_ref, grad_ref, sample_ref, *refs):
    mine_pair, other_pairs = refs[:2], pairs(refs[2:8])
    others_ref, mine_ref, total_ref = refs[8:]
    unpack(mine_pair, spot_ref[0] != 0, mine_ref, 0)
    others = others_ref[...]
    coefficient = coefficients_of(cols, spot_ref, scale_ref, bias_ref, grad_ref, sample_ref, mine_ref[...], others,
                                  [("both", mine_pair)], list(zip(THREE, other_pairs)))
    total_ref[...] = jnp.dot(coefficient, others, preferred_element_type=jnp.float32)


def pack_sum(total, texts, stay_ref, cross_ref):
    half, part = total.shape[0] // 2, total.shape[1] // 2

    @pl.when(texts)
    def _():
        stay_ref[:, :part] = total[:half, part:].astype(stay_ref.dtype)
        stay_ref[:, part:] = total[half:, part:].astype(stay_ref.dtype)
        cross_ref[:, :part] = total[:half, :part].astype(cross_ref.dtype)
        cross_ref[:, part:] = total[half:, :part].astype(cross_ref.dtype)

    @pl.when(jnp.logical_not(texts))
    def _():
        stay_ref[...] = total[:half].astype(stay_ref.dtype)
        cross_ref[...] = total[half:].astype(cross_ref.dtype)


def late_kernel(cols, spot_ref, scale_ref, bias_ref, grad_ref, sample_ref, *refs):
    mine_pair, other_pair = refs[:2], refs[2:4]
    mine_ref, total_ref = refs[4:6]
    others_ref, stay_ref, cross_ref = refs[6:]
    texts = spot_ref[0] != 0
    unpack(other_pair, jnp.logical_not(texts), others_ref, 0)
    others = others_ref[...]
    coefficient = coefficients_of(cols, spot_ref, scale_ref, bias_ref, grad_ref, sample_ref, mine_ref[...], others,
                                  [("both", mine_pair)], [("both", other_pair)])
    total = total_ref[...] + jnp.dot(coefficient, others, preferred_element_type=jnp.float32)
    pack_sum(total, texts, stay_ref, cross_ref)


def rest_kernel(cols, spot_ref, scale_ref, bias_ref, grad_ref, sample_ref, *refs):
    mine_pairs, other_pair = pairs(refs[:6]), refs[6:8]
    mine_ref, others_ref, total_ref = refs[8:11]
    own_stay, own_cross, near_stay, near_cross, far_stay, far_cross = refs[11:]
    texts = spot_ref[0] != 0
    others = others_ref[...]
    coefficient = coefficients_of(cols, spot_ref, scale_ref, bias_ref, grad_ref, sample_ref, mine_ref[...], others,
                                  list(zip(THREE, mine_pairs)), [("both", other_pair)])
    total = total_ref[...] + jnp.dot(coefficient, others, preferred_element_type=jnp.float32)
    size = total.shape[0] // 3
    pack_sum(total[2 * size :], texts, far_stay, far_cross)
    pack_sum(total[size : 2 * size], texts, near_stay, near_cross)
    pack_sum(total[:size], texts, own_stay, own_cross)


def last_kernel(spot_ref, stay_ref, crossed_ref, near_stay_ref, near_cross_ref, far_stay_ref, far_cross_ref,
                image_ref, text_ref):
    half, part = text_ref.shape[0] // 2, text_ref.shape[1]

    def add(own, near, far):
        return (own[...] + near[...].astype(jnp.float32) + far[...].astype(jnp.float32)).astype(image_ref.dtype)

    stay = add(stay_ref, near_stay_ref, far_stay_ref)
    crossed = add(crossed_ref, near_cross_ref, far_cross_ref)

    def put(images, texts):
        image_ref[...] = images
        text_ref[:half] = texts[:, :part]
        text_ref[half:] = texts[:, part:]

    @pl.when(spot_ref[0] == 0)
    def _():
        put(stay, crossed)

    @pl.when(spot_ref[0] != 0)
    def _():
        put(crossed, stay)


def call(kernel, out_shape, smem, *arrays, flops=0):
    size = sum(a.size * a.dtype.itemsize for a in (*arrays, *jax.tree.leaves(out_shape)))
    return pl.pallas_call(
        kernel,
        out_shape=out_shape,
        in_specs=[pl.BlockSpec(memory_space=pltpu.SMEM)] * smem
        + [pl.BlockSpec(memory_space=pltpu.VMEM)] * (len(arrays) - smem),
        out_specs=jax.tree.map(lambda _: pl.BlockSpec(memory_space=pltpu.VMEM), out_shape),
        compiler_params=pltpu.CompilerParams(vmem_limit_bytes=24 * 1024 * 1024),
        cost_estimate=pl.CostEstimate(flops=flops, bytes_accessed=size, transcendentals=0),
    )(*arrays)


def pair_body(
    image_emb, text_emb, image_valid, text_valid, sample_count, logit_scale, logit_bias, loss_grad
):
    half, width = image_emb.shape
    size = 2 * half
    cols = lax.axis_size("col")
    spot = jnp.stack([lax.axis_index("row"), lax.axis_index("col")]).astype(jnp.int32)
    near, far = masks(cols, None)
    scalars = (spot, logit_scale, logit_bias, loss_grad, sample_count)

    def shape(rows, dtype):
        return jax.ShapeDtypeStruct((rows, width), dtype)

    bf16, f32 = jnp.bfloat16, jnp.float32
    sent = shape(half + SPARE, bf16)
    first = (image_emb, text_emb, image_valid[None], text_valid[None])
    own_a, give = pl.pallas_call(
        first_kernel,
        out_shape=(sent, sent),
        in_specs=[pl.BlockSpec(memory_space=pltpu.SMEM)] + [pl.BlockSpec(memory_space=pltpu.HBM)] * 4,
        out_specs=(pl.BlockSpec(memory_space=pltpu.VMEM),) * 2,
        scratch_shapes=[pltpu.VMEM(a.shape, a.dtype) for a in first[1:]] + [pltpu.SemaphoreType.DMA((4,))],
        compiler_params=pltpu.CompilerParams(vmem_limit_bytes=60 * 1024 * 1024),
    )(spot, *first)
    far_a = hop(own_a, *far)
    own_b = swap(give)
    far_b = hop(own_b, *far)
    near_a = hop(own_a, *near)
    near_b = hop(own_b, *near)
    both_a = hop(far_a, *near)
    both_b = hop(far_b, *near)
    mine = (own_a, own_b, near_a, near_b, far_a, far_b)
    others = (swap(own_a), give, swap(near_a), swap(near_b), swap(far_a), swap(far_b))
    both = (both_a, both_b)

    pair_flops = 4 * size * size * width
    mine_rows, other_rows, early = call(
        functools.partial(early_kernel, cols), (shape(3 * size, bf16), shape(3 * size, bf16), shape(3 * size, f32)),
        5, *scalars, *mine, *others, flops=9 * pair_flops)
    both, early = lax.optimization_barrier((both, early))
    other_both = (swap(both[0]), swap(both[1]))
    both_rows, both_early = call(
        functools.partial(both_kernel, cols), (shape(size, bf16), shape(size, f32)), 5, *scalars, *both, *others,
        other_rows, flops=3 * pair_flops)
    other_late, late_stay, late_cross = call(
        functools.partial(late_kernel, cols), (shape(size, bf16), shape(half, bf16), shape(half, bf16)), 5, *scalars,
        *both, *other_both, both_rows, both_early, flops=pair_flops)
    in_cross = hop(late_cross, *near)
    in_stay = hop(late_stay, *near)
    own_stay, own_cross, near_stay, near_cross, far_stay, far_cross = call(
        functools.partial(rest_kernel, cols),
        (shape(half, f32), shape(half, f32), shape(half, bf16), shape(half, bf16), shape(half, f32), shape(half, f32)),
        5, *scalars, *mine, *other_both, mine_rows, other_late, early, flops=3 * pair_flops)
    crossed = swap(own_cross)
    far_cross = (far_cross + in_cross.astype(f32)).astype(bf16)
    far_stay = hop((far_stay + in_stay.astype(f32)).astype(bf16), *far)
    near_stay, near_cross, _ = lax.optimization_barrier((near_stay, near_cross, far_cross))
    far_cross = hop(far_cross, *far, across=True)
    near_cross = hop(near_cross, *near, across=True)
    near_stay = hop(near_stay, *near)
    return call(last_kernel, (shape(half, bf16), jax.ShapeDtypeStruct(text_emb.shape, bf16)), 1, spot, own_stay, crossed,
                near_stay, near_cross, far_stay, far_cross)


def partner(block, axis, distance):
    count = lax.axis_size(axis)
    route = []
    for low in range(count):
        high = low | 1 << distance
        if high != low and high < count:
            route += [(low, high), (high, low)]
    return lax.ppermute(block, axis, route)


def coefficients(
    image_rows, valid_rows, row_ids, texts, weight_text, text_ids, factor, logit_scale, logit_bias
):
    logits = lax.dot_general(
        image_rows, texts, (((1,), (1,)), ((), ())), preferred_element_type=jnp.float32
    )
    logits = logits * logit_scale[0] + logit_bias[0]
    label_sign = jnp.where(row_ids[:, None] == text_ids[None, :], 1.0, -1.0).astype(jnp.float32)
    weights = valid_rows.astype(jnp.float32)[:, None] * weight_text[None, :]
    return (-factor * label_sign * jax.nn.sigmoid(-label_sign * logits) * weights).astype(
        jnp.bfloat16
    )


def text_part(coefficient, image_rows):
    return lax.dot_general(
        coefficient, image_rows, (((0,), (0,)), ((), ())), preferred_element_type=jnp.float32
    )


def body(
    image_emb, text_emb, image_valid, text_valid, sample_count, logit_scale, logit_bias, loss_grad
):
    text_block = lax.all_gather(text_emb, "row", axis=1, tiled=True)
    per_device = image_emb.shape[0]
    col_count = lax.axis_size("col")
    col_index = lax.axis_index("col")
    row_index = lax.axis_index("row")
    text_count = text_block.shape[0]
    factor = loss_grad[0] * logit_scale[0] / sample_count[0].astype(jnp.float32)
    valid_wire = image_valid.astype(jnp.bfloat16)
    parity = col_index % 2
    bit_count = col_count.bit_length() - 1
    text_wire = text_valid.astype(jnp.bfloat16)
    other_texts, other_valid = partner((text_block, text_wire), "col", 0)
    own_first = parity == 0
    texts = jnp.where(
        own_first,
        jnp.concatenate([text_block, other_texts], 0),
        jnp.concatenate([other_texts, text_block], 0),
    )
    text_weights = jnp.where(
        own_first,
        jnp.concatenate([text_wire, other_valid], 0),
        jnp.concatenate([other_valid, text_wire], 0),
    ).astype(jnp.float32)
    text_ids = (col_index - parity) * text_count + jnp.arange(2 * text_count, dtype=jnp.int32)
    image_rows, valid_rows = (image_emb, valid_wire)
    for bit in range(1, bit_count):
        other_rows, other_counts = partner((image_rows, valid_rows), "col", bit)
        lower = col_index >> bit & 1 == 0
        image_rows = jnp.where(
            lower,
            jnp.concatenate([image_rows, other_rows], 0),
            jnp.concatenate([other_rows, image_rows], 0),
        )
        valid_rows = jnp.where(
            lower,
            jnp.concatenate([valid_rows, other_counts], 0),
            jnp.concatenate([other_counts, valid_rows], 0),
        )
    positions = jnp.arange(image_rows.shape[0], dtype=jnp.int32)
    row_ids = (
        row_index * col_count + 2 * (positions // per_device) + parity
    ) * per_device + positions % per_device
    coefficient = coefficients(
        image_rows,
        valid_rows,
        row_ids,
        texts,
        text_weights,
        text_ids,
        factor,
        logit_scale,
        logit_bias,
    )
    partial_image = jnp.dot(coefficient, texts, preferred_element_type=jnp.float32)
    for bit in range(bit_count - 1, 0, -1):
        half = partial_image.shape[0] // 2
        upper = col_index >> bit & 1 == 1
        send = jnp.where(upper, partial_image[:half], partial_image[half:])
        keep = jnp.where(upper, partial_image[half:], partial_image[:half])
        partial_image = keep + partner(send, "col", bit)
    partial_text = text_part(coefficient, image_rows)
    odd = parity == 1
    send_text = jnp.where(odd, partial_text[:text_count], partial_text[text_count:])
    keep_text = jnp.where(odd, partial_text[text_count:], partial_text[:text_count])
    text_partial = keep_text + partner(send_text, "col", 0)
    text_grad = lax.psum_scatter(text_partial, "row", scatter_dimension=1, tiled=True)
    return (partial_image.astype(jnp.bfloat16), text_grad.astype(jnp.bfloat16))


def solution(mesh):
    in_specs = (
        P(("row", "col"), None),
        P("col", "row"),
        P(("row", "col")),
        P("col"),
        P(),
        P(),
        P(),
        P(),
    )
    out_specs = (P(("row", "col"), None), P("col", "row"))
    paired = mesh.shape["row"] == 2 and mesh.shape["col"] == 16
    run = pair_body if paired else body
    return jax.shard_map(run, mesh=mesh, in_specs=in_specs, out_specs=out_specs, check_vma=False)
```

```python
import functools

import jax
import jax.numpy as jnp
from jax import lax
from jax.experimental import pallas as pl
from jax.experimental.pallas import tpu as pltpu
from jax.sharding import PartitionSpec as P

SPARE = 8
LINE = 256


def hop(block, image_bit, text_bit, across=False):
    count = lax.axis_size("col")
    turn = count if across else 0
    route = [(c, turn + (c ^ image_bit)) for c in range(count)]
    route += [(count + c, count - turn + (c ^ text_bit)) for c in range(count)]
    return lax.ppermute(block, ("row", "col"), route)


def swap(block):
    return lax.ppermute(block, "row", [(0, 1), (1, 0)])


def masks(count, row):
    top = count // 2
    near, far = (1, 2), (top, top // 2)
    if row is None:
        return near, far
    return tuple(jnp.where(row == 0, *pair) for pair in (near, far, near[::-1], far[::-1]))


def put_line(ref, *pieces):
    pieces = [piece.astype(jnp.float32) for piece in pieces]
    pieces += [jnp.zeros((1, LINE - sum(piece.shape[1] for piece in pieces)), jnp.float32)]
    line = jnp.broadcast_to(jnp.concatenate(pieces, axis=1), (SPARE, LINE))
    ref[ref.shape[0] - SPARE :, :LINE] = line.astype(ref.dtype)


def put_texts(ref, text_ref):
    half, part = text_ref.shape[0] // 2, text_ref.shape[1]
    ref[:half, :part] = text_ref[:half]
    ref[:half, part:] = text_ref[half:]


def first_kernel(spot_ref, image_ref, text_ref, image_valid_ref, text_valid_ref, mine_ref, give_ref, texts, image_line,
                 text_line, sems):
    half = image_ref.shape[0]

    def fill(image_to, text_to):
        copies = [
            pltpu.make_async_copy(source, target, sems.at[n])
            for n, (source, target) in enumerate((
                (text_ref, texts), (image_ref, image_to.at[pl.ds(0, half)]), (image_valid_ref, image_line),
                (text_valid_ref, text_line)))
        ]
        for copy in copies:
            copy.start()
        copies[0].wait()
        put_texts(text_to, texts)
        for copy in copies[1:]:
            copy.wait()
        put_line(image_to, image_line[...])
        put_line(text_to, text_line[...])

    @pl.when(spot_ref[0] == 0)
    def _():
        fill(mine_ref, give_ref)

    @pl.when(spot_ref[0] != 0)
    def _():
        fill(give_ref, mine_ref)


def unpack(pair, texts, out_ref, start):
    one, two = pair
    half, part = one.shape[0] - SPARE, one.shape[1] // 2

    @pl.when(texts)
    def _():
        out_ref[start : start + half, :part] = two[:half, :part]
        out_ref[start : start + half, part:] = one[:half, :part]
        out_ref[start + half : start + 2 * half, :part] = two[:half, part:]
        out_ref[start + half : start + 2 * half, part:] = one[:half, part:]

    @pl.when(jnp.logical_not(texts))
    def _():
        out_ref[start : start + half] = one[:half]
        out_ref[start + half : start + 2 * half] = two[:half]


def counts(pair, texts):
    one, two = pair
    half = one.shape[0] - SPARE
    line_one = one[half:, :LINE].astype(jnp.float32)[:1]
    line_two = two[half:, :LINE].astype(jnp.float32)[:1]
    images = jnp.concatenate([line_one[:, :half], line_two[:, :half]], axis=1)
    return jnp.where(texts, line_one[:, : 2 * half], images)


def upright(line):
    size = line.shape[1]
    at = lax.broadcasted_iota(jnp.int32, (size, size), 0)
    to = lax.broadcasted_iota(jnp.int32, (size, size), 1)
    return jnp.sum(jnp.where(at == to, line, 0.0), axis=1, keepdims=True)


def sample_ids(col, texts, half, cols, axis):
    shape = (2 * half, 1) if axis == 0 else (1, 2 * half)
    at = lax.broadcasted_iota(jnp.int32, shape, axis)
    jump = jnp.where(texts, 0, (cols - 1) * half)
    first = col * jnp.where(texts, 2 * half, half)
    return at + first + jnp.where(at >= half, jump, 0)


def coefficients_of(cols, row_ref, col_ref, scale_ref, bias_ref, grad_ref, sample_ref, mine, others, my_sets, other_sets):
    row, col = row_ref[0], col_ref[0]
    my_texts, other_texts = row != 0, row == 0
    near, far, other_near, other_far = masks(cols, row)
    my_masks = {"own": 0, "near": near, "far": far, "both": near ^ far}
    other_masks = {"own": 0, "near": other_near, "far": other_far, "both": other_near ^ other_far}
    half = my_sets[0][1][0].shape[0] - SPARE
    scale, bias = scale_ref[0], bias_ref[0]
    factor = grad_ref[0] * scale / sample_ref[0].astype(jnp.float32)
    my_ids = jnp.concatenate([sample_ids(col ^ my_masks[k], my_texts, half, cols, 0) for k, _ in my_sets], axis=0)
    other_ids = jnp.concatenate(
        [sample_ids(col ^ other_masks[k], other_texts, half, cols, 1) for k, _ in other_sets], axis=1)
    my_weights = jnp.concatenate([upright(counts(pair, my_texts)) for _, pair in my_sets], axis=0)
    other_weights = factor * jnp.concatenate([counts(pair, other_texts) for _, pair in other_sets], axis=1)
    logits = lax.dot_general(mine, others, (((1,), (1,)), ((), ())), preferred_element_type=jnp.float32)
    logits = logits * scale + bias
    match = my_ids == other_ids
    rate = 1.0 / (1.0 + jnp.exp(jnp.where(match, logits, -logits)))
    return (jnp.where(match, -rate, rate) * my_weights * other_weights).astype(jnp.bfloat16)


def pairs(refs):
    return [refs[n : n + 2] for n in range(0, len(refs), 2)]


THREE = ("own", "near", "far")


def early_kernel(cols, row_ref, col_ref, scale_ref, bias_ref, grad_ref, sample_ref, *refs):
    mine_pairs, other_pairs = pairs(refs[:6]), pairs(refs[6:12])
    mine_ref, others_ref, total_ref = refs[12:]
    texts = row_ref[0] != 0
    size = 2 * (refs[0].shape[0] - SPARE)
    for n in range(3):
        unpack(mine_pairs[n], texts, mine_ref, n * size)
        unpack(other_pairs[n], jnp.logical_not(texts), others_ref, n * size)
    others = others_ref[...]
    coefficient = coefficients_of(cols, row_ref, col_ref, scale_ref, bias_ref, grad_ref, sample_ref, mine_ref[...], others,
                                  list(zip(THREE, mine_pairs)), list(zip(THREE, other_pairs)))
    total_ref[...] = jnp.dot(coefficient, others, preferred_element_type=jnp.float32)


def both_kernel(cols, row_ref, col_ref, scale_ref, bias_ref, grad_ref, sample_ref, *refs):
    mine_pair, other_pairs = refs[:2], pairs(refs[2:8])
    others_ref, mine_ref, total_ref = refs[8:]
    unpack(mine_pair, row_ref[0] != 0, mine_ref, 0)
    others = others_ref[...]
    coefficient = coefficients_of(cols, row_ref, col_ref, scale_ref, bias_ref, grad_ref, sample_ref, mine_ref[...], others,
                                  [("both", mine_pair)], list(zip(THREE, other_pairs)))
    total_ref[...] = jnp.dot(coefficient, others, preferred_element_type=jnp.float32)


def pack_sum(total, texts, stay_ref, cross_ref):
    half, part = total.shape[0] // 2, total.shape[1] // 2

    @pl.when(texts)
    def _():
        stay_ref[:, :part] = total[:half, part:].astype(stay_ref.dtype)
        stay_ref[:, part:] = total[half:, part:].astype(stay_ref.dtype)
        cross_ref[:, :part] = total[:half, :part].astype(cross_ref.dtype)
        cross_ref[:, part:] = total[half:, :part].astype(cross_ref.dtype)

    @pl.when(jnp.logical_not(texts))
    def _():
        stay_ref[...] = total[:half].astype(stay_ref.dtype)
        cross_ref[...] = total[half:].astype(cross_ref.dtype)


def late_kernel(cols, row_ref, col_ref, scale_ref, bias_ref, grad_ref, sample_ref, *refs):
    mine_pair, other_pair = refs[:2], refs[2:4]
    mine_ref, total_ref = refs[4:6]
    others_ref, stay_ref, cross_ref = refs[6:]
    texts = row_ref[0] != 0
    unpack(other_pair, jnp.logical_not(texts), others_ref, 0)
    others = others_ref[...]
    coefficient = coefficients_of(cols, row_ref, col_ref, scale_ref, bias_ref, grad_ref, sample_ref, mine_ref[...], others,
                                  [("both", mine_pair)], [("both", other_pair)])
    total = total_ref[...] + jnp.dot(coefficient, others, preferred_element_type=jnp.float32)
    pack_sum(total, texts, stay_ref, cross_ref)


def rest_kernel(cols, row_ref, col_ref, scale_ref, bias_ref, grad_ref, sample_ref, *refs):
    mine_pairs, other_pair = pairs(refs[:6]), refs[6:8]
    mine_ref, others_ref, total_ref = refs[8:11]
    own_stay, own_cross, near_stay, near_cross, far_stay, far_cross = refs[11:]
    texts = row_ref[0] != 0
    others = others_ref[...]
    coefficient = coefficients_of(cols, row_ref, col_ref, scale_ref, bias_ref, grad_ref, sample_ref, mine_ref[...], others,
                                  list(zip(THREE, mine_pairs)), [("both", other_pair)])
    total = total_ref[...] + jnp.dot(coefficient, others, preferred_element_type=jnp.float32)
    size = total.shape[0] // 3
    pack_sum(total[2 * size :], texts, far_stay, far_cross)
    pack_sum(total[size : 2 * size], texts, near_stay, near_cross)
    pack_sum(total[:size], texts, own_stay, own_cross)


def last_kernel(spot_ref, stay_ref, crossed_ref, near_stay_ref, near_cross_ref, far_stay_ref, far_cross_ref,
                image_ref, text_ref):
    half, part = text_ref.shape[0] // 2, text_ref.shape[1]

    def add(own, near, far):
        return (own[...] + near[...].astype(jnp.float32) + far[...].astype(jnp.float32)).astype(image_ref.dtype)

    stay = add(stay_ref, near_stay_ref, far_stay_ref)
    crossed = add(crossed_ref, near_cross_ref, far_cross_ref)

    def put(images, texts):
        image_ref[...] = images
        text_ref[:half] = texts[:, :part]
        text_ref[half:] = texts[:, part:]

    @pl.when(spot_ref[0] == 0)
    def _():
        put(stay, crossed)

    @pl.when(spot_ref[0] != 0)
    def _():
        put(crossed, stay)


def call(kernel, out_shape, smem, *arrays, flops=0):
    size = sum(a.size * a.dtype.itemsize for a in (*arrays, *jax.tree.leaves(out_shape)))
    return pl.pallas_call(
        kernel,
        out_shape=out_shape,
        in_specs=[pl.BlockSpec(memory_space=pltpu.SMEM)] * smem
        + [pl.BlockSpec(memory_space=pltpu.VMEM)] * (len(arrays) - smem),
        out_specs=jax.tree.map(lambda _: pl.BlockSpec(memory_space=pltpu.VMEM), out_shape),
        compiler_params=pltpu.CompilerParams(vmem_limit_bytes=24 * 1024 * 1024),
        cost_estimate=pl.CostEstimate(flops=flops, bytes_accessed=size, transcendentals=0),
    )(*arrays)


def pair_body(
    image_emb, text_emb, image_valid, text_valid, sample_count, logit_scale, logit_bias, loss_grad
):
    half, width = image_emb.shape
    size = 2 * half
    cols = lax.axis_size("col")
    row, col = lax.axis_index("row")[None], lax.axis_index("col")[None]
    near, far = masks(cols, None)
    scalars = (row, col, logit_scale, logit_bias, loss_grad, sample_count)

    def shape(rows, dtype):
        return jax.ShapeDtypeStruct((rows, width), dtype)

    bf16, f32 = jnp.bfloat16, jnp.float32
    sent = shape(half + SPARE, bf16)
    first = (image_emb, text_emb, image_valid[None], text_valid[None])
    own_a, give = pl.pallas_call(
        first_kernel,
        out_shape=(sent, sent),
        in_specs=[pl.BlockSpec(memory_space=pltpu.SMEM)] + [pl.BlockSpec(memory_space=pltpu.HBM)] * 4,
        out_specs=(pl.BlockSpec(memory_space=pltpu.VMEM),) * 2,
        scratch_shapes=[pltpu.VMEM(a.shape, a.dtype) for a in first[1:]] + [pltpu.SemaphoreType.DMA((4,))],
        compiler_params=pltpu.CompilerParams(vmem_limit_bytes=60 * 1024 * 1024),
    )(row, *first)
    far_a = hop(own_a, *far)
    own_b = swap(give)
    far_b = hop(own_b, *far)
    near_a = hop(own_a, *near)
    near_b = hop(own_b, *near)
    both_a = hop(far_a, *near)
    both_b = hop(far_b, *near)
    mine = (own_a, own_b, near_a, near_b, far_a, far_b)
    others = (swap(own_a), give, swap(near_a), swap(near_b), swap(far_a), swap(far_b))
    others, other_both_a = lax.optimization_barrier((others, swap(both_a)))

    pair_flops = 4 * size * size * width
    mine_rows, other_rows, early = call(
        functools.partial(early_kernel, cols), (shape(3 * size, bf16), shape(3 * size, bf16), shape(3 * size, f32)),
        6, *scalars, *mine, *others, flops=9 * pair_flops)
    both_b, early = lax.optimization_barrier((both_b, early))
    both = (both_a, both_b)
    other_both = (other_both_a, swap(both_b))
    both_rows, both_early = call(
        functools.partial(both_kernel, cols), (shape(size, bf16), shape(size, f32)), 6, *scalars, *both, *others,
        other_rows, flops=3 * pair_flops)
    other_late, late_stay, late_cross = call(
        functools.partial(late_kernel, cols), (shape(size, bf16), shape(half, bf16), shape(half, bf16)), 6, *scalars,
        *both, *other_both, both_rows, both_early, flops=pair_flops)
    in_cross = hop(late_cross, *near)
    in_stay = hop(late_stay, *near)
    own_stay, own_cross, near_stay, near_cross, far_stay, far_cross = call(
        functools.partial(rest_kernel, cols),
        (shape(half, f32), shape(half, f32), shape(half, bf16), shape(half, bf16), shape(half, f32), shape(half, f32)),
        6, *scalars, *mine, *other_both, mine_rows, other_late, early, flops=3 * pair_flops)
    crossed = swap(own_cross)
    far_cross = (far_cross + in_cross.astype(f32)).astype(bf16)
    far_stay = (far_stay + in_stay.astype(f32)).astype(bf16)
    near_stay, _ = lax.optimization_barrier((near_stay, far_cross))
    near_stay = hop(near_stay, *near)
    near_cross, _, _ = lax.optimization_barrier((near_cross, far_cross, far_stay))
    far_cross = hop(far_cross, *far, across=True)
    far_stay = hop(far_stay, *far)
    near_cross = hop(near_cross, *near, across=True)
    return call(last_kernel, (shape(half, bf16), jax.ShapeDtypeStruct(text_emb.shape, bf16)), 1, row, own_stay, crossed,
                near_stay, near_cross, far_stay, far_cross)


def partner(block, axis, distance):
    count = lax.axis_size(axis)
    route = []
    for low in range(count):
        high = low | 1 << distance
        if high != low and high < count:
            route += [(low, high), (high, low)]
    return lax.ppermute(block, axis, route)


def coefficients(
    image_rows, valid_rows, row_ids, texts, weight_text, text_ids, factor, logit_scale, logit_bias
):
    logits = lax.dot_general(
        image_rows, texts, (((1,), (1,)), ((), ())), preferred_element_type=jnp.float32
    )
    logits = logits * logit_scale[0] + logit_bias[0]
    label_sign = jnp.where(row_ids[:, None] == text_ids[None, :], 1.0, -1.0).astype(jnp.float32)
    weights = valid_rows.astype(jnp.float32)[:, None] * weight_text[None, :]
    return (-factor * label_sign * jax.nn.sigmoid(-label_sign * logits) * weights).astype(
        jnp.bfloat16
    )


def text_part(coefficient, image_rows):
    return lax.dot_general(
        coefficient, image_rows, (((0,), (0,)), ((), ())), preferred_element_type=jnp.float32
    )


def body(
    image_emb, text_emb, image_valid, text_valid, sample_count, logit_scale, logit_bias, loss_grad
):
    text_block = lax.all_gather(text_emb, "row", axis=1, tiled=True)
    per_device = image_emb.shape[0]
    col_count = lax.axis_size("col")
    col_index = lax.axis_index("col")
    row_index = lax.axis_index("row")
    text_count = text_block.shape[0]
    factor = loss_grad[0] * logit_scale[0] / sample_count[0].astype(jnp.float32)
    valid_wire = image_valid.astype(jnp.bfloat16)
    parity = col_index % 2
    bit_count = col_count.bit_length() - 1
    text_wire = text_valid.astype(jnp.bfloat16)
    other_texts, other_valid = partner((text_block, text_wire), "col", 0)
    own_first = parity == 0
    texts = jnp.where(
        own_first,
        jnp.concatenate([text_block, other_texts], 0),
        jnp.concatenate([other_texts, text_block], 0),
    )
    text_weights = jnp.where(
        own_first,
        jnp.concatenate([text_wire, other_valid], 0),
        jnp.concatenate([other_valid, text_wire], 0),
    ).astype(jnp.float32)
    text_ids = (col_index - parity) * text_count + jnp.arange(2 * text_count, dtype=jnp.int32)
    image_rows, valid_rows = (image_emb, valid_wire)
    for bit in range(1, bit_count):
        other_rows, other_counts = partner((image_rows, valid_rows), "col", bit)
        lower = col_index >> bit & 1 == 0
        image_rows = jnp.where(
            lower,
            jnp.concatenate([image_rows, other_rows], 0),
            jnp.concatenate([other_rows, image_rows], 0),
        )
        valid_rows = jnp.where(
            lower,
            jnp.concatenate([valid_rows, other_counts], 0),
            jnp.concatenate([other_counts, valid_rows], 0),
        )
    positions = jnp.arange(image_rows.shape[0], dtype=jnp.int32)
    row_ids = (
        row_index * col_count + 2 * (positions // per_device) + parity
    ) * per_device + positions % per_device
    coefficient = coefficients(
        image_rows,
        valid_rows,
        row_ids,
        texts,
        text_weights,
        text_ids,
        factor,
        logit_scale,
        logit_bias,
    )
    partial_image = jnp.dot(coefficient, texts, preferred_element_type=jnp.float32)
    for bit in range(bit_count - 1, 0, -1):
        half = partial_image.shape[0] // 2
        upper = col_index >> bit & 1 == 1
        send = jnp.where(upper, partial_image[:half], partial_image[half:])
        keep = jnp.where(upper, partial_image[half:], partial_image[:half])
        partial_image = keep + partner(send, "col", bit)
    partial_text = text_part(coefficient, image_rows)
    odd = parity == 1
    send_text = jnp.where(odd, partial_text[:text_count], partial_text[text_count:])
    keep_text = jnp.where(odd, partial_text[text_count:], partial_text[:text_count])
    text_partial = keep_text + partner(send_text, "col", 0)
    text_grad = lax.psum_scatter(text_partial, "row", scatter_dimension=1, tiled=True)
    return (partial_image.astype(jnp.bfloat16), text_grad.astype(jnp.bfloat16))


def solution(mesh):
    in_specs = (
        P(("row", "col"), None),
        P("col", "row"),
        P(("row", "col")),
        P("col"),
        P(),
        P(),
        P(),
        P(),
    )
    out_specs = (P(("row", "col"), None), P("col", "row"))
    paired = mesh.shape["row"] == 2 and mesh.shape["col"] == 16
    run = pair_body if paired else body
    return jax.shard_map(run, mesh=mesh, in_specs=in_specs, out_specs=out_specs, check_vma=False)
```

```python
import functools

import jax
import jax.numpy as jnp
from jax import lax
from jax.experimental import pallas as pl
from jax.experimental.pallas import tpu as pltpu
from jax.sharding import PartitionSpec as P

SPARE = 8
LINE = 256


def hop(block, image_bit, text_bit, across=False):
    count = lax.axis_size("col")
    turn = count if across else 0
    route = [(c, turn + (c ^ image_bit)) for c in range(count)]
    route += [(count + c, count - turn + (c ^ text_bit)) for c in range(count)]
    return lax.ppermute(block, ("row", "col"), route)


def swap(block):
    return lax.ppermute(block, "row", [(0, 1), (1, 0)])


def masks(count, row):
    top = count // 2
    near, far = (1, 2), (top, top // 2)
    if row is None:
        return near, far
    return tuple(jnp.where(row == 0, *pair) for pair in (near, far, near[::-1], far[::-1]))


def put_line(ref, *pieces):
    pieces = [piece.astype(jnp.float32) for piece in pieces]
    pieces += [jnp.zeros((1, LINE - sum(piece.shape[1] for piece in pieces)), jnp.float32)]
    line = jnp.broadcast_to(jnp.concatenate(pieces, axis=1), (SPARE, LINE))
    ref[ref.shape[0] - SPARE :, :LINE] = line.astype(ref.dtype)


def put_texts(ref, text_ref):
    half, part = text_ref.shape[0] // 2, text_ref.shape[1]
    ref[:half, :part] = text_ref[:half]
    ref[:half, part:] = text_ref[half:]


def first_kernel(spot_ref, image_ref, text_ref, image_valid_ref, text_valid_ref, mine_ref, give_ref, texts, image_line,
                 text_line, sems):
    half = image_ref.shape[0]

    def fill(image_to, text_to):
        copies = [
            pltpu.make_async_copy(source, target, sems.at[n])
            for n, (source, target) in enumerate((
                (text_ref, texts), (image_ref, image_to.at[pl.ds(0, half)]), (image_valid_ref, image_line),
                (text_valid_ref, text_line)))
        ]
        for copy in copies:
            copy.start()
        copies[0].wait()
        put_texts(text_to, texts)
        for copy in copies[1:]:
            copy.wait()
        put_line(image_to, image_line[...])
        put_line(text_to, text_line[...])

    @pl.when(spot_ref[0] == 0)
    def _():
        fill(mine_ref, give_ref)

    @pl.when(spot_ref[0] != 0)
    def _():
        fill(give_ref, mine_ref)


def unpack(pair, texts, out_ref, start):
    one, two = pair
    half, part = one.shape[0] - SPARE, one.shape[1] // 2

    @pl.when(texts)
    def _():
        out_ref[start : start + half, :part] = two[:half, :part]
        out_ref[start : start + half, part:] = one[:half, :part]
        out_ref[start + half : start + 2 * half, :part] = two[:half, part:]
        out_ref[start + half : start + 2 * half, part:] = one[:half, part:]

    @pl.when(jnp.logical_not(texts))
    def _():
        out_ref[start : start + half] = one[:half]
        out_ref[start + half : start + 2 * half] = two[:half]


def counts(pair, texts):
    one, two = pair
    half = one.shape[0] - SPARE
    line_one = one[half:, :LINE].astype(jnp.float32)[:1]
    line_two = two[half:, :LINE].astype(jnp.float32)[:1]
    images = jnp.concatenate([line_one[:, :half], line_two[:, :half]], axis=1)
    return jnp.where(texts, line_one[:, : 2 * half], images)


def upright(line):
    size = line.shape[1]
    at = lax.broadcasted_iota(jnp.int32, (size, size), 0)
    to = lax.broadcasted_iota(jnp.int32, (size, size), 1)
    return jnp.sum(jnp.where(at == to, line, 0.0), axis=1, keepdims=True)


def sample_ids(col, texts, half, cols, axis):
    shape = (2 * half, 1) if axis == 0 else (1, 2 * half)
    at = lax.broadcasted_iota(jnp.int32, shape, axis)
    jump = jnp.where(texts, 0, (cols - 1) * half)
    first = col * jnp.where(texts, 2 * half, half)
    return at + first + jnp.where(at >= half, jump, 0)


def coefficients_of(cols, row_ref, col_ref, number_ref, mine, others, my_sets, other_sets):
    row, col = row_ref[0], col_ref[0]
    my_texts, other_texts = row != 0, row == 0
    near, far, other_near, other_far = masks(cols, row)
    my_masks = {"own": 0, "near": near, "far": far, "both": near ^ far}
    other_masks = {"own": 0, "near": other_near, "far": other_far, "both": other_near ^ other_far}
    half = my_sets[0][1][0].shape[0] - SPARE
    scale, bias, factor = (number_ref[n : n + 1, :1] for n in range(3))
    my_ids = jnp.concatenate([sample_ids(col ^ my_masks[k], my_texts, half, cols, 0) for k, _ in my_sets], axis=0)
    other_ids = jnp.concatenate(
        [sample_ids(col ^ other_masks[k], other_texts, half, cols, 1) for k, _ in other_sets], axis=1)
    my_weights = jnp.concatenate([upright(counts(pair, my_texts)) for _, pair in my_sets], axis=0)
    other_weights = factor * jnp.concatenate([counts(pair, other_texts) for _, pair in other_sets], axis=1)
    logits = lax.dot_general(mine, others, (((1,), (1,)), ((), ())), preferred_element_type=jnp.float32)
    logits = logits * scale + bias
    match = my_ids == other_ids
    rate = 1.0 / (1.0 + jnp.exp(jnp.where(match, logits, -logits)))
    return (jnp.where(match, -rate, rate) * my_weights * other_weights).astype(jnp.bfloat16)


def pairs(refs):
    return [refs[n : n + 2] for n in range(0, len(refs), 2)]


THREE = ("own", "near", "far")


def number_kernel(scale_ref, bias_ref, grad_ref, sample_ref, out_ref):
    factor = grad_ref[0] * scale_ref[0] / sample_ref[0].astype(jnp.float32)
    line = lax.broadcasted_iota(jnp.int32, out_ref.shape, 0)
    out_ref[...] = jnp.where(line == 0, scale_ref[0], jnp.where(line == 1, bias_ref[0], factor))


def early_kernel(cols, row_ref, col_ref, number_ref, *refs):
    mine_pairs, other_pairs = pairs(refs[:6]), pairs(refs[6:12])
    mine_ref, others_ref, total_ref = refs[12:]
    texts = row_ref[0] != 0
    size = 2 * (refs[0].shape[0] - SPARE)
    for n in range(3):
        unpack(mine_pairs[n], texts, mine_ref, n * size)
        unpack(other_pairs[n], jnp.logical_not(texts), others_ref, n * size)
    others = others_ref[...]
    coefficient = coefficients_of(cols, row_ref, col_ref, number_ref, mine_ref[...], others,
                                  list(zip(THREE, mine_pairs)), list(zip(THREE, other_pairs)))
    total_ref[...] = jnp.dot(coefficient, others, preferred_element_type=jnp.float32)


def both_kernel(cols, row_ref, col_ref, number_ref, *refs):
    mine_pair, other_pairs = refs[:2], pairs(refs[2:8])
    others_ref, mine_ref, total_ref = refs[8:]
    unpack(mine_pair, row_ref[0] != 0, mine_ref, 0)
    others = others_ref[...]
    coefficient = coefficients_of(cols, row_ref, col_ref, number_ref, mine_ref[...], others,
                                  [("both", mine_pair)], list(zip(THREE, other_pairs)))
    total_ref[...] = jnp.dot(coefficient, others, preferred_element_type=jnp.float32)


def pack_sum(total, texts, stay_ref, cross_ref):
    half, part = total.shape[0] // 2, total.shape[1] // 2

    @pl.when(texts)
    def _():
        stay_ref[:, :part] = total[:half, part:].astype(stay_ref.dtype)
        stay_ref[:, part:] = total[half:, part:].astype(stay_ref.dtype)
        cross_ref[:, :part] = total[:half, :part].astype(cross_ref.dtype)
        cross_ref[:, part:] = total[half:, :part].astype(cross_ref.dtype)

    @pl.when(jnp.logical_not(texts))
    def _():
        stay_ref[...] = total[:half].astype(stay_ref.dtype)
        cross_ref[...] = total[half:].astype(cross_ref.dtype)


def late_kernel(cols, row_ref, col_ref, number_ref, *refs):
    mine_pair, other_pair = refs[:2], refs[2:4]
    mine_ref, total_ref = refs[4:6]
    others_ref, stay_ref, cross_ref = refs[6:]
    texts = row_ref[0] != 0
    unpack(other_pair, jnp.logical_not(texts), others_ref, 0)
    others = others_ref[...]
    coefficient = coefficients_of(cols, row_ref, col_ref, number_ref, mine_ref[...], others,
                                  [("both", mine_pair)], [("both", other_pair)])
    total = total_ref[...] + jnp.dot(coefficient, others, preferred_element_type=jnp.float32)
    pack_sum(total, texts, stay_ref, cross_ref)


def rest_kernel(cols, row_ref, col_ref, number_ref, *refs):
    mine_pairs, other_pair = pairs(refs[:6]), refs[6:8]
    mine_ref, others_ref, total_ref = refs[8:11]
    own_stay, own_cross, near_stay, near_cross, far_stay, far_cross = refs[11:]
    texts = row_ref[0] != 0
    others = others_ref[...]
    coefficient = coefficients_of(cols, row_ref, col_ref, number_ref, mine_ref[...], others,
                                  list(zip(THREE, mine_pairs)), [("both", other_pair)])
    total = total_ref[...] + jnp.dot(coefficient, others, preferred_element_type=jnp.float32)
    size = total.shape[0] // 3
    pack_sum(total[2 * size :], texts, far_stay, far_cross)
    pack_sum(total[size : 2 * size], texts, near_stay, near_cross)
    pack_sum(total[:size], texts, own_stay, own_cross)


def last_kernel(spot_ref, stay_ref, crossed_ref, near_stay_ref, near_cross_ref, image_ref, text_ref):
    half, part = text_ref.shape[0] // 2, text_ref.shape[1]

    stay = (stay_ref[...] + near_stay_ref[...].astype(jnp.float32)).astype(image_ref.dtype)
    crossed = (crossed_ref[...] + near_cross_ref[...].astype(jnp.float32)).astype(image_ref.dtype)

    def put(images, texts):
        image_ref[...] = images
        text_ref[:half] = texts[:, :part]
        text_ref[half:] = texts[:, part:]

    @pl.when(spot_ref[0] == 0)
    def _():
        put(stay, crossed)

    @pl.when(spot_ref[0] != 0)
    def _():
        put(crossed, stay)


def call(kernel, out_shape, smem, *arrays, flops=0):
    size = sum(a.size * a.dtype.itemsize for a in (*arrays, *jax.tree.leaves(out_shape)))
    return pl.pallas_call(
        kernel,
        out_shape=out_shape,
        in_specs=[pl.BlockSpec(memory_space=pltpu.SMEM)] * smem
        + [pl.BlockSpec(memory_space=pltpu.VMEM)] * (len(arrays) - smem),
        out_specs=jax.tree.map(lambda _: pl.BlockSpec(memory_space=pltpu.VMEM), out_shape),
        compiler_params=pltpu.CompilerParams(vmem_limit_bytes=24 * 1024 * 1024),
        cost_estimate=pl.CostEstimate(flops=flops, bytes_accessed=size, transcendentals=0),
    )(*arrays)


def pair_body(
    image_emb, text_emb, image_valid, text_valid, sample_count, logit_scale, logit_bias, loss_grad
):
    half, width = image_emb.shape
    size = 2 * half
    cols = lax.axis_size("col")
    row, col = lax.axis_index("row")[None], lax.axis_index("col")[None]
    near, far = masks(cols, None)

    def shape(rows, dtype):
        return jax.ShapeDtypeStruct((rows, width), dtype)

    bf16, f32 = jnp.bfloat16, jnp.float32
    sent = shape(half + SPARE, bf16)
    first = (image_emb, text_emb, image_valid[None], text_valid[None])
    own_a, give = pl.pallas_call(
        first_kernel,
        out_shape=(sent, sent),
        in_specs=[pl.BlockSpec(memory_space=pltpu.SMEM)] + [pl.BlockSpec(memory_space=pltpu.HBM)] * 4,
        out_specs=(pl.BlockSpec(memory_space=pltpu.VMEM),) * 2,
        scratch_shapes=[pltpu.VMEM(a.shape, a.dtype) for a in first[1:]] + [pltpu.SemaphoreType.DMA((4,))],
        compiler_params=pltpu.CompilerParams(vmem_limit_bytes=60 * 1024 * 1024),
    )(row, *first)
    far_a = hop(own_a, *far)
    own_b = swap(give)
    far_b = hop(own_b, *far)
    near_a = hop(own_a, *near)
    near_b = hop(own_b, *near)
    both_a = hop(far_a, *near)
    both_b = hop(far_b, *near)
    mine = (own_a, own_b, near_a, near_b, far_a, far_b)
    number = call(number_kernel, jax.ShapeDtypeStruct((8, 128), f32), 4, logit_scale, logit_bias, loss_grad, sample_count)
    near_a, number = lax.optimization_barrier((near_a, number))
    others = (swap(own_a), give, swap(near_a), swap(near_b), swap(far_a), swap(far_b))
    others, other_both_a = lax.optimization_barrier((others, swap(both_a)))

    pair_flops = 4 * size * size * width
    scalars = (row, col, number)
    mine_rows, other_rows, early = call(
        functools.partial(early_kernel, cols), (shape(3 * size, bf16), shape(3 * size, bf16), shape(3 * size, f32)),
        2, *scalars, *mine, *others, flops=9 * pair_flops)
    both_b, early = lax.optimization_barrier((both_b, early))
    both = (both_a, both_b)
    other_both = (other_both_a, swap(both_b))
    both_rows, both_early = call(
        functools.partial(both_kernel, cols), (shape(size, bf16), shape(size, f32)), 2, *scalars, *both, *others,
        other_rows, flops=3 * pair_flops)
    other_late, late_stay, late_cross = call(
        functools.partial(late_kernel, cols), (shape(size, bf16), shape(half, bf16), shape(half, bf16)), 2, *scalars,
        *both, *other_both, both_rows, both_early, flops=pair_flops)
    in_cross = hop(late_cross, *near)
    in_stay = hop(late_stay, *near)
    own_stay, own_cross, near_stay, near_cross, far_stay, far_cross = call(
        functools.partial(rest_kernel, cols),
        (shape(half, f32), shape(half, f32), shape(half, bf16), shape(half, bf16), shape(half, f32), shape(half, f32)),
        2, *scalars, *mine, *other_both, mine_rows, other_late, early, flops=3 * pair_flops)
    crossed = swap(own_cross)
    far_cross = (far_cross + in_cross.astype(f32)).astype(bf16)
    far_stay = (far_stay + in_stay.astype(f32)).astype(bf16)
    near_stay, _ = lax.optimization_barrier((near_stay, far_cross))
    near_stay = hop(near_stay, *near)
    near_cross, _, _ = lax.optimization_barrier((near_cross, far_cross, far_stay))
    far_cross = hop(far_cross, *far, across=True)
    far_stay = hop(far_stay, *far)
    near_cross = hop(near_cross, *near, across=True)
    own_stay = own_stay + far_stay.astype(f32)
    crossed = crossed + far_cross.astype(f32)
    return call(last_kernel, (shape(half, bf16), jax.ShapeDtypeStruct(text_emb.shape, bf16)), 1, row, own_stay, crossed,
                near_stay, near_cross)


def partner(block, axis, distance):
    count = lax.axis_size(axis)
    route = []
    for low in range(count):
        high = low | 1 << distance
        if high != low and high < count:
            route += [(low, high), (high, low)]
    return lax.ppermute(block, axis, route)


def coefficients(
    image_rows, valid_rows, row_ids, texts, weight_text, text_ids, factor, logit_scale, logit_bias
):
    logits = lax.dot_general(
        image_rows, texts, (((1,), (1,)), ((), ())), preferred_element_type=jnp.float32
    )
    logits = logits * logit_scale[0] + logit_bias[0]
    label_sign = jnp.where(row_ids[:, None] == text_ids[None, :], 1.0, -1.0).astype(jnp.float32)
    weights = valid_rows.astype(jnp.float32)[:, None] * weight_text[None, :]
    return (-factor * label_sign * jax.nn.sigmoid(-label_sign * logits) * weights).astype(
        jnp.bfloat16
    )


def text_part(coefficient, image_rows):
    return lax.dot_general(
        coefficient, image_rows, (((0,), (0,)), ((), ())), preferred_element_type=jnp.float32
    )


def body(
    image_emb, text_emb, image_valid, text_valid, sample_count, logit_scale, logit_bias, loss_grad
):
    text_block = lax.all_gather(text_emb, "row", axis=1, tiled=True)
    per_device = image_emb.shape[0]
    col_count = lax.axis_size("col")
    col_index = lax.axis_index("col")
    row_index = lax.axis_index("row")
    text_count = text_block.shape[0]
    factor = loss_grad[0] * logit_scale[0] / sample_count[0].astype(jnp.float32)
    valid_wire = image_valid.astype(jnp.bfloat16)
    parity = col_index % 2
    bit_count = col_count.bit_length() - 1
    text_wire = text_valid.astype(jnp.bfloat16)
    other_texts, other_valid = partner((text_block, text_wire), "col", 0)
    own_first = parity == 0
    texts = jnp.where(
        own_first,
        jnp.concatenate([text_block, other_texts], 0),
        jnp.concatenate([other_texts, text_block], 0),
    )
    text_weights = jnp.where(
        own_first,
        jnp.concatenate([text_wire, other_valid], 0),
        jnp.concatenate([other_valid, text_wire], 0),
    ).astype(jnp.float32)
    text_ids = (col_index - parity) * text_count + jnp.arange(2 * text_count, dtype=jnp.int32)
    image_rows, valid_rows = (image_emb, valid_wire)
    for bit in range(1, bit_count):
        other_rows, other_counts = partner((image_rows, valid_rows), "col", bit)
        lower = col_index >> bit & 1 == 0
        image_rows = jnp.where(
            lower,
            jnp.concatenate([image_rows, other_rows], 0),
            jnp.concatenate([other_rows, image_rows], 0),
        )
        valid_rows = jnp.where(
            lower,
            jnp.concatenate([valid_rows, other_counts], 0),
            jnp.concatenate([other_counts, valid_rows], 0),
        )
    positions = jnp.arange(image_rows.shape[0], dtype=jnp.int32)
    row_ids = (
        row_index * col_count + 2 * (positions // per_device) + parity
    ) * per_device + positions % per_device
    coefficient = coefficients(
        image_rows,
        valid_rows,
        row_ids,
        texts,
        text_weights,
        text_ids,
        factor,
        logit_scale,
        logit_bias,
    )
    partial_image = jnp.dot(coefficient, texts, preferred_element_type=jnp.float32)
    for bit in range(bit_count - 1, 0, -1):
        half = partial_image.shape[0] // 2
        upper = col_index >> bit & 1 == 1
        send = jnp.where(upper, partial_image[:half], partial_image[half:])
        keep = jnp.where(upper, partial_image[half:], partial_image[:half])
        partial_image = keep + partner(send, "col", bit)
    partial_text = text_part(coefficient, image_rows)
    odd = parity == 1
    send_text = jnp.where(odd, partial_text[:text_count], partial_text[text_count:])
    keep_text = jnp.where(odd, partial_text[text_count:], partial_text[:text_count])
    text_partial = keep_text + partner(send_text, "col", 0)
    text_grad = lax.psum_scatter(text_partial, "row", scatter_dimension=1, tiled=True)
    return (partial_image.astype(jnp.bfloat16), text_grad.astype(jnp.bfloat16))


def solution(mesh):
    in_specs = (
        P(("row", "col"), None),
        P("col", "row"),
        P(("row", "col")),
        P("col"),
        P(),
        P(),
        P(),
        P(),
    )
    out_specs = (P(("row", "col"), None), P("col", "row"))
    paired = mesh.shape["row"] == 2 and mesh.shape["col"] == 16
    run = pair_body if paired else body
    return jax.shard_map(run, mesh=mesh, in_specs=in_specs, out_specs=out_specs, check_vma=False)
```

```python
import functools

import jax
import jax.numpy as jnp
from jax import lax
from jax.experimental import pallas as pl
from jax.experimental.pallas import tpu as pltpu
from jax.sharding import PartitionSpec as P

SPARE = 8
LINE = 256


def hop(block, image_bit, text_bit, across=False):
    count = lax.axis_size("col")
    turn = count if across else 0
    route = [(c, turn + (c ^ image_bit)) for c in range(count)]
    route += [(count + c, count - turn + (c ^ text_bit)) for c in range(count)]
    return lax.ppermute(block, ("row", "col"), route)


def swap(block):
    return lax.ppermute(block, "row", [(0, 1), (1, 0)])


def masks(count, row):
    top = count // 2
    near, far = (1, 2), (top, top // 2)
    if row is None:
        return near, far
    return tuple(jnp.where(row == 0, *pair) for pair in (near, far, near[::-1], far[::-1]))


def put_line(ref, *pieces):
    pieces = [piece.astype(jnp.float32) for piece in pieces]
    pieces += [jnp.zeros((1, LINE - sum(piece.shape[1] for piece in pieces)), jnp.float32)]
    line = jnp.broadcast_to(jnp.concatenate(pieces, axis=1), (SPARE, LINE))
    ref[ref.shape[0] - SPARE :, :LINE] = line.astype(ref.dtype)


def put_texts(ref, text_ref):
    half, part = text_ref.shape[0] // 2, text_ref.shape[1]
    ref[:half, :part] = text_ref[:half]
    ref[:half, part:] = text_ref[half:]


def first_kernel(spot_ref, image_ref, text_ref, image_valid_ref, text_valid_ref, mine_ref, give_ref, texts, image_line,
                 text_line, sems):
    half = image_ref.shape[0]

    def fill(image_to, text_to):
        copies = [
            pltpu.make_async_copy(source, target, sems.at[n])
            for n, (source, target) in enumerate((
                (text_ref, texts), (image_ref, image_to.at[pl.ds(0, half)]), (image_valid_ref, image_line),
                (text_valid_ref, text_line)))
        ]
        for copy in copies:
            copy.start()
        copies[0].wait()
        put_texts(text_to, texts)
        for copy in copies[1:]:
            copy.wait()
        put_line(image_to, image_line[...])
        put_line(text_to, text_line[...])

    @pl.when(spot_ref[0] == 0)
    def _():
        fill(mine_ref, give_ref)

    @pl.when(spot_ref[0] != 0)
    def _():
        fill(give_ref, mine_ref)


def unpack(pair, texts, out_ref, start):
    one, two = pair
    half, part = one.shape[0] - SPARE, one.shape[1] // 2

    @pl.when(texts)
    def _():
        out_ref[start : start + half, :part] = two[:half, :part]
        out_ref[start : start + half, part:] = one[:half, :part]
        out_ref[start + half : start + 2 * half, :part] = two[:half, part:]
        out_ref[start + half : start + 2 * half, part:] = one[:half, part:]

    @pl.when(jnp.logical_not(texts))
    def _():
        out_ref[start : start + half] = one[:half]
        out_ref[start + half : start + 2 * half] = two[:half]


def counts(pair, texts):
    one, two = pair
    half = one.shape[0] - SPARE
    line_one = one[half:, :LINE].astype(jnp.float32)[:1]
    line_two = two[half:, :LINE].astype(jnp.float32)[:1]
    images = jnp.concatenate([line_one[:, :half], line_two[:, :half]], axis=1)
    return jnp.where(texts, line_one[:, : 2 * half], images)


def upright(line):
    size = line.shape[1]
    at = lax.broadcasted_iota(jnp.int32, (size, size), 0)
    to = lax.broadcasted_iota(jnp.int32, (size, size), 1)
    return jnp.sum(jnp.where(at == to, line, 0.0), axis=1, keepdims=True)


def sample_ids(col, texts, half, cols, axis):
    shape = (2 * half, 1) if axis == 0 else (1, 2 * half)
    at = lax.broadcasted_iota(jnp.int32, shape, axis)
    jump = jnp.where(texts, 0, (cols - 1) * half)
    first = col * jnp.where(texts, 2 * half, half)
    return at + first + jnp.where(at >= half, jump, 0)


def coefficients_of(cols, row_ref, col_ref, number_ref, mine, others, my_sets, other_sets):
    row, col = row_ref[0], col_ref[0]
    my_texts, other_texts = row != 0, row == 0
    near, far, other_near, other_far = masks(cols, row)
    my_masks = {"own": 0, "near": near, "far": far, "both": near ^ far}
    other_masks = {"own": 0, "near": other_near, "far": other_far, "both": other_near ^ other_far}
    half = my_sets[0][1][0].shape[0] - SPARE
    scale, bias, factor = (number_ref[n : n + 1, :1] for n in range(3))
    my_ids = jnp.concatenate([sample_ids(col ^ my_masks[k], my_texts, half, cols, 0) for k, _ in my_sets], axis=0)
    other_ids = jnp.concatenate(
        [sample_ids(col ^ other_masks[k], other_texts, half, cols, 1) for k, _ in other_sets], axis=1)
    my_weights = jnp.concatenate([upright(counts(pair, my_texts)) for _, pair in my_sets], axis=0)
    other_weights = factor * jnp.concatenate([counts(pair, other_texts) for _, pair in other_sets], axis=1)
    logits = lax.dot_general(mine, others, (((1,), (1,)), ((), ())), preferred_element_type=jnp.float32)
    logits = logits * scale + bias
    match = my_ids == other_ids
    rate = 1.0 / (1.0 + jnp.exp(jnp.where(match, logits, -logits)))
    return (jnp.where(match, -rate, rate) * my_weights * other_weights).astype(jnp.bfloat16)


def pairs(refs):
    return [refs[n : n + 2] for n in range(0, len(refs), 2)]


THREE = ("own", "near", "far")


def number_kernel(scale_ref, bias_ref, grad_ref, sample_ref, out_ref):
    factor = grad_ref[0] * scale_ref[0] / sample_ref[0].astype(jnp.float32)
    line = lax.broadcasted_iota(jnp.int32, out_ref.shape, 0)
    out_ref[...] = jnp.where(line == 0, scale_ref[0], jnp.where(line == 1, bias_ref[0], factor))


def early_kernel(cols, row_ref, col_ref, number_ref, *refs):
    mine_pairs, other_pairs = pairs(refs[:6]), pairs(refs[6:12])
    mine_ref, others_ref, total_ref = refs[12:]
    texts = row_ref[0] != 0
    size = 2 * (refs[0].shape[0] - SPARE)
    for n in range(3):
        unpack(mine_pairs[n], texts, mine_ref, n * size)
        unpack(other_pairs[n], jnp.logical_not(texts), others_ref, n * size)
    others = others_ref[...]
    coefficient = coefficients_of(cols, row_ref, col_ref, number_ref, mine_ref[...], others,
                                  list(zip(THREE, mine_pairs)), list(zip(THREE, other_pairs)))
    total_ref[...] = jnp.dot(coefficient, others, preferred_element_type=jnp.float32)


def both_kernel(cols, row_ref, col_ref, number_ref, *refs):
    mine_pair, other_pairs = refs[:2], pairs(refs[2:8])
    others_ref, mine_ref, total_ref = refs[8:]
    unpack(mine_pair, row_ref[0] != 0, mine_ref, 0)
    others = others_ref[...]
    coefficient = coefficients_of(cols, row_ref, col_ref, number_ref, mine_ref[...], others,
                                  [("both", mine_pair)], list(zip(THREE, other_pairs)))
    total_ref[...] = jnp.dot(coefficient, others, preferred_element_type=jnp.float32)


def pack_sum(total, texts, stay_ref, cross_ref):
    half, part = total.shape[0] // 2, total.shape[1] // 2

    @pl.when(texts)
    def _():
        stay_ref[:, :part] = total[:half, part:].astype(stay_ref.dtype)
        stay_ref[:, part:] = total[half:, part:].astype(stay_ref.dtype)
        cross_ref[:, :part] = total[:half, :part].astype(cross_ref.dtype)
        cross_ref[:, part:] = total[half:, :part].astype(cross_ref.dtype)

    @pl.when(jnp.logical_not(texts))
    def _():
        stay_ref[...] = total[:half].astype(stay_ref.dtype)
        cross_ref[...] = total[half:].astype(cross_ref.dtype)


def late_kernel(cols, row_ref, col_ref, number_ref, *refs):
    mine_pair, other_pair = refs[:2], refs[2:4]
    mine_ref, total_ref = refs[4:6]
    others_ref, stay_ref, cross_ref = refs[6:]
    texts = row_ref[0] != 0
    unpack(other_pair, jnp.logical_not(texts), others_ref, 0)
    others = others_ref[...]
    coefficient = coefficients_of(cols, row_ref, col_ref, number_ref, mine_ref[...], others,
                                  [("both", mine_pair)], [("both", other_pair)])
    total = total_ref[...] + jnp.dot(coefficient, others, preferred_element_type=jnp.float32)
    pack_sum(total, texts, stay_ref, cross_ref)


def rest_kernel(cols, row_ref, col_ref, number_ref, *refs):
    mine_pairs, other_pair = pairs(refs[:6]), refs[6:8]
    mine_ref, others_ref, total_ref = refs[8:11]
    own_stay, own_cross, near_stay, near_cross, far_stay, far_cross = refs[11:]
    texts = row_ref[0] != 0
    others = others_ref[...]
    coefficient = coefficients_of(cols, row_ref, col_ref, number_ref, mine_ref[...], others,
                                  list(zip(THREE, mine_pairs)), [("both", other_pair)])
    total = total_ref[...] + jnp.dot(coefficient, others, preferred_element_type=jnp.float32)
    size = total.shape[0] // 3
    pack_sum(total[2 * size :], texts, far_stay, far_cross)
    pack_sum(total[size : 2 * size], texts, near_stay, near_cross)
    pack_sum(total[:size], texts, own_stay, own_cross)


def last_kernel(spot_ref, stay_ref, crossed_ref, near_stay_ref, near_cross_ref, image_ref, text_ref):
    half, part = text_ref.shape[0] // 2, text_ref.shape[1]

    stay = (stay_ref[...] + near_stay_ref[...].astype(jnp.float32)).astype(image_ref.dtype)
    crossed = (crossed_ref[...] + near_cross_ref[...].astype(jnp.float32)).astype(image_ref.dtype)

    def put(images, texts):
        image_ref[...] = images
        text_ref[:half] = texts[:, :part]
        text_ref[half:] = texts[:, part:]

    @pl.when(spot_ref[0] == 0)
    def _():
        put(stay, crossed)

    @pl.when(spot_ref[0] != 0)
    def _():
        put(crossed, stay)


def call(kernel, out_shape, smem, *arrays, flops=0):
    size = sum(a.size * a.dtype.itemsize for a in (*arrays, *jax.tree.leaves(out_shape)))
    return pl.pallas_call(
        kernel,
        out_shape=out_shape,
        in_specs=[pl.BlockSpec(memory_space=pltpu.SMEM)] * smem
        + [pl.BlockSpec(memory_space=pltpu.VMEM)] * (len(arrays) - smem),
        out_specs=jax.tree.map(lambda _: pl.BlockSpec(memory_space=pltpu.VMEM), out_shape),
        compiler_params=pltpu.CompilerParams(vmem_limit_bytes=24 * 1024 * 1024),
        cost_estimate=pl.CostEstimate(flops=flops, bytes_accessed=size, transcendentals=0),
    )(*arrays)


def pair_body(
    image_emb, text_emb, image_valid, text_valid, sample_count, logit_scale, logit_bias, loss_grad
):
    half, width = image_emb.shape
    size = 2 * half
    cols = lax.axis_size("col")
    row, col = lax.axis_index("row")[None], lax.axis_index("col")[None]
    near, far = masks(cols, None)

    def shape(rows, dtype):
        return jax.ShapeDtypeStruct((rows, width), dtype)

    bf16, f32 = jnp.bfloat16, jnp.float32
    sent = shape(half + SPARE, bf16)
    first = (image_emb, text_emb, image_valid[None], text_valid[None])
    own_a, give = pl.pallas_call(
        first_kernel,
        out_shape=(sent, sent),
        in_specs=[pl.BlockSpec(memory_space=pltpu.SMEM)] + [pl.BlockSpec(memory_space=pltpu.HBM)] * 4,
        out_specs=(pl.BlockSpec(memory_space=pltpu.VMEM),) * 2,
        scratch_shapes=[pltpu.VMEM(a.shape, a.dtype) for a in first[1:]] + [pltpu.SemaphoreType.DMA((4,))],
        compiler_params=pltpu.CompilerParams(vmem_limit_bytes=60 * 1024 * 1024),
    )(row, *first)
    far_a = hop(own_a, *far)
    own_b = swap(give)
    far_b = hop(own_b, *far)
    near_a = hop(own_a, *near)
    near_b = hop(own_b, *near)
    both_a = hop(far_a, *near)
    both_b = hop(far_b, *near)
    mine = (own_a, own_b, near_a, near_b, far_a, far_b)
    number = call(number_kernel, jax.ShapeDtypeStruct((8, 128), f32), 4, logit_scale, logit_bias, loss_grad, sample_count)
    near_a, number = lax.optimization_barrier((near_a, number))
    others = (swap(own_a), give, swap(near_a), swap(near_b), swap(far_a), swap(far_b))
    others, other_both_a = lax.optimization_barrier((others, swap(both_a)))

    pair_flops = 4 * size * size * width
    scalars = (row, col, number)
    mine_rows, other_rows, early = call(
        functools.partial(early_kernel, cols), (shape(3 * size, bf16), shape(3 * size, bf16), shape(3 * size, f32)),
        2, *scalars, *mine, *others, flops=9 * pair_flops)
    both_b, early = lax.optimization_barrier((both_b, early))
    both = (both_a, both_b)
    other_both = (other_both_a, swap(both_b))
    both_rows, both_early = call(
        functools.partial(both_kernel, cols), (shape(size, bf16), shape(size, f32)), 2, *scalars, *both, *others,
        other_rows, flops=3 * pair_flops)
    other_late, late_stay, late_cross = call(
        functools.partial(late_kernel, cols), (shape(size, bf16), shape(half, bf16), shape(half, bf16)), 2, *scalars,
        *both, *other_both, both_rows, both_early, flops=pair_flops)
    in_cross = hop(late_cross, *near)
    in_stay = hop(late_stay, *near)
    own_stay, own_cross, near_stay, near_cross, far_stay, far_cross = call(
        functools.partial(rest_kernel, cols),
        (shape(half, f32), shape(half, f32), shape(half, bf16), shape(half, bf16), shape(half, f32), shape(half, f32)),
        2, *scalars, *mine, *other_both, mine_rows, other_late, early, flops=3 * pair_flops)
    crossed = swap(own_cross)
    far_cross = (far_cross + in_cross.astype(f32)).astype(bf16)
    far_stay = (far_stay + in_stay.astype(f32)).astype(bf16)
    near_stay, _ = lax.optimization_barrier((near_stay, far_stay))
    near_stay = hop(near_stay, *near)
    near_cross, _, _ = lax.optimization_barrier((near_cross, far_cross, far_stay))
    far_cross = hop(far_cross, *far, across=True)
    far_stay = hop(far_stay, *far)
    near_cross = hop(near_cross, *near, across=True)
    own_stay = own_stay + far_stay.astype(f32)
    crossed = crossed + far_cross.astype(f32)
    return call(last_kernel, (shape(half, bf16), jax.ShapeDtypeStruct(text_emb.shape, bf16)), 1, row, own_stay, crossed,
                near_stay, near_cross)


def partner(block, axis, distance):
    count = lax.axis_size(axis)
    route = []
    for low in range(count):
        high = low | 1 << distance
        if high != low and high < count:
            route += [(low, high), (high, low)]
    return lax.ppermute(block, axis, route)


def coefficients(
    image_rows, valid_rows, row_ids, texts, weight_text, text_ids, factor, logit_scale, logit_bias
):
    logits = lax.dot_general(
        image_rows, texts, (((1,), (1,)), ((), ())), preferred_element_type=jnp.float32
    )
    logits = logits * logit_scale[0] + logit_bias[0]
    label_sign = jnp.where(row_ids[:, None] == text_ids[None, :], 1.0, -1.0).astype(jnp.float32)
    weights = valid_rows.astype(jnp.float32)[:, None] * weight_text[None, :]
    return (-factor * label_sign * jax.nn.sigmoid(-label_sign * logits) * weights).astype(
        jnp.bfloat16
    )


def text_part(coefficient, image_rows):
    return lax.dot_general(
        coefficient, image_rows, (((0,), (0,)), ((), ())), preferred_element_type=jnp.float32
    )


def body(
    image_emb, text_emb, image_valid, text_valid, sample_count, logit_scale, logit_bias, loss_grad
):
    text_block = lax.all_gather(text_emb, "row", axis=1, tiled=True)
    per_device = image_emb.shape[0]
    col_count = lax.axis_size("col")
    col_index = lax.axis_index("col")
    row_index = lax.axis_index("row")
    text_count = text_block.shape[0]
    factor = loss_grad[0] * logit_scale[0] / sample_count[0].astype(jnp.float32)
    valid_wire = image_valid.astype(jnp.bfloat16)
    parity = col_index % 2
    bit_count = col_count.bit_length() - 1
    text_wire = text_valid.astype(jnp.bfloat16)
    other_texts, other_valid = partner((text_block, text_wire), "col", 0)
    own_first = parity == 0
    texts = jnp.where(
        own_first,
        jnp.concatenate([text_block, other_texts], 0),
        jnp.concatenate([other_texts, text_block], 0),
    )
    text_weights = jnp.where(
        own_first,
        jnp.concatenate([text_wire, other_valid], 0),
        jnp.concatenate([other_valid, text_wire], 0),
    ).astype(jnp.float32)
    text_ids = (col_index - parity) * text_count + jnp.arange(2 * text_count, dtype=jnp.int32)
    image_rows, valid_rows = (image_emb, valid_wire)
    for bit in range(1, bit_count):
        other_rows, other_counts = partner((image_rows, valid_rows), "col", bit)
        lower = col_index >> bit & 1 == 0
        image_rows = jnp.where(
            lower,
            jnp.concatenate([image_rows, other_rows], 0),
            jnp.concatenate([other_rows, image_rows], 0),
        )
        valid_rows = jnp.where(
            lower,
            jnp.concatenate([valid_rows, other_counts], 0),
            jnp.concatenate([other_counts, valid_rows], 0),
        )
    positions = jnp.arange(image_rows.shape[0], dtype=jnp.int32)
    row_ids = (
        row_index * col_count + 2 * (positions // per_device) + parity
    ) * per_device + positions % per_device
    coefficient = coefficients(
        image_rows,
        valid_rows,
        row_ids,
        texts,
        text_weights,
        text_ids,
        factor,
        logit_scale,
        logit_bias,
    )
    partial_image = jnp.dot(coefficient, texts, preferred_element_type=jnp.float32)
    for bit in range(bit_count - 1, 0, -1):
        half = partial_image.shape[0] // 2
        upper = col_index >> bit & 1 == 1
        send = jnp.where(upper, partial_image[:half], partial_image[half:])
        keep = jnp.where(upper, partial_image[half:], partial_image[:half])
        partial_image = keep + partner(send, "col", bit)
    partial_text = text_part(coefficient, image_rows)
    odd = parity == 1
    send_text = jnp.where(odd, partial_text[:text_count], partial_text[text_count:])
    keep_text = jnp.where(odd, partial_text[text_count:], partial_text[:text_count])
    text_partial = keep_text + partner(send_text, "col", 0)
    text_grad = lax.psum_scatter(text_partial, "row", scatter_dimension=1, tiled=True)
    return (partial_image.astype(jnp.bfloat16), text_grad.astype(jnp.bfloat16))


def solution(mesh):
    in_specs = (
        P(("row", "col"), None),
        P("col", "row"),
        P(("row", "col")),
        P("col"),
        P(),
        P(),
        P(),
        P(),
    )
    out_specs = (P(("row", "col"), None), P("col", "row"))
    paired = mesh.shape["row"] == 2 and mesh.shape["col"] == 16
    run = pair_body if paired else body
    return jax.shard_map(run, mesh=mesh, in_specs=in_specs, out_specs=out_specs, check_vma=False)
```

```python
import functools

import jax
import jax.numpy as jnp
from jax import lax
from jax.experimental import pallas as pl
from jax.experimental.pallas import tpu as pltpu
from jax.sharding import PartitionSpec as P

SPARE = 8
LINE = 256


def hop(block, image_bit, text_bit, across=False):
    count = lax.axis_size("col")
    turn = count if across else 0
    route = [(c, turn + (c ^ image_bit)) for c in range(count)]
    route += [(count + c, count - turn + (c ^ text_bit)) for c in range(count)]
    return lax.ppermute(block, ("row", "col"), route)


def swap(block):
    return lax.ppermute(block, "row", [(0, 1), (1, 0)])


def masks(count, row):
    top = count // 2
    near, far = (1, 2), (top, top // 2)
    if row is None:
        return near, far
    return tuple(jnp.where(row == 0, *pair) for pair in (near, far, near[::-1], far[::-1]))


def put_line(ref, *pieces):
    pieces = [piece.astype(jnp.float32) for piece in pieces]
    pieces += [jnp.zeros((1, LINE - sum(piece.shape[1] for piece in pieces)), jnp.float32)]
    line = jnp.broadcast_to(jnp.concatenate(pieces, axis=1), (SPARE, LINE))
    ref[ref.shape[0] - SPARE :, :LINE] = line.astype(ref.dtype)


def put_texts(ref, text_ref):
    half, part = text_ref.shape[0] // 2, text_ref.shape[1]
    ref[:half, :part] = text_ref[:half]
    ref[:half, part:] = text_ref[half:]


def first_kernel(row_ref, image_ref, text_ref, image_valid_ref, text_valid_ref, mine_ref, give_ref, images, packed, texts,
                 image_line, text_line, sems):
    half = image_ref.shape[0]
    copies = [
        pltpu.make_async_copy(source, target, sems.at[n])
        for n, (source, target) in enumerate((
            (image_ref, images.at[pl.ds(0, half)]), (image_valid_ref, image_line), (text_ref, texts),
            (text_valid_ref, text_line)))
    ]
    for copy in copies:
        copy.start()

    def fill(image_to, text_to):
        copies[0].wait()
        copies[1].wait()
        put_line(images, image_line[...])
        image_out = pltpu.make_async_copy(images, image_to, sems.at[4])
        image_out.start()
        copies[2].wait()
        copies[3].wait()
        put_texts(packed, texts)
        put_line(packed, text_line[...])
        text_out = pltpu.make_async_copy(packed, text_to, sems.at[5])
        text_out.start()
        image_out.wait()
        text_out.wait()

    @pl.when(row_ref[0] == 0)
    def _():
        fill(mine_ref, give_ref)

    @pl.when(row_ref[0] != 0)
    def _():
        fill(give_ref, mine_ref)


def unpack(pair, texts, out_ref, start):
    one, two = pair
    half, part = one.shape[0] - SPARE, one.shape[1] // 2

    @pl.when(texts)
    def _():
        out_ref[start : start + half, :part] = two[:half, :part]
        out_ref[start : start + half, part:] = one[:half, :part]
        out_ref[start + half : start + 2 * half, :part] = two[:half, part:]
        out_ref[start + half : start + 2 * half, part:] = one[:half, part:]

    @pl.when(jnp.logical_not(texts))
    def _():
        out_ref[start : start + half] = one[:half]
        out_ref[start + half : start + 2 * half] = two[:half]


def counts(pair, texts):
    one, two = pair
    half = one.shape[0] - SPARE
    line_one = one[half:, :LINE].astype(jnp.float32)[:1]
    line_two = two[half:, :LINE].astype(jnp.float32)[:1]
    images = jnp.concatenate([line_one[:, :half], line_two[:, :half]], axis=1)
    return jnp.where(texts, line_one[:, : 2 * half], images)


def upright(line):
    size = line.shape[1]
    at = lax.broadcasted_iota(jnp.int32, (size, size), 0)
    to = lax.broadcasted_iota(jnp.int32, (size, size), 1)
    return jnp.sum(jnp.where(at == to, line, 0.0), axis=1, keepdims=True)


def sample_ids(col, texts, half, cols, axis):
    shape = (2 * half, 1) if axis == 0 else (1, 2 * half)
    at = lax.broadcasted_iota(jnp.int32, shape, axis)
    jump = jnp.where(texts, 0, (cols - 1) * half)
    first = col * jnp.where(texts, 2 * half, half)
    return at + first + jnp.where(at >= half, jump, 0)


def coefficients_of(cols, row_ref, col_ref, number_ref, mine, others, my_sets, other_sets):
    row, col = row_ref[0], col_ref[0]
    my_texts, other_texts = row != 0, row == 0
    near, far, other_near, other_far = masks(cols, row)
    my_masks = {"own": 0, "near": near, "far": far, "both": near ^ far}
    other_masks = {"own": 0, "near": other_near, "far": other_far, "both": other_near ^ other_far}
    half = my_sets[0][1][0].shape[0] - SPARE
    scale, bias, factor = (number_ref[n : n + 1, :1] for n in range(3))
    my_ids = jnp.concatenate([sample_ids(col ^ my_masks[k], my_texts, half, cols, 0) for k, _ in my_sets], axis=0)
    other_ids = jnp.concatenate(
        [sample_ids(col ^ other_masks[k], other_texts, half, cols, 1) for k, _ in other_sets], axis=1)
    my_weights = jnp.concatenate([upright(counts(pair, my_texts)) for _, pair in my_sets], axis=0)
    other_weights = factor * jnp.concatenate([counts(pair, other_texts) for _, pair in other_sets], axis=1)
    logits = lax.dot_general(mine, others, (((1,), (1,)), ((), ())), preferred_element_type=jnp.float32)
    logits = logits * scale + bias
    match = my_ids == other_ids
    rate = 1.0 / (1.0 + jnp.exp(jnp.where(match, logits, -logits)))
    return (jnp.where(match, -rate, rate) * my_weights * other_weights).astype(jnp.bfloat16)


def pairs(refs):
    return [refs[n : n + 2] for n in range(0, len(refs), 2)]


THREE = ("own", "near", "far")


def number_kernel(scale_ref, bias_ref, grad_ref, sample_ref, out_ref):
    factor = grad_ref[0] * scale_ref[0] / sample_ref[0].astype(jnp.float32)
    line = lax.broadcasted_iota(jnp.int32, out_ref.shape, 0)
    out_ref[...] = jnp.where(line == 0, scale_ref[0], jnp.where(line == 1, bias_ref[0], factor))


def early_kernel(cols, row_ref, col_ref, number_ref, *refs):
    mine_pairs, other_pairs = pairs(refs[:6]), pairs(refs[6:12])
    mine_ref, others_ref, total_ref = refs[12:]
    texts = row_ref[0] != 0
    size = 2 * (refs[0].shape[0] - SPARE)
    for n in range(3):
        unpack(mine_pairs[n], texts, mine_ref, n * size)
        unpack(other_pairs[n], jnp.logical_not(texts), others_ref, n * size)
    others = others_ref[...]
    coefficient = coefficients_of(cols, row_ref, col_ref, number_ref, mine_ref[...], others,
                                  list(zip(THREE, mine_pairs)), list(zip(THREE, other_pairs)))
    total_ref[...] = jnp.dot(coefficient, others, preferred_element_type=jnp.float32)


def both_kernel(cols, row_ref, col_ref, number_ref, *refs):
    mine_pair, other_pairs = refs[:2], pairs(refs[2:8])
    others_ref, mine_ref, total_ref = refs[8:]
    unpack(mine_pair, row_ref[0] != 0, mine_ref, 0)
    others = others_ref[...]
    coefficient = coefficients_of(cols, row_ref, col_ref, number_ref, mine_ref[...], others,
                                  [("both", mine_pair)], list(zip(THREE, other_pairs)))
    total_ref[...] = jnp.dot(coefficient, others, preferred_element_type=jnp.float32)


def pack_sum(total, texts, stay_ref, cross_ref):
    half, part = total.shape[0] // 2, total.shape[1] // 2

    @pl.when(texts)
    def _():
        stay_ref[:, :part] = total[:half, part:].astype(stay_ref.dtype)
        stay_ref[:, part:] = total[half:, part:].astype(stay_ref.dtype)
        cross_ref[:, :part] = total[:half, :part].astype(cross_ref.dtype)
        cross_ref[:, part:] = total[half:, :part].astype(cross_ref.dtype)

    @pl.when(jnp.logical_not(texts))
    def _():
        stay_ref[...] = total[:half].astype(stay_ref.dtype)
        cross_ref[...] = total[half:].astype(cross_ref.dtype)


def late_kernel(cols, row_ref, col_ref, number_ref, *refs):
    mine_pair, other_pair = refs[:2], refs[2:4]
    mine_ref, total_ref = refs[4:6]
    others_ref, stay_ref, cross_ref = refs[6:]
    texts = row_ref[0] != 0
    unpack(other_pair, jnp.logical_not(texts), others_ref, 0)
    others = others_ref[...]
    coefficient = coefficients_of(cols, row_ref, col_ref, number_ref, mine_ref[...], others,
                                  [("both", mine_pair)], [("both", other_pair)])
    total = total_ref[...] + jnp.dot(coefficient, others, preferred_element_type=jnp.float32)
    pack_sum(total, texts, stay_ref, cross_ref)


def rest_kernel(cols, row_ref, col_ref, number_ref, *refs):
    mine_pairs, other_pair = pairs(refs[:6]), refs[6:8]
    mine_ref, others_ref, total_ref = refs[8:11]
    own_stay, own_cross, near_stay, near_cross, far_stay, far_cross = refs[11:]
    texts = row_ref[0] != 0
    others = others_ref[...]
    coefficient = coefficients_of(cols, row_ref, col_ref, number_ref, mine_ref[...], others,
                                  list(zip(THREE, mine_pairs)), [("both", other_pair)])
    total = total_ref[...] + jnp.dot(coefficient, others, preferred_element_type=jnp.float32)
    size = total.shape[0] // 3
    pack_sum(total[2 * size :], texts, far_stay, far_cross)
    pack_sum(total[size : 2 * size], texts, near_stay, near_cross)
    pack_sum(total[:size], texts, own_stay, own_cross)


def last_kernel(row_ref, stay_ref, crossed_ref, near_stay_ref, near_cross_ref, image_ref, text_ref, images, texts, sems):
    half, part = text_ref.shape[0] // 2, text_ref.shape[1]

    def put(image_sums, text_sums):
        images[...] = (image_sums[0][...] + image_sums[1][...].astype(jnp.float32)).astype(images.dtype)
        image_out = pltpu.make_async_copy(images, image_ref, sems.at[0])
        image_out.start()
        rows = (text_sums[0][...] + text_sums[1][...].astype(jnp.float32)).astype(texts.dtype)
        texts[:half] = rows[:, :part]
        texts[half:] = rows[:, part:]
        text_out = pltpu.make_async_copy(texts, text_ref, sems.at[1])
        text_out.start()
        image_out.wait()
        text_out.wait()

    @pl.when(row_ref[0] == 0)
    def _():
        put((stay_ref, near_stay_ref), (crossed_ref, near_cross_ref))

    @pl.when(row_ref[0] != 0)
    def _():
        put((crossed_ref, near_cross_ref), (stay_ref, near_stay_ref))


def call(kernel, out_shape, smem, *arrays, flops=0):
    size = sum(a.size * a.dtype.itemsize for a in (*arrays, *jax.tree.leaves(out_shape)))
    return pl.pallas_call(
        kernel,
        out_shape=out_shape,
        in_specs=[pl.BlockSpec(memory_space=pltpu.SMEM)] * smem
        + [pl.BlockSpec(memory_space=pltpu.VMEM)] * (len(arrays) - smem),
        out_specs=jax.tree.map(lambda _: pl.BlockSpec(memory_space=pltpu.VMEM), out_shape),
        compiler_params=pltpu.CompilerParams(vmem_limit_bytes=24 * 1024 * 1024),
        cost_estimate=pl.CostEstimate(flops=flops, bytes_accessed=size, transcendentals=0),
    )(*arrays)


def pair_body(
    image_emb, text_emb, image_valid, text_valid, sample_count, logit_scale, logit_bias, loss_grad
):
    half, width = image_emb.shape
    size = 2 * half
    cols = lax.axis_size("col")
    row, col = lax.axis_index("row")[None], lax.axis_index("col")[None]
    near, far = masks(cols, None)

    def shape(rows, dtype):
        return jax.ShapeDtypeStruct((rows, width), dtype)

    bf16, f32 = jnp.bfloat16, jnp.float32
    sent = shape(half + SPARE, bf16)
    first = (image_emb, text_emb, image_valid[None], text_valid[None])
    own_a, give = pl.pallas_call(
        first_kernel,
        out_shape=(sent, sent),
        in_specs=[pl.BlockSpec(memory_space=pltpu.SMEM)] + [pl.BlockSpec(memory_space=pltpu.HBM)] * 4,
        out_specs=(pl.BlockSpec(memory_space=pltpu.HBM),) * 2,
        scratch_shapes=[pltpu.VMEM(sent.shape, bf16)] * 2 + [pltpu.VMEM(a.shape, a.dtype) for a in first[1:]]
        + [pltpu.SemaphoreType.DMA((6,))],
        compiler_params=pltpu.CompilerParams(vmem_limit_bytes=60 * 1024 * 1024),
    )(row, *first)
    far_a = hop(own_a, *far)
    own_b = swap(give)
    far_b = hop(own_b, *far)
    near_a = hop(own_a, *near)
    near_b = hop(own_b, *near)
    both_a = hop(far_a, *near)
    both_b = hop(far_b, *near)
    mine = (own_a, own_b, near_a, near_b, far_a, far_b)
    number = call(number_kernel, jax.ShapeDtypeStruct((8, 128), f32), 4, logit_scale, logit_bias, loss_grad, sample_count)
    near_a, number = lax.optimization_barrier((near_a, number))
    others = (swap(own_a), give, swap(near_a), swap(near_b), swap(far_a), swap(far_b))
    others, other_both_a = lax.optimization_barrier((others, swap(both_a)))

    pair_flops = 4 * size * size * width
    scalars = (row, col, number)
    mine_rows, other_rows, early = call(
        functools.partial(early_kernel, cols), (shape(3 * size, bf16), shape(3 * size, bf16), shape(3 * size, f32)),
        2, *scalars, *mine, *others, flops=9 * pair_flops)
    both_b, early = lax.optimization_barrier((both_b, early))
    both = (both_a, both_b)
    other_both = (other_both_a, swap(both_b))
    both_rows, both_early = call(
        functools.partial(both_kernel, cols), (shape(size, bf16), shape(size, f32)), 2, *scalars, *both, *others,
        other_rows, flops=3 * pair_flops)
    other_late, late_stay, late_cross = call(
        functools.partial(late_kernel, cols), (shape(size, bf16), shape(half, bf16), shape(half, bf16)), 2, *scalars,
        *both, *other_both, both_rows, both_early, flops=pair_flops)
    in_cross = hop(late_cross, *near)
    in_stay = hop(late_stay, *near)
    own_stay, own_cross, near_stay, near_cross, far_stay, far_cross = call(
        functools.partial(rest_kernel, cols),
        (shape(half, f32), shape(half, f32), shape(half, bf16), shape(half, bf16), shape(half, f32), shape(half, f32)),
        2, *scalars, *mine, *other_both, mine_rows, other_late, early, flops=3 * pair_flops)
    crossed = swap(own_cross)
    far_cross = (far_cross + in_cross.astype(f32)).astype(bf16)
    far_stay = (far_stay + in_stay.astype(f32)).astype(bf16)
    near_stay, _ = lax.optimization_barrier((near_stay, far_stay))
    near_stay = hop(near_stay, *near)
    near_cross, _, _ = lax.optimization_barrier((near_cross, far_cross, far_stay))
    far_cross = hop(far_cross, *far, across=True)
    far_stay = hop(far_stay, *far)
    near_cross = hop(near_cross, *near, across=True)
    own_stay = own_stay + far_stay.astype(f32)
    crossed = crossed + far_cross.astype(f32)
    outs = (shape(half, bf16), jax.ShapeDtypeStruct(text_emb.shape, bf16))
    return pl.pallas_call(
        last_kernel,
        out_shape=outs,
        in_specs=[pl.BlockSpec(memory_space=pltpu.SMEM)] + [pl.BlockSpec(memory_space=pltpu.VMEM)] * 4,
        out_specs=(pl.BlockSpec(memory_space=pltpu.HBM),) * 2,
        scratch_shapes=[pltpu.VMEM(out.shape, out.dtype) for out in outs] + [pltpu.SemaphoreType.DMA((2,))],
        compiler_params=pltpu.CompilerParams(vmem_limit_bytes=24 * 1024 * 1024),
    )(row, own_stay, crossed, near_stay, near_cross)


def partner(block, axis, distance):
    count = lax.axis_size(axis)
    route = []
    for low in range(count):
        high = low | 1 << distance
        if high != low and high < count:
            route += [(low, high), (high, low)]
    return lax.ppermute(block, axis, route)


def coefficients(
    image_rows, valid_rows, row_ids, texts, weight_text, text_ids, factor, logit_scale, logit_bias
):
    logits = lax.dot_general(
        image_rows, texts, (((1,), (1,)), ((), ())), preferred_element_type=jnp.float32
    )
    logits = logits * logit_scale[0] + logit_bias[0]
    label_sign = jnp.where(row_ids[:, None] == text_ids[None, :], 1.0, -1.0).astype(jnp.float32)
    weights = valid_rows.astype(jnp.float32)[:, None] * weight_text[None, :]
    return (-factor * label_sign * jax.nn.sigmoid(-label_sign * logits) * weights).astype(
        jnp.bfloat16
    )


def text_part(coefficient, image_rows):
    return lax.dot_general(
        coefficient, image_rows, (((0,), (0,)), ((), ())), preferred_element_type=jnp.float32
    )


def body(
    image_emb, text_emb, image_valid, text_valid, sample_count, logit_scale, logit_bias, loss_grad
):
    text_block = lax.all_gather(text_emb, "row", axis=1, tiled=True)
    per_device = image_emb.shape[0]
    col_count = lax.axis_size("col")
    col_index = lax.axis_index("col")
    row_index = lax.axis_index("row")
    text_count = text_block.shape[0]
    factor = loss_grad[0] * logit_scale[0] / sample_count[0].astype(jnp.float32)
    valid_wire = image_valid.astype(jnp.bfloat16)
    parity = col_index % 2
    bit_count = col_count.bit_length() - 1
    text_wire = text_valid.astype(jnp.bfloat16)
    other_texts, other_valid = partner((text_block, text_wire), "col", 0)
    own_first = parity == 0
    texts = jnp.where(
        own_first,
        jnp.concatenate([text_block, other_texts], 0),
        jnp.concatenate([other_texts, text_block], 0),
    )
    text_weights = jnp.where(
        own_first,
        jnp.concatenate([text_wire, other_valid], 0),
        jnp.concatenate([other_valid, text_wire], 0),
    ).astype(jnp.float32)
    text_ids = (col_index - parity) * text_count + jnp.arange(2 * text_count, dtype=jnp.int32)
    image_rows, valid_rows = (image_emb, valid_wire)
    for bit in range(1, bit_count):
        other_rows, other_counts = partner((image_rows, valid_rows), "col", bit)
        lower = col_index >> bit & 1 == 0
        image_rows = jnp.where(
            lower,
            jnp.concatenate([image_rows, other_rows], 0),
            jnp.concatenate([other_rows, image_rows], 0),
        )
        valid_rows = jnp.where(
            lower,
            jnp.concatenate([valid_rows, other_counts], 0),
            jnp.concatenate([other_counts, valid_rows], 0),
        )
    positions = jnp.arange(image_rows.shape[0], dtype=jnp.int32)
    row_ids = (
        row_index * col_count + 2 * (positions // per_device) + parity
    ) * per_device + positions % per_device
    coefficient = coefficients(
        image_rows,
        valid_rows,
        row_ids,
        texts,
        text_weights,
        text_ids,
        factor,
        logit_scale,
        logit_bias,
    )
    partial_image = jnp.dot(coefficient, texts, preferred_element_type=jnp.float32)
    for bit in range(bit_count - 1, 0, -1):
        half = partial_image.shape[0] // 2
        upper = col_index >> bit & 1 == 1
        send = jnp.where(upper, partial_image[:half], partial_image[half:])
        keep = jnp.where(upper, partial_image[half:], partial_image[:half])
        partial_image = keep + partner(send, "col", bit)
    partial_text = text_part(coefficient, image_rows)
    odd = parity == 1
    send_text = jnp.where(odd, partial_text[:text_count], partial_text[text_count:])
    keep_text = jnp.where(odd, partial_text[text_count:], partial_text[:text_count])
    text_partial = keep_text + partner(send_text, "col", 0)
    text_grad = lax.psum_scatter(text_partial, "row", scatter_dimension=1, tiled=True)
    return (partial_image.astype(jnp.bfloat16), text_grad.astype(jnp.bfloat16))


def solution(mesh):
    in_specs = (
        P(("row", "col"), None),
        P("col", "row"),
        P(("row", "col")),
        P("col"),
        P(),
        P(),
        P(),
        P(),
    )
    out_specs = (P(("row", "col"), None), P("col", "row"))
    paired = mesh.shape["row"] == 2 and mesh.shape["col"] == 16
    run = pair_body if paired else body
    return jax.shard_map(run, mesh=mesh, in_specs=in_specs, out_specs=out_specs, check_vma=False)
```

```python
import functools

import jax
import jax.numpy as jnp
from jax import lax
from jax.experimental import pallas as pl
from jax.experimental.pallas import tpu as pltpu
from jax.sharding import PartitionSpec as P

SPARE = 8
LINE = 256


def hop(block, image_bit, text_bit, across=False):
    count = lax.axis_size("col")
    turn = count if across else 0
    route = [(c, turn + (c ^ image_bit)) for c in range(count)]
    route += [(count + c, count - turn + (c ^ text_bit)) for c in range(count)]
    return lax.ppermute(block, ("row", "col"), route)


def swap(block):
    return lax.ppermute(block, "row", [(0, 1), (1, 0)])


def masks(count, row):
    top = count // 2
    near, far = (1, 2), (top, top // 2)
    if row is None:
        return near, far
    return tuple(jnp.where(row == 0, *pair) for pair in (near, far, near[::-1], far[::-1]))


def put_line(ref, *pieces):
    pieces = [piece.astype(jnp.float32) for piece in pieces]
    pieces += [jnp.zeros((1, LINE - sum(piece.shape[1] for piece in pieces)), jnp.float32)]
    line = jnp.broadcast_to(jnp.concatenate(pieces, axis=1), (SPARE, LINE))
    ref[ref.shape[0] - SPARE :, :LINE] = line.astype(ref.dtype)


def put_texts(ref, text_ref):
    half, part = text_ref.shape[0] // 2, text_ref.shape[1]
    ref[:half, :part] = text_ref[:half]
    ref[:half, part:] = text_ref[half:]


def first_kernel(spot_ref, image_ref, text_ref, image_valid_ref, text_valid_ref, mine_ref, give_ref, texts, image_line,
                 text_line, sems):
    half = image_ref.shape[0]

    def fill(image_to, text_to):
        copies = [
            pltpu.make_async_copy(source, target, sems.at[n])
            for n, (source, target) in enumerate((
                (text_ref, texts), (image_ref, image_to.at[pl.ds(0, half)]), (image_valid_ref, image_line),
                (text_valid_ref, text_line)))
        ]
        for copy in copies:
            copy.start()
        copies[0].wait()
        put_texts(text_to, texts)
        for copy in copies[1:]:
            copy.wait()
        put_line(image_to, image_line[...])
        put_line(text_to, text_line[...])

    @pl.when(spot_ref[0] == 0)
    def _():
        fill(mine_ref, give_ref)

    @pl.when(spot_ref[0] != 0)
    def _():
        fill(give_ref, mine_ref)


def unpack(pair, texts, out_ref, start):
    one, two = pair
    half, part = one.shape[0] - SPARE, one.shape[1] // 2

    @pl.when(texts)
    def _():
        out_ref[start : start + half, :part] = two[:half, :part]
        out_ref[start : start + half, part:] = one[:half, :part]
        out_ref[start + half : start + 2 * half, :part] = two[:half, part:]
        out_ref[start + half : start + 2 * half, part:] = one[:half, part:]

    @pl.when(jnp.logical_not(texts))
    def _():
        out_ref[start : start + half] = one[:half]
        out_ref[start + half : start + 2 * half] = two[:half]


def counts(pair, texts):
    one, two = pair
    half = one.shape[0] - SPARE
    line_one = one[half:, :LINE].astype(jnp.float32)[:1]
    line_two = two[half:, :LINE].astype(jnp.float32)[:1]
    images = jnp.concatenate([line_one[:, :half], line_two[:, :half]], axis=1)
    return jnp.where(texts, line_one[:, : 2 * half], images)


def upright(line):
    size = line.shape[1]
    at = lax.broadcasted_iota(jnp.int32, (size, size), 0)
    to = lax.broadcasted_iota(jnp.int32, (size, size), 1)
    return jnp.sum(jnp.where(at == to, line, 0.0), axis=1, keepdims=True)


def sample_ids(col, texts, half, cols, axis):
    shape = (2 * half, 1) if axis == 0 else (1, 2 * half)
    at = lax.broadcasted_iota(jnp.int32, shape, axis)
    jump = jnp.where(texts, 0, (cols - 1) * half)
    first = col * jnp.where(texts, 2 * half, half)
    return at + first + jnp.where(at >= half, jump, 0)


def coefficients_of(cols, row_ref, col_ref, number_ref, mine, others, my_sets, other_sets):
    row, col = row_ref[0], col_ref[0]
    my_texts, other_texts = row != 0, row == 0
    near, far, other_near, other_far = masks(cols, row)
    my_masks = {"own": 0, "near": near, "far": far, "both": near ^ far}
    other_masks = {"own": 0, "near": other_near, "far": other_far, "both": other_near ^ other_far}
    half = my_sets[0][1][0].shape[0] - SPARE
    scale, bias, factor = (number_ref[n : n + 1, :1] for n in range(3))
    my_ids = jnp.concatenate([sample_ids(col ^ my_masks[k], my_texts, half, cols, 0) for k, _ in my_sets], axis=0)
    other_ids = jnp.concatenate(
        [sample_ids(col ^ other_masks[k], other_texts, half, cols, 1) for k, _ in other_sets], axis=1)
    my_weights = jnp.concatenate([upright(counts(pair, my_texts)) for _, pair in my_sets], axis=0)
    other_weights = factor * jnp.concatenate([counts(pair, other_texts) for _, pair in other_sets], axis=1)
    logits = lax.dot_general(mine, others, (((1,), (1,)), ((), ())), preferred_element_type=jnp.float32)
    logits = logits * scale + bias
    match = my_ids == other_ids
    rate = 1.0 / (1.0 + jnp.exp(jnp.where(match, logits, -logits)))
    return (jnp.where(match, -rate, rate) * my_weights * other_weights).astype(jnp.bfloat16)


def pairs(refs):
    return [refs[n : n + 2] for n in range(0, len(refs), 2)]


def number_kernel(scale_ref, bias_ref, grad_ref, sample_ref, out_ref):
    factor = grad_ref[0] * scale_ref[0] / sample_ref[0].astype(jnp.float32)
    line = lax.broadcasted_iota(jnp.int32, out_ref.shape, 0)
    out_ref[...] = jnp.where(line == 0, scale_ref[0], jnp.where(line == 1, bias_ref[0], factor))


def early_kernel(cols, row_ref, col_ref, number_ref, *refs):
    near, far, other_far = pairs(refs[:6])
    mine_ref, far_ref, total_ref = refs[6:]
    texts = row_ref[0] != 0
    size = far_ref.shape[0]
    unpack(near, texts, mine_ref, 0)
    unpack(far, texts, mine_ref, size)
    unpack(other_far, jnp.logical_not(texts), far_ref, 0)
    others = far_ref[...]
    coefficient = coefficients_of(cols, row_ref, col_ref, number_ref, mine_ref[...], others,
                                  [("near", near), ("far", far)], [("far", other_far)])
    total_ref[...] = jnp.dot(coefficient, others, preferred_element_type=jnp.float32)


def both_kernel(cols, row_ref, col_ref, number_ref, *refs):
    both, own, near, far = pairs(refs[:8])
    far_ref, others_ref, mine_ref, total_ref = refs[8:]
    texts = row_ref[0] != 0
    size = far_ref.shape[0]
    unpack(both, texts, mine_ref, 0)
    unpack(own, jnp.logical_not(texts), others_ref, 0)
    unpack(near, jnp.logical_not(texts), others_ref, size)
    others = jnp.concatenate([others_ref[...], far_ref[...]], axis=0)
    coefficient = coefficients_of(cols, row_ref, col_ref, number_ref, mine_ref[...], others, [("both", both)],
                                  [("own", own), ("near", near), ("far", far)])
    total_ref[...] = jnp.dot(coefficient, others, preferred_element_type=jnp.float32)


def pack_sum(total, texts, stay_ref, cross_ref):
    half, part = total.shape[0] // 2, total.shape[1] // 2

    @pl.when(texts)
    def _():
        stay_ref[:, :part] = total[:half, part:].astype(stay_ref.dtype)
        stay_ref[:, part:] = total[half:, part:].astype(stay_ref.dtype)
        cross_ref[:, :part] = total[:half, :part].astype(cross_ref.dtype)
        cross_ref[:, part:] = total[half:, :part].astype(cross_ref.dtype)

    @pl.when(jnp.logical_not(texts))
    def _():
        stay_ref[...] = total[:half].astype(stay_ref.dtype)
        cross_ref[...] = total[half:].astype(cross_ref.dtype)


def late_kernel(cols, row_ref, col_ref, number_ref, *refs):
    mine_pair, other_pair = refs[:2], refs[2:4]
    mine_ref, total_ref = refs[4:6]
    others_ref, stay_ref, cross_ref = refs[6:]
    texts = row_ref[0] != 0
    unpack(other_pair, jnp.logical_not(texts), others_ref, 0)
    others = others_ref[...]
    coefficient = coefficients_of(cols, row_ref, col_ref, number_ref, mine_ref[...], others,
                                  [("both", mine_pair)], [("both", other_pair)])
    total = total_ref[...] + jnp.dot(coefficient, others, preferred_element_type=jnp.float32)
    pack_sum(total, texts, stay_ref, cross_ref)


def far_kernel(cols, row_ref, col_ref, number_ref, *refs):
    far, own, near, both = pairs(refs[:8])
    mine_ref, early_ref, late_ref, total_ref, stay_ref, cross_ref = refs[8:]
    size = late_ref.shape[0]
    others = jnp.concatenate([early_ref[...], late_ref[...]], axis=0)
    coefficient = coefficients_of(cols, row_ref, col_ref, number_ref, mine_ref[size:], others, [("far", far)],
                                  [("own", own), ("near", near), ("both", both)])
    total = total_ref[size:] + jnp.dot(coefficient, others, preferred_element_type=jnp.float32)
    pack_sum(total, row_ref[0] != 0, stay_ref, cross_ref)


def rest_kernel(cols, row_ref, col_ref, number_ref, *refs):
    mine_near, mine_own, own, near, far, both = pairs(refs[:12])
    mine_ref, early_ref, far_ref, late_ref, total_ref = refs[12:17]
    own_stay, own_cross, near_stay, near_cross, own_rows = refs[17:]
    texts = row_ref[0] != 0
    size = late_ref.shape[0]
    unpack(mine_own, texts, own_rows, 0)
    others = jnp.concatenate([early_ref[...], late_ref[...]], axis=0)
    coefficient = coefficients_of(cols, row_ref, col_ref, number_ref, mine_ref[:size], others, [("near", mine_near)],
                                  [("own", own), ("near", near), ("both", both)])
    total = total_ref[:size] + jnp.dot(coefficient, others, preferred_element_type=jnp.float32)
    pack_sum(total, texts, near_stay, near_cross)
    others = jnp.concatenate([others, far_ref[...]], axis=0)
    coefficient = coefficients_of(cols, row_ref, col_ref, number_ref, own_rows[...], others, [("own", mine_own)],
                                  [("own", own), ("near", near), ("both", both), ("far", far)])
    pack_sum(jnp.dot(coefficient, others, preferred_element_type=jnp.float32), texts, own_stay, own_cross)


def last_kernel(spot_ref, stay_ref, crossed_ref, near_stay_ref, near_cross_ref, image_ref, text_ref):
    half, part = text_ref.shape[0] // 2, text_ref.shape[1]

    stay = (stay_ref[...] + near_stay_ref[...].astype(jnp.float32)).astype(image_ref.dtype)
    crossed = (crossed_ref[...] + near_cross_ref[...].astype(jnp.float32)).astype(image_ref.dtype)

    def put(images, texts):
        image_ref[...] = images
        text_ref[:half] = texts[:, :part]
        text_ref[half:] = texts[:, part:]

    @pl.when(spot_ref[0] == 0)
    def _():
        put(stay, crossed)

    @pl.when(spot_ref[0] != 0)
    def _():
        put(crossed, stay)


def call(kernel, out_shape, smem, *arrays, flops=0, scratch=()):
    size = sum(a.size * a.dtype.itemsize for a in (*arrays, *jax.tree.leaves(out_shape)))
    return pl.pallas_call(
        kernel,
        out_shape=out_shape,
        in_specs=[pl.BlockSpec(memory_space=pltpu.SMEM)] * smem
        + [pl.BlockSpec(memory_space=pltpu.VMEM)] * (len(arrays) - smem),
        out_specs=jax.tree.map(lambda _: pl.BlockSpec(memory_space=pltpu.VMEM), out_shape),
        scratch_shapes=scratch,
        compiler_params=pltpu.CompilerParams(vmem_limit_bytes=24 * 1024 * 1024),
        cost_estimate=pl.CostEstimate(flops=flops, bytes_accessed=size, transcendentals=0),
    )(*arrays)


def pair_body(
    image_emb, text_emb, image_valid, text_valid, sample_count, logit_scale, logit_bias, loss_grad
):
    half, width = image_emb.shape
    size = 2 * half
    cols = lax.axis_size("col")
    row, col = lax.axis_index("row")[None], lax.axis_index("col")[None]
    near, far = masks(cols, None)

    def shape(rows, dtype):
        return jax.ShapeDtypeStruct((rows, width), dtype)

    bf16, f32 = jnp.bfloat16, jnp.float32
    sent = shape(half + SPARE, bf16)
    first = (image_emb, text_emb, image_valid[None], text_valid[None])
    own_a, give = pl.pallas_call(
        first_kernel,
        out_shape=(sent, sent),
        in_specs=[pl.BlockSpec(memory_space=pltpu.SMEM)] + [pl.BlockSpec(memory_space=pltpu.HBM)] * 4,
        out_specs=(pl.BlockSpec(memory_space=pltpu.VMEM),) * 2,
        scratch_shapes=[pltpu.VMEM(a.shape, a.dtype) for a in first[1:]] + [pltpu.SemaphoreType.DMA((4,))],
        compiler_params=pltpu.CompilerParams(vmem_limit_bytes=60 * 1024 * 1024),
    )(row, *first)
    far_a = hop(own_a, *far)
    own_b = swap(give)
    far_b = hop(own_b, *far)
    near_a = hop(own_a, *near)
    near_b = hop(own_b, *near)
    both_a = hop(far_a, *near)
    both_b = hop(far_b, *near)
    number = call(number_kernel, jax.ShapeDtypeStruct((8, 128), f32), 4, logit_scale, logit_bias, loss_grad, sample_count)
    far_a, number = lax.optimization_barrier((far_a, number))
    mine_own, mine_near, mine_far = (own_a, own_b), (near_a, near_b), (far_a, far_b)
    own, near_pair, far_pair = (swap(own_a), give), (swap(near_a), swap(near_b)), (swap(far_a), swap(far_b))
    other_both_a = swap(both_a)

    pair_flops = 4 * size * size * width
    scalars = (row, col, number)
    mine_rows, far_rows, early = call(
        functools.partial(early_kernel, cols), (shape(2 * size, bf16), shape(size, bf16), shape(2 * size, f32)), 2,
        *scalars, *mine_near, *mine_far, *far_pair, flops=2 * pair_flops)
    both_b, early = lax.optimization_barrier((both_b, early))
    both = (both_a, both_b)
    other_both = (other_both_a, swap(both_b))
    early_rows, both_rows, both_early = call(
        functools.partial(both_kernel, cols), (shape(2 * size, bf16), shape(size, bf16), shape(size, f32)), 2, *scalars,
        *both, *own, *near_pair, *far_pair, far_rows, flops=3 * pair_flops)
    late_rows, late_stay, late_cross = call(
        functools.partial(late_kernel, cols), (shape(size, bf16), shape(half, bf16), shape(half, bf16)), 2, *scalars,
        *both, *other_both, both_rows, both_early, flops=pair_flops)
    in_cross = hop(late_cross, *near)
    in_stay = hop(late_stay, *near)
    far_stay, far_cross = call(
        functools.partial(far_kernel, cols), (shape(half, f32), shape(half, f32)), 2, *scalars, *mine_far, *own,
        *near_pair, *other_both, mine_rows, early_rows, late_rows, early, flops=3 * pair_flops)
    own_stay, own_cross, near_stay, near_cross = call(
        functools.partial(rest_kernel, cols),
        (shape(half, f32), shape(half, f32), shape(half, bf16), shape(half, bf16)), 2, *scalars, *mine_near, *mine_own,
        *own, *near_pair, *far_pair, *other_both, mine_rows, early_rows, far_rows, late_rows, early,
        flops=7 * pair_flops, scratch=[pltpu.VMEM((size, width), bf16)])
    crossed = swap(own_cross)
    far_cross = (far_cross + in_cross.astype(f32)).astype(bf16)
    far_stay = (far_stay + in_stay.astype(f32)).astype(bf16)
    near_stay, _ = lax.optimization_barrier((near_stay, far_stay))
    near_stay = hop(near_stay, *near)
    near_cross, _, _ = lax.optimization_barrier((near_cross, far_cross, far_stay))
    far_cross = hop(far_cross, *far, across=True)
    far_stay = hop(far_stay, *far)
    near_cross = hop(near_cross, *near, across=True)
    own_stay = own_stay + far_stay.astype(f32)
    crossed = crossed + far_cross.astype(f32)
    return call(last_kernel, (shape(half, bf16), jax.ShapeDtypeStruct(text_emb.shape, bf16)), 1, row, own_stay, crossed,
                near_stay, near_cross)


def partner(block, axis, distance):
    count = lax.axis_size(axis)
    route = []
    for low in range(count):
        high = low | 1 << distance
        if high != low and high < count:
            route += [(low, high), (high, low)]
    return lax.ppermute(block, axis, route)


def coefficients(
    image_rows, valid_rows, row_ids, texts, weight_text, text_ids, factor, logit_scale, logit_bias
):
    logits = lax.dot_general(
        image_rows, texts, (((1,), (1,)), ((), ())), preferred_element_type=jnp.float32
    )
    logits = logits * logit_scale[0] + logit_bias[0]
    label_sign = jnp.where(row_ids[:, None] == text_ids[None, :], 1.0, -1.0).astype(jnp.float32)
    weights = valid_rows.astype(jnp.float32)[:, None] * weight_text[None, :]
    return (-factor * label_sign * jax.nn.sigmoid(-label_sign * logits) * weights).astype(
        jnp.bfloat16
    )


def text_part(coefficient, image_rows):
    return lax.dot_general(
        coefficient, image_rows, (((0,), (0,)), ((), ())), preferred_element_type=jnp.float32
    )


def body(
    image_emb, text_emb, image_valid, text_valid, sample_count, logit_scale, logit_bias, loss_grad
):
    text_block = lax.all_gather(text_emb, "row", axis=1, tiled=True)
    per_device = image_emb.shape[0]
    col_count = lax.axis_size("col")
    col_index = lax.axis_index("col")
    row_index = lax.axis_index("row")
    text_count = text_block.shape[0]
    factor = loss_grad[0] * logit_scale[0] / sample_count[0].astype(jnp.float32)
    valid_wire = image_valid.astype(jnp.bfloat16)
    parity = col_index % 2
    bit_count = col_count.bit_length() - 1
    text_wire = text_valid.astype(jnp.bfloat16)
    other_texts, other_valid = partner((text_block, text_wire), "col", 0)
    own_first = parity == 0
    texts = jnp.where(
        own_first,
        jnp.concatenate([text_block, other_texts], 0),
        jnp.concatenate([other_texts, text_block], 0),
    )
    text_weights = jnp.where(
        own_first,
        jnp.concatenate([text_wire, other_valid], 0),
        jnp.concatenate([other_valid, text_wire], 0),
    ).astype(jnp.float32)
    text_ids = (col_index - parity) * text_count + jnp.arange(2 * text_count, dtype=jnp.int32)
    image_rows, valid_rows = (image_emb, valid_wire)
    for bit in range(1, bit_count):
        other_rows, other_counts = partner((image_rows, valid_rows), "col", bit)
        lower = col_index >> bit & 1 == 0
        image_rows = jnp.where(
            lower,
            jnp.concatenate([image_rows, other_rows], 0),
            jnp.concatenate([other_rows, image_rows], 0),
        )
        valid_rows = jnp.where(
            lower,
            jnp.concatenate([valid_rows, other_counts], 0),
            jnp.concatenate([other_counts, valid_rows], 0),
        )
    positions = jnp.arange(image_rows.shape[0], dtype=jnp.int32)
    row_ids = (
        row_index * col_count + 2 * (positions // per_device) + parity
    ) * per_device + positions % per_device
    coefficient = coefficients(
        image_rows,
        valid_rows,
        row_ids,
        texts,
        text_weights,
        text_ids,
        factor,
        logit_scale,
        logit_bias,
    )
    partial_image = jnp.dot(coefficient, texts, preferred_element_type=jnp.float32)
    for bit in range(bit_count - 1, 0, -1):
        half = partial_image.shape[0] // 2
        upper = col_index >> bit & 1 == 1
        send = jnp.where(upper, partial_image[:half], partial_image[half:])
        keep = jnp.where(upper, partial_image[half:], partial_image[:half])
        partial_image = keep + partner(send, "col", bit)
    partial_text = text_part(coefficient, image_rows)
    odd = parity == 1
    send_text = jnp.where(odd, partial_text[:text_count], partial_text[text_count:])
    keep_text = jnp.where(odd, partial_text[text_count:], partial_text[:text_count])
    text_partial = keep_text + partner(send_text, "col", 0)
    text_grad = lax.psum_scatter(text_partial, "row", scatter_dimension=1, tiled=True)
    return (partial_image.astype(jnp.bfloat16), text_grad.astype(jnp.bfloat16))


def solution(mesh):
    in_specs = (
        P(("row", "col"), None),
        P("col", "row"),
        P(("row", "col")),
        P("col"),
        P(),
        P(),
        P(),
        P(),
    )
    out_specs = (P(("row", "col"), None), P("col", "row"))
    paired = mesh.shape["row"] == 2 and mesh.shape["col"] == 16
    run = pair_body if paired else body
    return jax.shard_map(run, mesh=mesh, in_specs=in_specs, out_specs=out_specs, check_vma=False)
```

```python
import functools

import jax
import jax.numpy as jnp
from jax import lax
from jax.experimental import pallas as pl
from jax.experimental.pallas import tpu as pltpu
from jax.sharding import PartitionSpec as P

SPARE = 8
LINE = 256


def hop(block, image_bit, text_bit, across=False):
    count = lax.axis_size("col")
    turn = count if across else 0
    route = [(c, turn + (c ^ image_bit)) for c in range(count)]
    route += [(count + c, count - turn + (c ^ text_bit)) for c in range(count)]
    return lax.ppermute(block, ("row", "col"), route)


def swap(block):
    return lax.ppermute(block, "row", [(0, 1), (1, 0)])


def masks(count, row):
    top = count // 2
    near, far = (1, 2), (top, top // 2)
    if row is None:
        return near, far
    return tuple(jnp.where(row == 0, *pair) for pair in (near, far, near[::-1], far[::-1]))


def put_line(ref, *pieces):
    pieces = [piece.astype(jnp.float32) for piece in pieces]
    pieces += [jnp.zeros((1, LINE - sum(piece.shape[1] for piece in pieces)), jnp.float32)]
    line = jnp.broadcast_to(jnp.concatenate(pieces, axis=1), (SPARE, LINE))
    ref[ref.shape[0] - SPARE :, :LINE] = line.astype(ref.dtype)


def put_texts(ref, text_ref):
    half, part = text_ref.shape[0] // 2, text_ref.shape[1]
    ref[:half, :part] = text_ref[:half]
    ref[:half, part:] = text_ref[half:]


def first_kernel(spot_ref, image_ref, text_ref, image_valid_ref, text_valid_ref, mine_ref, give_ref, texts, image_line,
                 text_line, sems):
    half = image_ref.shape[0]

    def fill(image_to, text_to):
        copies = [
            pltpu.make_async_copy(source, target, sems.at[n])
            for n, (source, target) in enumerate((
                (text_ref, texts), (image_ref, image_to.at[pl.ds(0, half)]), (image_valid_ref, image_line),
                (text_valid_ref, text_line)))
        ]
        for copy in copies:
            copy.start()
        copies[0].wait()
        put_texts(text_to, texts)
        for copy in copies[1:]:
            copy.wait()
        put_line(image_to, image_line[...])
        put_line(text_to, text_line[...])

    @pl.when(spot_ref[0] == 0)
    def _():
        fill(mine_ref, give_ref)

    @pl.when(spot_ref[0] != 0)
    def _():
        fill(give_ref, mine_ref)


def unpack(pair, texts, out_ref, start):
    one, two = pair
    half, part = one.shape[0] - SPARE, one.shape[1] // 2

    @pl.when(texts)
    def _():
        out_ref[start : start + half, :part] = two[:half, :part]
        out_ref[start : start + half, part:] = one[:half, :part]
        out_ref[start + half : start + 2 * half, :part] = two[:half, part:]
        out_ref[start + half : start + 2 * half, part:] = one[:half, part:]

    @pl.when(jnp.logical_not(texts))
    def _():
        out_ref[start : start + half] = one[:half]
        out_ref[start + half : start + 2 * half] = two[:half]


def counts(pair, texts):
    one, two = pair
    half = one.shape[0] - SPARE
    line_one = one[half:, :LINE].astype(jnp.float32)[:1]
    line_two = two[half:, :LINE].astype(jnp.float32)[:1]
    images = jnp.concatenate([line_one[:, :half], line_two[:, :half]], axis=1)
    return jnp.where(texts, line_one[:, : 2 * half], images)


def upright(line):
    size = line.shape[1]
    at = lax.broadcasted_iota(jnp.int32, (size, size), 0)
    to = lax.broadcasted_iota(jnp.int32, (size, size), 1)
    return jnp.sum(jnp.where(at == to, line, 0.0), axis=1, keepdims=True)


def sample_ids(col, texts, half, cols, axis):
    shape = (2 * half, 1) if axis == 0 else (1, 2 * half)
    at = lax.broadcasted_iota(jnp.int32, shape, axis)
    jump = jnp.where(texts, 0, (cols - 1) * half)
    first = col * jnp.where(texts, 2 * half, half)
    return at + first + jnp.where(at >= half, jump, 0)


def coefficients_of(cols, row_ref, col_ref, number_ref, mine, others, my_sets, other_sets):
    row, col = row_ref[0], col_ref[0]
    my_texts, other_texts = row != 0, row == 0
    near, far, other_near, other_far = masks(cols, row)
    my_masks = {"own": 0, "near": near, "far": far, "both": near ^ far}
    other_masks = {"own": 0, "near": other_near, "far": other_far, "both": other_near ^ other_far}
    half = my_sets[0][1][0].shape[0] - SPARE
    scale, bias, factor = (number_ref[n : n + 1, :1] for n in range(3))
    my_ids = jnp.concatenate([sample_ids(col ^ my_masks[k], my_texts, half, cols, 0) for k, _ in my_sets], axis=0)
    other_ids = jnp.concatenate(
        [sample_ids(col ^ other_masks[k], other_texts, half, cols, 1) for k, _ in other_sets], axis=1)
    my_weights = jnp.concatenate([upright(counts(pair, my_texts)) for _, pair in my_sets], axis=0)
    other_weights = factor * jnp.concatenate([counts(pair, other_texts) for _, pair in other_sets], axis=1)
    logits = lax.dot_general(mine, others, (((1,), (1,)), ((), ())), preferred_element_type=jnp.float32)
    logits = logits * scale + bias
    match = my_ids == other_ids
    rate = 1.0 / (1.0 + jnp.exp(jnp.where(match, logits, -logits)))
    return (jnp.where(match, -rate, rate) * my_weights * other_weights).astype(jnp.bfloat16)


def pairs(refs):
    return [refs[n : n + 2] for n in range(0, len(refs), 2)]


def number_kernel(scale_ref, bias_ref, grad_ref, sample_ref, out_ref):
    factor = grad_ref[0] * scale_ref[0] / sample_ref[0].astype(jnp.float32)
    line = lax.broadcasted_iota(jnp.int32, out_ref.shape, 0)
    out_ref[...] = jnp.where(line == 0, scale_ref[0], jnp.where(line == 1, bias_ref[0], factor))


def early_kernel(cols, row_ref, col_ref, number_ref, *refs):
    near, far, other_far = pairs(refs[:6])
    mine_ref, far_ref, total_ref = refs[6:]
    texts = row_ref[0] != 0
    size = far_ref.shape[0]
    unpack(near, texts, mine_ref, 0)
    unpack(far, texts, mine_ref, size)
    unpack(other_far, jnp.logical_not(texts), far_ref, 0)
    others = far_ref[...]
    coefficient = coefficients_of(cols, row_ref, col_ref, number_ref, mine_ref[...], others,
                                  [("near", near), ("far", far)], [("far", other_far)])
    total_ref[...] = jnp.dot(coefficient, others, preferred_element_type=jnp.float32)


def both_kernel(cols, row_ref, col_ref, number_ref, *refs):
    both, own, near, far = pairs(refs[:8])
    far_ref, others_ref, mine_ref, total_ref = refs[8:]
    texts = row_ref[0] != 0
    size = far_ref.shape[0]
    unpack(both, texts, mine_ref, 0)
    unpack(own, jnp.logical_not(texts), others_ref, 0)
    unpack(near, jnp.logical_not(texts), others_ref, size)
    others = jnp.concatenate([others_ref[...], far_ref[...]], axis=0)
    coefficient = coefficients_of(cols, row_ref, col_ref, number_ref, mine_ref[...], others, [("both", both)],
                                  [("own", own), ("near", near), ("far", far)])
    total_ref[...] = jnp.dot(coefficient, others, preferred_element_type=jnp.float32)


def pack_sum(total, texts, stay_ref, cross_ref):
    half, part = total.shape[0] // 2, total.shape[1] // 2

    @pl.when(texts)
    def _():
        stay_ref[:, :part] = total[:half, part:].astype(stay_ref.dtype)
        stay_ref[:, part:] = total[half:, part:].astype(stay_ref.dtype)
        cross_ref[:, :part] = total[:half, :part].astype(cross_ref.dtype)
        cross_ref[:, part:] = total[half:, :part].astype(cross_ref.dtype)

    @pl.when(jnp.logical_not(texts))
    def _():
        stay_ref[...] = total[:half].astype(stay_ref.dtype)
        cross_ref[...] = total[half:].astype(cross_ref.dtype)


def late_kernel(cols, row_ref, col_ref, number_ref, *refs):
    mine_pair, other_pair = refs[:2], refs[2:4]
    mine_ref, total_ref = refs[4:6]
    others_ref, stay_ref, cross_ref = refs[6:]
    texts = row_ref[0] != 0
    unpack(other_pair, jnp.logical_not(texts), others_ref, 0)
    others = others_ref[...]
    coefficient = coefficients_of(cols, row_ref, col_ref, number_ref, mine_ref[...], others,
                                  [("both", mine_pair)], [("both", other_pair)])
    total = total_ref[...] + jnp.dot(coefficient, others, preferred_element_type=jnp.float32)
    pack_sum(total, texts, stay_ref, cross_ref)


def far_kernel(cols, row_ref, col_ref, number_ref, *refs):
    far, own, near, both = pairs(refs[:8])
    mine_ref, early_ref, late_ref, total_ref, stay_ref, cross_ref = refs[8:]
    size = late_ref.shape[0]
    others = jnp.concatenate([early_ref[...], late_ref[...]], axis=0)
    coefficient = coefficients_of(cols, row_ref, col_ref, number_ref, mine_ref[size:], others, [("far", far)],
                                  [("own", own), ("near", near), ("both", both)])
    total = total_ref[size:] + jnp.dot(coefficient, others, preferred_element_type=jnp.float32)
    pack_sum(total, row_ref[0] != 0, stay_ref, cross_ref)


def rest_kernel(cols, row_ref, col_ref, number_ref, *refs):
    mine_near, mine_own, own, near, far, both = pairs(refs[:12])
    mine_ref, early_ref, far_ref, late_ref, total_ref = refs[12:17]
    own_stay, own_cross, near_stay, near_cross, own_rows = refs[17:]
    texts = row_ref[0] != 0
    size = late_ref.shape[0]
    unpack(mine_own, texts, own_rows, 0)
    others = jnp.concatenate([early_ref[...], late_ref[...]], axis=0)
    coefficient = coefficients_of(cols, row_ref, col_ref, number_ref, mine_ref[:size], others, [("near", mine_near)],
                                  [("own", own), ("near", near), ("both", both)])
    total = total_ref[:size] + jnp.dot(coefficient, others, preferred_element_type=jnp.float32)
    pack_sum(total, texts, near_stay, near_cross)
    others = jnp.concatenate([others, far_ref[...]], axis=0)
    coefficient = coefficients_of(cols, row_ref, col_ref, number_ref, own_rows[...], others, [("own", mine_own)],
                                  [("own", own), ("near", near), ("both", both), ("far", far)])
    pack_sum(jnp.dot(coefficient, others, preferred_element_type=jnp.float32), texts, own_stay, own_cross)


def last_kernel(spot_ref, stay_ref, crossed_ref, near_stay_ref, near_cross_ref, image_ref, text_ref):
    half, part = text_ref.shape[0] // 2, text_ref.shape[1]

    stay = (stay_ref[...] + near_stay_ref[...].astype(jnp.float32)).astype(image_ref.dtype)
    crossed = (crossed_ref[...] + near_cross_ref[...].astype(jnp.float32)).astype(image_ref.dtype)

    def put(images, texts):
        image_ref[...] = images
        text_ref[:half] = texts[:, :part]
        text_ref[half:] = texts[:, part:]

    @pl.when(spot_ref[0] == 0)
    def _():
        put(stay, crossed)

    @pl.when(spot_ref[0] != 0)
    def _():
        put(crossed, stay)


def call(kernel, out_shape, smem, *arrays, flops=0, scratch=()):
    size = sum(a.size * a.dtype.itemsize for a in (*arrays, *jax.tree.leaves(out_shape)))
    return pl.pallas_call(
        kernel,
        out_shape=out_shape,
        in_specs=[pl.BlockSpec(memory_space=pltpu.SMEM)] * smem
        + [pl.BlockSpec(memory_space=pltpu.VMEM)] * (len(arrays) - smem),
        out_specs=jax.tree.map(lambda _: pl.BlockSpec(memory_space=pltpu.VMEM), out_shape),
        scratch_shapes=scratch,
        compiler_params=pltpu.CompilerParams(vmem_limit_bytes=24 * 1024 * 1024),
        cost_estimate=pl.CostEstimate(flops=flops, bytes_accessed=size, transcendentals=0),
    )(*arrays)


def pair_body(
    image_emb, text_emb, image_valid, text_valid, sample_count, logit_scale, logit_bias, loss_grad
):
    half, width = image_emb.shape
    size = 2 * half
    cols = lax.axis_size("col")
    row, col = lax.axis_index("row")[None], lax.axis_index("col")[None]
    near, far = masks(cols, None)

    def shape(rows, dtype):
        return jax.ShapeDtypeStruct((rows, width), dtype)

    bf16, f32 = jnp.bfloat16, jnp.float32
    sent = shape(half + SPARE, bf16)
    first = (image_emb, text_emb, image_valid[None], text_valid[None])
    own_a, give = pl.pallas_call(
        first_kernel,
        out_shape=(sent, sent),
        in_specs=[pl.BlockSpec(memory_space=pltpu.SMEM)] + [pl.BlockSpec(memory_space=pltpu.HBM)] * 4,
        out_specs=(pl.BlockSpec(memory_space=pltpu.VMEM),) * 2,
        scratch_shapes=[pltpu.VMEM(a.shape, a.dtype) for a in first[1:]] + [pltpu.SemaphoreType.DMA((4,))],
        compiler_params=pltpu.CompilerParams(vmem_limit_bytes=60 * 1024 * 1024),
    )(row, *first)
    far_a = hop(own_a, *far)
    own_b = swap(give)
    far_b = hop(own_b, *far)
    near_a = hop(own_a, *near)
    near_b = hop(own_b, *near)
    both_a = hop(far_a, *near)
    both_b = hop(far_b, *near)
    number = call(number_kernel, jax.ShapeDtypeStruct((8, 128), f32), 4, logit_scale, logit_bias, loss_grad, sample_count)
    far_a, number = lax.optimization_barrier((far_a, number))
    mine_own, mine_near, mine_far = (own_a, own_b), (near_a, near_b), (far_a, far_b)
    own, near_pair, far_pair = (swap(own_a), swap(own_b)), (swap(near_a), swap(near_b)), (swap(far_a), swap(far_b))
    other_both_a = swap(both_a)

    pair_flops = 4 * size * size * width
    scalars = (row, col, number)
    mine_rows, far_rows, early = call(
        functools.partial(early_kernel, cols), (shape(2 * size, bf16), shape(size, bf16), shape(2 * size, f32)), 2,
        *scalars, *mine_near, *mine_far, *far_pair, flops=2 * pair_flops)
    both_b, early = lax.optimization_barrier((both_b, early))
    both = (both_a, both_b)
    other_both = (other_both_a, swap(both_b))
    early_rows, both_rows, both_early = call(
        functools.partial(both_kernel, cols), (shape(2 * size, bf16), shape(size, bf16), shape(size, f32)), 2, *scalars,
        *both, *own, *near_pair, *far_pair, far_rows, flops=3 * pair_flops)
    late_rows, late_stay, late_cross = call(
        functools.partial(late_kernel, cols), (shape(size, bf16), shape(half, bf16), shape(half, bf16)), 2, *scalars,
        *both, *other_both, both_rows, both_early, flops=pair_flops)
    in_cross = hop(late_cross, *near)
    in_stay = hop(late_stay, *near)
    far_stay, far_cross = call(
        functools.partial(far_kernel, cols), (shape(half, f32), shape(half, f32)), 2, *scalars, *mine_far, *own,
        *near_pair, *other_both, mine_rows, early_rows, late_rows, early, flops=3 * pair_flops)
    own_stay, own_cross, near_stay, near_cross = call(
        functools.partial(rest_kernel, cols),
        (shape(half, f32), shape(half, f32), shape(half, bf16), shape(half, bf16)), 2, *scalars, *mine_near, *mine_own,
        *own, *near_pair, *far_pair, *other_both, mine_rows, early_rows, far_rows, late_rows, early,
        flops=7 * pair_flops, scratch=[pltpu.VMEM((size, width), bf16)])
    crossed = swap(own_cross)
    far_cross = (far_cross + in_cross.astype(f32)).astype(bf16)
    far_stay = (far_stay + in_stay.astype(f32)).astype(bf16)
    near_stay, _ = lax.optimization_barrier((near_stay, far_stay))
    near_stay = hop(near_stay, *near)
    near_cross, _, _ = lax.optimization_barrier((near_cross, far_cross, far_stay))
    far_cross = hop(far_cross, *far, across=True)
    far_stay = hop(far_stay, *far)
    near_cross = hop(near_cross, *near, across=True)
    own_stay = own_stay + far_stay.astype(f32)
    crossed = crossed + far_cross.astype(f32)
    return call(last_kernel, (shape(half, bf16), jax.ShapeDtypeStruct(text_emb.shape, bf16)), 1, row, own_stay, crossed,
                near_stay, near_cross)


def partner(block, axis, distance):
    count = lax.axis_size(axis)
    route = []
    for low in range(count):
        high = low | 1 << distance
        if high != low and high < count:
            route += [(low, high), (high, low)]
    return lax.ppermute(block, axis, route)


def coefficients(
    image_rows, valid_rows, row_ids, texts, weight_text, text_ids, factor, logit_scale, logit_bias
):
    logits = lax.dot_general(
        image_rows, texts, (((1,), (1,)), ((), ())), preferred_element_type=jnp.float32
    )
    logits = logits * logit_scale[0] + logit_bias[0]
    label_sign = jnp.where(row_ids[:, None] == text_ids[None, :], 1.0, -1.0).astype(jnp.float32)
    weights = valid_rows.astype(jnp.float32)[:, None] * weight_text[None, :]
    return (-factor * label_sign * jax.nn.sigmoid(-label_sign * logits) * weights).astype(
        jnp.bfloat16
    )


def text_part(coefficient, image_rows):
    return lax.dot_general(
        coefficient, image_rows, (((0,), (0,)), ((), ())), preferred_element_type=jnp.float32
    )


def body(
    image_emb, text_emb, image_valid, text_valid, sample_count, logit_scale, logit_bias, loss_grad
):
    text_block = lax.all_gather(text_emb, "row", axis=1, tiled=True)
    per_device = image_emb.shape[0]
    col_count = lax.axis_size("col")
    col_index = lax.axis_index("col")
    row_index = lax.axis_index("row")
    text_count = text_block.shape[0]
    factor = loss_grad[0] * logit_scale[0] / sample_count[0].astype(jnp.float32)
    valid_wire = image_valid.astype(jnp.bfloat16)
    parity = col_index % 2
    bit_count = col_count.bit_length() - 1
    text_wire = text_valid.astype(jnp.bfloat16)
    other_texts, other_valid = partner((text_block, text_wire), "col", 0)
    own_first = parity == 0
    texts = jnp.where(
        own_first,
        jnp.concatenate([text_block, other_texts], 0),
        jnp.concatenate([other_texts, text_block], 0),
    )
    text_weights = jnp.where(
        own_first,
        jnp.concatenate([text_wire, other_valid], 0),
        jnp.concatenate([other_valid, text_wire], 0),
    ).astype(jnp.float32)
    text_ids = (col_index - parity) * text_count + jnp.arange(2 * text_count, dtype=jnp.int32)
    image_rows, valid_rows = (image_emb, valid_wire)
    for bit in range(1, bit_count):
        other_rows, other_counts = partner((image_rows, valid_rows), "col", bit)
        lower = col_index >> bit & 1 == 0
        image_rows = jnp.where(
            lower,
            jnp.concatenate([image_rows, other_rows], 0),
            jnp.concatenate([other_rows, image_rows], 0),
        )
        valid_rows = jnp.where(
            lower,
            jnp.concatenate([valid_rows, other_counts], 0),
            jnp.concatenate([other_counts, valid_rows], 0),
        )
    positions = jnp.arange(image_rows.shape[0], dtype=jnp.int32)
    row_ids = (
        row_index * col_count + 2 * (positions // per_device) + parity
    ) * per_device + positions % per_device
    coefficient = coefficients(
        image_rows,
        valid_rows,
        row_ids,
        texts,
        text_weights,
        text_ids,
        factor,
        logit_scale,
        logit_bias,
    )
    partial_image = jnp.dot(coefficient, texts, preferred_element_type=jnp.float32)
    for bit in range(bit_count - 1, 0, -1):
        half = partial_image.shape[0] // 2
        upper = col_index >> bit & 1 == 1
        send = jnp.where(upper, partial_image[:half], partial_image[half:])
        keep = jnp.where(upper, partial_image[half:], partial_image[:half])
        partial_image = keep + partner(send, "col", bit)
    partial_text = text_part(coefficient, image_rows)
    odd = parity == 1
    send_text = jnp.where(odd, partial_text[:text_count], partial_text[text_count:])
    keep_text = jnp.where(odd, partial_text[text_count:], partial_text[:text_count])
    text_partial = keep_text + partner(send_text, "col", 0)
    text_grad = lax.psum_scatter(text_partial, "row", scatter_dimension=1, tiled=True)
    return (partial_image.astype(jnp.bfloat16), text_grad.astype(jnp.bfloat16))


def solution(mesh):
    in_specs = (
        P(("row", "col"), None),
        P("col", "row"),
        P(("row", "col")),
        P("col"),
        P(),
        P(),
        P(),
        P(),
    )
    out_specs = (P(("row", "col"), None), P("col", "row"))
    paired = mesh.shape["row"] == 2 and mesh.shape["col"] == 16
    run = pair_body if paired else body
    return jax.shard_map(run, mesh=mesh, in_specs=in_specs, out_specs=out_specs, check_vma=False)
```

```python
import functools

import jax
import jax.numpy as jnp
from jax import lax
from jax.experimental import pallas as pl
from jax.experimental.pallas import tpu as pltpu
from jax.sharding import PartitionSpec as P

SPARE = 8
LINE = 256


def hop(block, image_bit, text_bit, across=False):
    count = lax.axis_size("col")
    turn = count if across else 0
    route = [(c, turn + (c ^ image_bit)) for c in range(count)]
    route += [(count + c, count - turn + (c ^ text_bit)) for c in range(count)]
    return lax.ppermute(block, ("row", "col"), route)


def swap(block):
    return lax.ppermute(block, "row", [(0, 1), (1, 0)])


def masks(count, row):
    top = count // 2
    near, far = (1, 2), (top, top // 2)
    if row is None:
        return near, far
    return tuple(jnp.where(row == 0, *pair) for pair in (near, far, near[::-1], far[::-1]))


def put_line(ref, *pieces):
    pieces = [piece.astype(jnp.float32) for piece in pieces]
    pieces += [jnp.zeros((1, LINE - sum(piece.shape[1] for piece in pieces)), jnp.float32)]
    line = jnp.broadcast_to(jnp.concatenate(pieces, axis=1), (SPARE, LINE))
    ref[ref.shape[0] - SPARE :, :LINE] = line.astype(ref.dtype)


def put_texts(ref, text_ref):
    half, part = text_ref.shape[0] // 2, text_ref.shape[1]
    ref[:half, :part] = text_ref[:half]
    ref[:half, part:] = text_ref[half:]


def first_kernel(spot_ref, image_ref, text_ref, image_valid_ref, text_valid_ref, mine_ref, give_ref, texts, image_line,
                 text_line, sems):
    half = image_ref.shape[0]

    def fill(image_to, text_to):
        copies = [
            pltpu.make_async_copy(source, target, sems.at[n])
            for n, (source, target) in enumerate((
                (text_ref, texts), (image_ref, image_to.at[pl.ds(0, half)]), (image_valid_ref, image_line),
                (text_valid_ref, text_line)))
        ]
        for copy in copies:
            copy.start()
        copies[0].wait()
        put_texts(text_to, texts)
        for copy in copies[1:]:
            copy.wait()
        put_line(image_to, image_line[...])
        put_line(text_to, text_line[...])

    @pl.when(spot_ref[0] == 0)
    def _():
        fill(mine_ref, give_ref)

    @pl.when(spot_ref[0] != 0)
    def _():
        fill(give_ref, mine_ref)


def unpack(pair, texts, out_ref, start):
    one, two = pair
    half, part = one.shape[0] - SPARE, one.shape[1] // 2

    @pl.when(texts)
    def _():
        out_ref[start : start + half, :part] = two[:half, :part]
        out_ref[start : start + half, part:] = one[:half, :part]
        out_ref[start + half : start + 2 * half, :part] = two[:half, part:]
        out_ref[start + half : start + 2 * half, part:] = one[:half, part:]

    @pl.when(jnp.logical_not(texts))
    def _():
        out_ref[start : start + half] = one[:half]
        out_ref[start + half : start + 2 * half] = two[:half]


def counts(pair, texts):
    one, two = pair
    half = one.shape[0] - SPARE
    line_one = one[half:, :LINE].astype(jnp.float32)[:1]
    line_two = two[half:, :LINE].astype(jnp.float32)[:1]
    images = jnp.concatenate([line_one[:, :half], line_two[:, :half]], axis=1)
    return jnp.where(texts, line_one[:, : 2 * half], images)


def upright(line):
    size = line.shape[1]
    at = lax.broadcasted_iota(jnp.int32, (size, size), 0)
    to = lax.broadcasted_iota(jnp.int32, (size, size), 1)
    return jnp.sum(jnp.where(at == to, line, 0.0), axis=1, keepdims=True)


def sample_ids(col, texts, half, cols, axis):
    shape = (2 * half, 1) if axis == 0 else (1, 2 * half)
    at = lax.broadcasted_iota(jnp.int32, shape, axis)
    jump = jnp.where(texts, 0, (cols - 1) * half)
    first = col * jnp.where(texts, 2 * half, half)
    return at + first + jnp.where(at >= half, jump, 0)


def coefficients_of(cols, row_ref, col_ref, number_ref, mine, others, my_sets, other_sets):
    row, col = row_ref[0], col_ref[0]
    my_texts, other_texts = row != 0, row == 0
    near, far, other_near, other_far = masks(cols, row)
    my_masks = {"own": 0, "near": near, "far": far, "both": near ^ far}
    other_masks = {"own": 0, "near": other_near, "far": other_far, "both": other_near ^ other_far}
    half = my_sets[0][1][0].shape[0] - SPARE
    scale, bias, factor = (number_ref[n : n + 1, :1] for n in range(3))
    my_ids = jnp.concatenate([sample_ids(col ^ my_masks[k], my_texts, half, cols, 0) for k, _ in my_sets], axis=0)
    other_ids = jnp.concatenate(
        [sample_ids(col ^ other_masks[k], other_texts, half, cols, 1) for k, _ in other_sets], axis=1)
    my_weights = jnp.concatenate([upright(counts(pair, my_texts)) for _, pair in my_sets], axis=0)
    other_weights = factor * jnp.concatenate([counts(pair, other_texts) for _, pair in other_sets], axis=1)
    logits = lax.dot_general(mine, others, (((1,), (1,)), ((), ())), preferred_element_type=jnp.float32)
    logits = logits * scale + bias
    match = my_ids == other_ids
    rate = 1.0 / (1.0 + jnp.exp(jnp.where(match, logits, -logits)))
    return (jnp.where(match, -rate, rate) * my_weights * other_weights).astype(jnp.bfloat16)


def pairs(refs):
    return [refs[n : n + 2] for n in range(0, len(refs), 2)]


def number_kernel(scale_ref, bias_ref, grad_ref, sample_ref, out_ref):
    factor = grad_ref[0] * scale_ref[0] / sample_ref[0].astype(jnp.float32)
    line = lax.broadcasted_iota(jnp.int32, out_ref.shape, 0)
    out_ref[...] = jnp.where(line == 0, scale_ref[0], jnp.where(line == 1, bias_ref[0], factor))


def early_kernel(cols, row_ref, col_ref, number_ref, *refs):
    near, far, other_far = pairs(refs[:6])
    mine_ref, far_ref, total_ref = refs[6:]
    texts = row_ref[0] != 0
    size = far_ref.shape[0]
    unpack(near, texts, mine_ref, 0)
    unpack(far, texts, mine_ref, size)
    unpack(other_far, jnp.logical_not(texts), far_ref, 0)
    others = far_ref[...]
    coefficient = coefficients_of(cols, row_ref, col_ref, number_ref, mine_ref[...], others,
                                  [("near", near), ("far", far)], [("far", other_far)])
    total_ref[...] = jnp.dot(coefficient, others, preferred_element_type=jnp.float32)


def both_kernel(cols, row_ref, col_ref, number_ref, *refs):
    both, own, near, far = pairs(refs[:8])
    far_ref, others_ref, mine_ref, total_ref = refs[8:]
    texts = row_ref[0] != 0
    size = far_ref.shape[0]
    unpack(both, texts, mine_ref, 0)
    unpack(own, jnp.logical_not(texts), others_ref, 0)
    unpack(near, jnp.logical_not(texts), others_ref, size)
    others = jnp.concatenate([others_ref[...], far_ref[...]], axis=0)
    coefficient = coefficients_of(cols, row_ref, col_ref, number_ref, mine_ref[...], others, [("both", both)],
                                  [("own", own), ("near", near), ("far", far)])
    total_ref[...] = jnp.dot(coefficient, others, preferred_element_type=jnp.float32)


def pack_sum(total, texts, stay_ref, cross_ref):
    half, part = total.shape[0] // 2, total.shape[1] // 2

    @pl.when(texts)
    def _():
        stay_ref[:, :part] = total[:half, part:].astype(stay_ref.dtype)
        stay_ref[:, part:] = total[half:, part:].astype(stay_ref.dtype)
        cross_ref[:, :part] = total[:half, :part].astype(cross_ref.dtype)
        cross_ref[:, part:] = total[half:, :part].astype(cross_ref.dtype)

    @pl.when(jnp.logical_not(texts))
    def _():
        stay_ref[...] = total[:half].astype(stay_ref.dtype)
        cross_ref[...] = total[half:].astype(cross_ref.dtype)


def late_kernel(cols, row_ref, col_ref, number_ref, *refs):
    mine_pair, other_pair = refs[:2], refs[2:4]
    mine_ref, total_ref = refs[4:6]
    others_ref, stay_ref, cross_ref = refs[6:]
    texts = row_ref[0] != 0
    unpack(other_pair, jnp.logical_not(texts), others_ref, 0)
    others = others_ref[...]
    coefficient = coefficients_of(cols, row_ref, col_ref, number_ref, mine_ref[...], others,
                                  [("both", mine_pair)], [("both", other_pair)])
    total = total_ref[...] + jnp.dot(coefficient, others, preferred_element_type=jnp.float32)
    pack_sum(total, texts, stay_ref, cross_ref)


def far_kernel(cols, row_ref, col_ref, number_ref, *refs):
    far, own, near, both = pairs(refs[:8])
    mine_ref, early_ref, late_ref, total_ref, stay_ref, cross_ref = refs[8:]
    size = late_ref.shape[0]
    others = jnp.concatenate([early_ref[...], late_ref[...]], axis=0)
    coefficient = coefficients_of(cols, row_ref, col_ref, number_ref, mine_ref[size:], others, [("far", far)],
                                  [("own", own), ("near", near), ("both", both)])
    total = total_ref[size:] + jnp.dot(coefficient, others, preferred_element_type=jnp.float32)
    pack_sum(total, row_ref[0] != 0, stay_ref, cross_ref)


def rest_kernel(cols, row_ref, col_ref, number_ref, *refs):
    mine_near, mine_own, own, near, far, both = pairs(refs[:12])
    mine_ref, early_ref, far_ref, late_ref, total_ref = refs[12:17]
    own_stay, own_cross, near_stay, near_cross, own_rows = refs[17:]
    texts = row_ref[0] != 0
    size = late_ref.shape[0]
    unpack(mine_own, texts, own_rows, 0)
    others = jnp.concatenate([early_ref[...], late_ref[...]], axis=0)
    coefficient = coefficients_of(cols, row_ref, col_ref, number_ref, mine_ref[:size], others, [("near", mine_near)],
                                  [("own", own), ("near", near), ("both", both)])
    total = total_ref[:size] + jnp.dot(coefficient, others, preferred_element_type=jnp.float32)
    pack_sum(total, texts, near_stay, near_cross)
    others = jnp.concatenate([others, far_ref[...]], axis=0)
    coefficient = coefficients_of(cols, row_ref, col_ref, number_ref, own_rows[...], others, [("own", mine_own)],
                                  [("own", own), ("near", near), ("both", both), ("far", far)])
    pack_sum(jnp.dot(coefficient, others, preferred_element_type=jnp.float32), texts, own_stay, own_cross)


def last_kernel(row_ref, stay_ref, crossed_ref, near_stay_ref, near_cross_ref, image_ref, text_ref, images, texts, sems):
    half, part = text_ref.shape[0] // 2, text_ref.shape[1]

    def put(image_sums, text_sums):
        images[...] = (image_sums[0][...] + image_sums[1][...].astype(jnp.float32)).astype(images.dtype)
        image_out = pltpu.make_async_copy(images, image_ref, sems.at[0])
        image_out.start()
        rows = (text_sums[0][...] + text_sums[1][...].astype(jnp.float32)).astype(texts.dtype)
        texts[:half] = rows[:, :part]
        texts[half:] = rows[:, part:]
        text_out = pltpu.make_async_copy(texts, text_ref, sems.at[1])
        text_out.start()
        image_out.wait()
        text_out.wait()

    @pl.when(row_ref[0] == 0)
    def _():
        put((stay_ref, near_stay_ref), (crossed_ref, near_cross_ref))

    @pl.when(row_ref[0] != 0)
    def _():
        put((crossed_ref, near_cross_ref), (stay_ref, near_stay_ref))


def call(kernel, out_shape, smem, *arrays, flops=0, scratch=()):
    size = sum(a.size * a.dtype.itemsize for a in (*arrays, *jax.tree.leaves(out_shape)))
    return pl.pallas_call(
        kernel,
        out_shape=out_shape,
        in_specs=[pl.BlockSpec(memory_space=pltpu.SMEM)] * smem
        + [pl.BlockSpec(memory_space=pltpu.VMEM)] * (len(arrays) - smem),
        out_specs=jax.tree.map(lambda _: pl.BlockSpec(memory_space=pltpu.VMEM), out_shape),
        scratch_shapes=scratch,
        compiler_params=pltpu.CompilerParams(vmem_limit_bytes=24 * 1024 * 1024),
        cost_estimate=pl.CostEstimate(flops=flops, bytes_accessed=size, transcendentals=0),
    )(*arrays)


def pair_body(
    image_emb, text_emb, image_valid, text_valid, sample_count, logit_scale, logit_bias, loss_grad
):
    half, width = image_emb.shape
    size = 2 * half
    cols = lax.axis_size("col")
    row, col = lax.axis_index("row")[None], lax.axis_index("col")[None]
    near, far = masks(cols, None)

    def shape(rows, dtype):
        return jax.ShapeDtypeStruct((rows, width), dtype)

    bf16, f32 = jnp.bfloat16, jnp.float32
    sent = shape(half + SPARE, bf16)
    first = (image_emb, text_emb, image_valid[None], text_valid[None])
    own_a, give = pl.pallas_call(
        first_kernel,
        out_shape=(sent, sent),
        in_specs=[pl.BlockSpec(memory_space=pltpu.SMEM)] + [pl.BlockSpec(memory_space=pltpu.HBM)] * 4,
        out_specs=(pl.BlockSpec(memory_space=pltpu.VMEM),) * 2,
        scratch_shapes=[pltpu.VMEM(a.shape, a.dtype) for a in first[1:]] + [pltpu.SemaphoreType.DMA((4,))],
        compiler_params=pltpu.CompilerParams(vmem_limit_bytes=60 * 1024 * 1024),
    )(row, *first)
    far_a = hop(own_a, *far)
    own_b = swap(give)
    far_b = hop(own_b, *far)
    near_a = hop(own_a, *near)
    near_b = hop(own_b, *near)
    both_a = hop(far_a, *near)
    both_b = hop(far_b, *near)
    number = call(number_kernel, jax.ShapeDtypeStruct((8, 128), f32), 4, logit_scale, logit_bias, loss_grad, sample_count)
    far_a, number = lax.optimization_barrier((far_a, number))
    mine_own, mine_near, mine_far = (own_a, own_b), (near_a, near_b), (far_a, far_b)
    own, near_pair, far_pair = (swap(own_a), swap(own_b)), (swap(near_a), swap(near_b)), (swap(far_a), swap(far_b))
    other_both_a = swap(both_a)

    pair_flops = 4 * size * size * width
    scalars = (row, col, number)
    mine_rows, far_rows, early = call(
        functools.partial(early_kernel, cols), (shape(2 * size, bf16), shape(size, bf16), shape(2 * size, f32)), 2,
        *scalars, *mine_near, *mine_far, *far_pair, flops=2 * pair_flops)
    both_b, early = lax.optimization_barrier((both_b, early))
    both = (both_a, both_b)
    other_both = (other_both_a, swap(both_b))
    early_rows, both_rows, both_early = call(
        functools.partial(both_kernel, cols), (shape(2 * size, bf16), shape(size, bf16), shape(size, f32)), 2, *scalars,
        *both, *own, *near_pair, *far_pair, far_rows, flops=3 * pair_flops)
    late_rows, late_stay, late_cross = call(
        functools.partial(late_kernel, cols), (shape(size, bf16), shape(half, bf16), shape(half, bf16)), 2, *scalars,
        *both, *other_both, both_rows, both_early, flops=pair_flops)
    in_cross = hop(late_cross, *near)
    in_stay = hop(late_stay, *near)
    far_stay, far_cross = call(
        functools.partial(far_kernel, cols), (shape(half, f32), shape(half, f32)), 2, *scalars, *mine_far, *own,
        *near_pair, *other_both, mine_rows, early_rows, late_rows, early, flops=3 * pair_flops)
    own_stay, own_cross, near_stay, near_cross = call(
        functools.partial(rest_kernel, cols),
        (shape(half, f32), shape(half, f32), shape(half, bf16), shape(half, bf16)), 2, *scalars, *mine_near, *mine_own,
        *own, *near_pair, *far_pair, *other_both, mine_rows, early_rows, far_rows, late_rows, early,
        flops=7 * pair_flops, scratch=[pltpu.VMEM((size, width), bf16)])
    crossed = swap(own_cross)
    far_cross = (far_cross + in_cross.astype(f32)).astype(bf16)
    far_stay = (far_stay + in_stay.astype(f32)).astype(bf16)
    near_stay, _ = lax.optimization_barrier((near_stay, far_stay))
    near_stay = hop(near_stay, *near)
    near_cross, _, _ = lax.optimization_barrier((near_cross, far_cross, far_stay))
    far_cross = hop(far_cross, *far, across=True)
    far_stay = hop(far_stay, *far)
    near_cross = hop(near_cross, *near, across=True)
    own_stay = own_stay + far_stay.astype(f32)
    crossed = crossed + far_cross.astype(f32)
    outs = (shape(half, bf16), jax.ShapeDtypeStruct(text_emb.shape, bf16))
    return pl.pallas_call(
        last_kernel,
        out_shape=outs,
        in_specs=[pl.BlockSpec(memory_space=pltpu.SMEM)] + [pl.BlockSpec(memory_space=pltpu.VMEM)] * 4,
        out_specs=(pl.BlockSpec(memory_space=pltpu.HBM),) * 2,
        scratch_shapes=[pltpu.VMEM(out.shape, out.dtype) for out in outs] + [pltpu.SemaphoreType.DMA((2,))],
        compiler_params=pltpu.CompilerParams(vmem_limit_bytes=24 * 1024 * 1024),
    )(row, own_stay, crossed, near_stay, near_cross)


def partner(block, axis, distance):
    count = lax.axis_size(axis)
    route = []
    for low in range(count):
        high = low | 1 << distance
        if high != low and high < count:
            route += [(low, high), (high, low)]
    return lax.ppermute(block, axis, route)


def coefficients(
    image_rows, valid_rows, row_ids, texts, weight_text, text_ids, factor, logit_scale, logit_bias
):
    logits = lax.dot_general(
        image_rows, texts, (((1,), (1,)), ((), ())), preferred_element_type=jnp.float32
    )
    logits = logits * logit_scale[0] + logit_bias[0]
    label_sign = jnp.where(row_ids[:, None] == text_ids[None, :], 1.0, -1.0).astype(jnp.float32)
    weights = valid_rows.astype(jnp.float32)[:, None] * weight_text[None, :]
    return (-factor * label_sign * jax.nn.sigmoid(-label_sign * logits) * weights).astype(
        jnp.bfloat16
    )


def text_part(coefficient, image_rows):
    return lax.dot_general(
        coefficient, image_rows, (((0,), (0,)), ((), ())), preferred_element_type=jnp.float32
    )


def body(
    image_emb, text_emb, image_valid, text_valid, sample_count, logit_scale, logit_bias, loss_grad
):
    text_block = lax.all_gather(text_emb, "row", axis=1, tiled=True)
    per_device = image_emb.shape[0]
    col_count = lax.axis_size("col")
    col_index = lax.axis_index("col")
    row_index = lax.axis_index("row")
    text_count = text_block.shape[0]
    factor = loss_grad[0] * logit_scale[0] / sample_count[0].astype(jnp.float32)
    valid_wire = image_valid.astype(jnp.bfloat16)
    parity = col_index % 2
    bit_count = col_count.bit_length() - 1
    text_wire = text_valid.astype(jnp.bfloat16)
    other_texts, other_valid = partner((text_block, text_wire), "col", 0)
    own_first = parity == 0
    texts = jnp.where(
        own_first,
        jnp.concatenate([text_block, other_texts], 0),
        jnp.concatenate([other_texts, text_block], 0),
    )
    text_weights = jnp.where(
        own_first,
        jnp.concatenate([text_wire, other_valid], 0),
        jnp.concatenate([other_valid, text_wire], 0),
    ).astype(jnp.float32)
    text_ids = (col_index - parity) * text_count + jnp.arange(2 * text_count, dtype=jnp.int32)
    image_rows, valid_rows = (image_emb, valid_wire)
    for bit in range(1, bit_count):
        other_rows, other_counts = partner((image_rows, valid_rows), "col", bit)
        lower = col_index >> bit & 1 == 0
        image_rows = jnp.where(
            lower,
            jnp.concatenate([image_rows, other_rows], 0),
            jnp.concatenate([other_rows, image_rows], 0),
        )
        valid_rows = jnp.where(
            lower,
            jnp.concatenate([valid_rows, other_counts], 0),
            jnp.concatenate([other_counts, valid_rows], 0),
        )
    positions = jnp.arange(image_rows.shape[0], dtype=jnp.int32)
    row_ids = (
        row_index * col_count + 2 * (positions // per_device) + parity
    ) * per_device + positions % per_device
    coefficient = coefficients(
        image_rows,
        valid_rows,
        row_ids,
        texts,
        text_weights,
        text_ids,
        factor,
        logit_scale,
        logit_bias,
    )
    partial_image = jnp.dot(coefficient, texts, preferred_element_type=jnp.float32)
    for bit in range(bit_count - 1, 0, -1):
        half = partial_image.shape[0] // 2
        upper = col_index >> bit & 1 == 1
        send = jnp.where(upper, partial_image[:half], partial_image[half:])
        keep = jnp.where(upper, partial_image[half:], partial_image[:half])
        partial_image = keep + partner(send, "col", bit)
    partial_text = text_part(coefficient, image_rows)
    odd = parity == 1
    send_text = jnp.where(odd, partial_text[:text_count], partial_text[text_count:])
    keep_text = jnp.where(odd, partial_text[text_count:], partial_text[:text_count])
    text_partial = keep_text + partner(send_text, "col", 0)
    text_grad = lax.psum_scatter(text_partial, "row", scatter_dimension=1, tiled=True)
    return (partial_image.astype(jnp.bfloat16), text_grad.astype(jnp.bfloat16))


def solution(mesh):
    in_specs = (
        P(("row", "col"), None),
        P("col", "row"),
        P(("row", "col")),
        P("col"),
        P(),
        P(),
        P(),
        P(),
    )
    out_specs = (P(("row", "col"), None), P("col", "row"))
    paired = mesh.shape["row"] == 2 and mesh.shape["col"] == 16
    run = pair_body if paired else body
    return jax.shard_map(run, mesh=mesh, in_specs=in_specs, out_specs=out_specs, check_vma=False)
```

```python
import functools

import jax
import jax.numpy as jnp
from jax import lax
from jax.experimental import pallas as pl
from jax.experimental.pallas import tpu as pltpu
from jax.sharding import PartitionSpec as P

SPARE = 8
LINE = 256


def hop(block, image_bit, text_bit, across=False):
    count = lax.axis_size("col")
    turn = count if across else 0
    route = [(c, turn + (c ^ image_bit)) for c in range(count)]
    route += [(count + c, count - turn + (c ^ text_bit)) for c in range(count)]
    return lax.ppermute(block, ("row", "col"), route)


def swap(block):
    return lax.ppermute(block, "row", [(0, 1), (1, 0)])


def masks(count, row):
    top = count // 2
    near, far = (1, 2), (top, top // 2)
    if row is None:
        return near, far
    return tuple(jnp.where(row == 0, *pair) for pair in (near, far, near[::-1], far[::-1]))


def put_line(ref, *pieces):
    pieces = [piece.astype(jnp.float32) for piece in pieces]
    pieces += [jnp.zeros((1, LINE - sum(piece.shape[1] for piece in pieces)), jnp.float32)]
    line = jnp.broadcast_to(jnp.concatenate(pieces, axis=1), (SPARE, LINE))
    ref[ref.shape[0] - SPARE :, :LINE] = line.astype(ref.dtype)


def put_texts(ref, text_ref):
    half, part = text_ref.shape[0] // 2, text_ref.shape[1]
    ref[:half, :part] = text_ref[:half]
    ref[:half, part:] = text_ref[half:]


def first_kernel(spot_ref, image_ref, text_ref, image_valid_ref, text_valid_ref, mine_ref, give_ref, texts, image_line,
                 text_line, sems):
    half = image_ref.shape[0]

    def fill(image_to, text_to):
        copies = [
            pltpu.make_async_copy(source, target, sems.at[n])
            for n, (source, target) in enumerate((
                (text_ref, texts), (image_ref, image_to.at[pl.ds(0, half)]), (image_valid_ref, image_line),
                (text_valid_ref, text_line)))
        ]
        for copy in copies:
            copy.start()
        copies[0].wait()
        put_texts(text_to, texts)
        for copy in copies[1:]:
            copy.wait()
        put_line(image_to, image_line[...])
        put_line(text_to, text_line[...])

    @pl.when(spot_ref[0] == 0)
    def _():
        fill(mine_ref, give_ref)

    @pl.when(spot_ref[0] != 0)
    def _():
        fill(give_ref, mine_ref)


def unpack(pair, texts, out_ref, start):
    one, two = pair
    half, part = one.shape[0] - SPARE, one.shape[1] // 2

    @pl.when(texts)
    def _():
        out_ref[start : start + half, :part] = two[:half, :part]
        out_ref[start : start + half, part:] = one[:half, :part]
        out_ref[start + half : start + 2 * half, :part] = two[:half, part:]
        out_ref[start + half : start + 2 * half, part:] = one[:half, part:]

    @pl.when(jnp.logical_not(texts))
    def _():
        out_ref[start : start + half] = one[:half]
        out_ref[start + half : start + 2 * half] = two[:half]


def counts(pair, texts):
    one, two = pair
    half = one.shape[0] - SPARE
    line_one = one[half:, :LINE].astype(jnp.float32)[:1]
    line_two = two[half:, :LINE].astype(jnp.float32)[:1]
    images = jnp.concatenate([line_one[:, :half], line_two[:, :half]], axis=1)
    return jnp.where(texts, line_one[:, : 2 * half], images)


def upright(line):
    return jnp.transpose(jnp.broadcast_to(line, (8, line.shape[1])))[:, :1]


def sample_ids(col, texts, half, cols, axis):
    shape = (2 * half, 1) if axis == 0 else (1, 2 * half)
    at = lax.broadcasted_iota(jnp.int32, shape, axis)
    jump = jnp.where(texts, 0, (cols - 1) * half)
    first = col * jnp.where(texts, 2 * half, half)
    return at + first + jnp.where(at >= half, jump, 0)


def coefficients_of(cols, row_ref, col_ref, number_ref, mine, others, my_sets, other_sets):
    row, col = row_ref[0], col_ref[0]
    my_texts, other_texts = row != 0, row == 0
    near, far, other_near, other_far = masks(cols, row)
    my_masks = {"own": 0, "near": near, "far": far, "both": near ^ far}
    other_masks = {"own": 0, "near": other_near, "far": other_far, "both": other_near ^ other_far}
    half = my_sets[0][1][0].shape[0] - SPARE
    scale, bias, factor = (number_ref[n : n + 1, :1] for n in range(3))
    my_ids = jnp.concatenate([sample_ids(col ^ my_masks[k], my_texts, half, cols, 0) for k, _ in my_sets], axis=0)
    other_ids = jnp.concatenate(
        [sample_ids(col ^ other_masks[k], other_texts, half, cols, 1) for k, _ in other_sets], axis=1)
    my_weights = jnp.concatenate([upright(counts(pair, my_texts)) for _, pair in my_sets], axis=0)
    other_weights = factor * jnp.concatenate([counts(pair, other_texts) for _, pair in other_sets], axis=1)
    logits = lax.dot_general(mine, others, (((1,), (1,)), ((), ())), preferred_element_type=jnp.float32)
    logits = logits * scale + bias
    match = my_ids == other_ids
    rate = 1.0 / (1.0 + jnp.exp(jnp.where(match, logits, -logits)))
    return (jnp.where(match, -rate, rate) * my_weights * other_weights).astype(jnp.bfloat16)


def pairs(refs):
    return [refs[n : n + 2] for n in range(0, len(refs), 2)]


def number_kernel(scale_ref, bias_ref, grad_ref, sample_ref, out_ref):
    factor = grad_ref[0] * scale_ref[0] / sample_ref[0].astype(jnp.float32)
    line = lax.broadcasted_iota(jnp.int32, out_ref.shape, 0)
    out_ref[...] = jnp.where(line == 0, scale_ref[0], jnp.where(line == 1, bias_ref[0], factor))


def early_kernel(cols, row_ref, col_ref, number_ref, *refs):
    near, far, other_far = pairs(refs[:6])
    mine_ref, far_ref, total_ref = refs[6:]
    texts = row_ref[0] != 0
    size = far_ref.shape[0]
    unpack(near, texts, mine_ref, 0)
    unpack(far, texts, mine_ref, size)
    unpack(other_far, jnp.logical_not(texts), far_ref, 0)
    others = far_ref[...]
    coefficient = coefficients_of(cols, row_ref, col_ref, number_ref, mine_ref[...], others,
                                  [("near", near), ("far", far)], [("far", other_far)])
    total_ref[...] = jnp.dot(coefficient, others, preferred_element_type=jnp.float32)


def both_kernel(cols, row_ref, col_ref, number_ref, *refs):
    both, own, near, far = pairs(refs[:8])
    far_ref, others_ref, mine_ref, total_ref = refs[8:]
    texts = row_ref[0] != 0
    size = far_ref.shape[0]
    unpack(both, texts, mine_ref, 0)
    unpack(own, jnp.logical_not(texts), others_ref, 0)
    unpack(near, jnp.logical_not(texts), others_ref, size)
    others = jnp.concatenate([others_ref[...], far_ref[...]], axis=0)
    coefficient = coefficients_of(cols, row_ref, col_ref, number_ref, mine_ref[...], others, [("both", both)],
                                  [("own", own), ("near", near), ("far", far)])
    total_ref[...] = jnp.dot(coefficient, others, preferred_element_type=jnp.float32)


def pack_sum(total, texts, stay_ref, cross_ref):
    half, part = total.shape[0] // 2, total.shape[1] // 2

    @pl.when(texts)
    def _():
        stay_ref[:, :part] = total[:half, part:].astype(stay_ref.dtype)
        stay_ref[:, part:] = total[half:, part:].astype(stay_ref.dtype)
        cross_ref[:, :part] = total[:half, :part].astype(cross_ref.dtype)
        cross_ref[:, part:] = total[half:, :part].astype(cross_ref.dtype)

    @pl.when(jnp.logical_not(texts))
    def _():
        stay_ref[...] = total[:half].astype(stay_ref.dtype)
        cross_ref[...] = total[half:].astype(cross_ref.dtype)


def late_kernel(cols, row_ref, col_ref, number_ref, *refs):
    mine_pair, other_pair = refs[:2], refs[2:4]
    mine_ref, total_ref = refs[4:6]
    others_ref, stay_ref, cross_ref = refs[6:]
    texts = row_ref[0] != 0
    unpack(other_pair, jnp.logical_not(texts), others_ref, 0)
    others = others_ref[...]
    coefficient = coefficients_of(cols, row_ref, col_ref, number_ref, mine_ref[...], others,
                                  [("both", mine_pair)], [("both", other_pair)])
    total = total_ref[...] + jnp.dot(coefficient, others, preferred_element_type=jnp.float32)
    pack_sum(total, texts, stay_ref, cross_ref)


def far_kernel(cols, row_ref, col_ref, number_ref, *refs):
    far, own, near, both = pairs(refs[:8])
    mine_ref, early_ref, late_ref, total_ref, stay_ref, cross_ref = refs[8:]
    size = late_ref.shape[0]
    others = jnp.concatenate([early_ref[...], late_ref[...]], axis=0)
    coefficient = coefficients_of(cols, row_ref, col_ref, number_ref, mine_ref[size:], others, [("far", far)],
                                  [("own", own), ("near", near), ("both", both)])
    total = total_ref[size:] + jnp.dot(coefficient, others, preferred_element_type=jnp.float32)
    pack_sum(total, row_ref[0] != 0, stay_ref, cross_ref)


def rest_kernel(cols, row_ref, col_ref, number_ref, *refs):
    mine_near, mine_own, own, near, far, both = pairs(refs[:12])
    mine_ref, early_ref, far_ref, late_ref, total_ref = refs[12:17]
    own_stay, own_cross, near_stay, near_cross, own_rows = refs[17:]
    texts = row_ref[0] != 0
    size = late_ref.shape[0]
    unpack(mine_own, texts, own_rows, 0)
    others = jnp.concatenate([early_ref[...], late_ref[...]], axis=0)
    coefficient = coefficients_of(cols, row_ref, col_ref, number_ref, mine_ref[:size], others, [("near", mine_near)],
                                  [("own", own), ("near", near), ("both", both)])
    total = total_ref[:size] + jnp.dot(coefficient, others, preferred_element_type=jnp.float32)
    pack_sum(total, texts, near_stay, near_cross)
    others = jnp.concatenate([others, far_ref[...]], axis=0)
    coefficient = coefficients_of(cols, row_ref, col_ref, number_ref, own_rows[...], others, [("own", mine_own)],
                                  [("own", own), ("near", near), ("both", both), ("far", far)])
    pack_sum(jnp.dot(coefficient, others, preferred_element_type=jnp.float32), texts, own_stay, own_cross)


def last_kernel(row_ref, stay_ref, crossed_ref, near_stay_ref, near_cross_ref, image_ref, text_ref, images, texts, sems):
    half, part = text_ref.shape[0] // 2, text_ref.shape[1]

    def put(image_sums, text_sums):
        images[...] = (image_sums[0][...] + image_sums[1][...].astype(jnp.float32)).astype(images.dtype)
        image_out = pltpu.make_async_copy(images, image_ref, sems.at[0])
        image_out.start()
        rows = (text_sums[0][...] + text_sums[1][...].astype(jnp.float32)).astype(texts.dtype)
        texts[:half] = rows[:, :part]
        texts[half:] = rows[:, part:]
        text_out = pltpu.make_async_copy(texts, text_ref, sems.at[1])
        text_out.start()
        image_out.wait()
        text_out.wait()

    @pl.when(row_ref[0] == 0)
    def _():
        put((stay_ref, near_stay_ref), (crossed_ref, near_cross_ref))

    @pl.when(row_ref[0] != 0)
    def _():
        put((crossed_ref, near_cross_ref), (stay_ref, near_stay_ref))


def call(kernel, out_shape, smem, *arrays, flops=0, scratch=()):
    size = sum(a.size * a.dtype.itemsize for a in (*arrays, *jax.tree.leaves(out_shape)))
    return pl.pallas_call(
        kernel,
        out_shape=out_shape,
        in_specs=[pl.BlockSpec(memory_space=pltpu.SMEM)] * smem
        + [pl.BlockSpec(memory_space=pltpu.VMEM)] * (len(arrays) - smem),
        out_specs=jax.tree.map(lambda _: pl.BlockSpec(memory_space=pltpu.VMEM), out_shape),
        scratch_shapes=scratch,
        compiler_params=pltpu.CompilerParams(vmem_limit_bytes=24 * 1024 * 1024),
        cost_estimate=pl.CostEstimate(flops=flops, bytes_accessed=size, transcendentals=0),
    )(*arrays)


def pair_body(
    image_emb, text_emb, image_valid, text_valid, sample_count, logit_scale, logit_bias, loss_grad
):
    half, width = image_emb.shape
    size = 2 * half
    cols = lax.axis_size("col")
    row, col = lax.axis_index("row")[None], lax.axis_index("col")[None]
    near, far = masks(cols, None)

    def shape(rows, dtype):
        return jax.ShapeDtypeStruct((rows, width), dtype)

    bf16, f32 = jnp.bfloat16, jnp.float32
    sent = shape(half + SPARE, bf16)
    first = (image_emb, text_emb, image_valid[None], text_valid[None])
    own_a, give = pl.pallas_call(
        first_kernel,
        out_shape=(sent, sent),
        in_specs=[pl.BlockSpec(memory_space=pltpu.SMEM)] + [pl.BlockSpec(memory_space=pltpu.HBM)] * 4,
        out_specs=(pl.BlockSpec(memory_space=pltpu.VMEM),) * 2,
        scratch_shapes=[pltpu.VMEM(a.shape, a.dtype) for a in first[1:]] + [pltpu.SemaphoreType.DMA((4,))],
        compiler_params=pltpu.CompilerParams(vmem_limit_bytes=60 * 1024 * 1024),
    )(row, *first)
    far_a = hop(own_a, *far)
    own_b = swap(give)
    far_b = hop(own_b, *far)
    near_a = hop(own_a, *near)
    near_b = hop(own_b, *near)
    both_a = hop(far_a, *near)
    both_b = hop(far_b, *near)
    number = call(number_kernel, jax.ShapeDtypeStruct((8, 128), f32), 4, logit_scale, logit_bias, loss_grad, sample_count)
    far_a, number = lax.optimization_barrier((far_a, number))
    mine_own, mine_near, mine_far = (own_a, own_b), (near_a, near_b), (far_a, far_b)
    own, near_pair, far_pair = (swap(own_a), swap(own_b)), (swap(near_a), swap(near_b)), (swap(far_a), swap(far_b))
    other_both_a = swap(both_a)

    pair_flops = 4 * size * size * width
    scalars = (row, col, number)
    mine_rows, far_rows, early = call(
        functools.partial(early_kernel, cols), (shape(2 * size, bf16), shape(size, bf16), shape(2 * size, f32)), 2,
        *scalars, *mine_near, *mine_far, *far_pair, flops=2 * pair_flops)
    both_b, early = lax.optimization_barrier((both_b, early))
    both = (both_a, both_b)
    other_both = (other_both_a, swap(both_b))
    early_rows, both_rows, both_early = call(
        functools.partial(both_kernel, cols), (shape(2 * size, bf16), shape(size, bf16), shape(size, f32)), 2, *scalars,
        *both, *own, *near_pair, *far_pair, far_rows, flops=3 * pair_flops)
    late_rows, late_stay, late_cross = call(
        functools.partial(late_kernel, cols), (shape(size, bf16), shape(half, bf16), shape(half, bf16)), 2, *scalars,
        *both, *other_both, both_rows, both_early, flops=pair_flops)
    in_cross = hop(late_cross, *near)
    in_stay = hop(late_stay, *near)
    far_stay, far_cross = call(
        functools.partial(far_kernel, cols), (shape(half, f32), shape(half, f32)), 2, *scalars, *mine_far, *own,
        *near_pair, *other_both, mine_rows, early_rows, late_rows, early, flops=3 * pair_flops)
    own_stay, own_cross, near_stay, near_cross = call(
        functools.partial(rest_kernel, cols),
        (shape(half, f32), shape(half, f32), shape(half, bf16), shape(half, bf16)), 2, *scalars, *mine_near, *mine_own,
        *own, *near_pair, *far_pair, *other_both, mine_rows, early_rows, far_rows, late_rows, early,
        flops=7 * pair_flops, scratch=[pltpu.VMEM((size, width), bf16)])
    crossed = swap(own_cross)
    far_cross = (far_cross + in_cross.astype(f32)).astype(bf16)
    far_stay = (far_stay + in_stay.astype(f32)).astype(bf16)
    near_stay, _ = lax.optimization_barrier((near_stay, far_stay))
    near_stay = hop(near_stay, *near)
    near_cross, _, _ = lax.optimization_barrier((near_cross, far_cross, far_stay))
    far_cross = hop(far_cross, *far, across=True)
    far_stay = hop(far_stay, *far)
    near_cross = hop(near_cross, *near, across=True)
    own_stay = own_stay + far_stay.astype(f32)
    crossed = crossed + far_cross.astype(f32)
    outs = (shape(half, bf16), jax.ShapeDtypeStruct(text_emb.shape, bf16))
    return pl.pallas_call(
        last_kernel,
        out_shape=outs,
        in_specs=[pl.BlockSpec(memory_space=pltpu.SMEM)] + [pl.BlockSpec(memory_space=pltpu.VMEM)] * 4,
        out_specs=(pl.BlockSpec(memory_space=pltpu.HBM),) * 2,
        scratch_shapes=[pltpu.VMEM(out.shape, out.dtype) for out in outs] + [pltpu.SemaphoreType.DMA((2,))],
        compiler_params=pltpu.CompilerParams(vmem_limit_bytes=24 * 1024 * 1024),
    )(row, own_stay, crossed, near_stay, near_cross)


def partner(block, axis, distance):
    count = lax.axis_size(axis)
    route = []
    for low in range(count):
        high = low | 1 << distance
        if high != low and high < count:
            route += [(low, high), (high, low)]
    return lax.ppermute(block, axis, route)


def coefficients(
    image_rows, valid_rows, row_ids, texts, weight_text, text_ids, factor, logit_scale, logit_bias
):
    logits = lax.dot_general(
        image_rows, texts, (((1,), (1,)), ((), ())), preferred_element_type=jnp.float32
    )
    logits = logits * logit_scale[0] + logit_bias[0]
    label_sign = jnp.where(row_ids[:, None] == text_ids[None, :], 1.0, -1.0).astype(jnp.float32)
    weights = valid_rows.astype(jnp.float32)[:, None] * weight_text[None, :]
    return (-factor * label_sign * jax.nn.sigmoid(-label_sign * logits) * weights).astype(
        jnp.bfloat16
    )


def text_part(coefficient, image_rows):
    return lax.dot_general(
        coefficient, image_rows, (((0,), (0,)), ((), ())), preferred_element_type=jnp.float32
    )


def body(
    image_emb, text_emb, image_valid, text_valid, sample_count, logit_scale, logit_bias, loss_grad
):
    text_block = lax.all_gather(text_emb, "row", axis=1, tiled=True)
    per_device = image_emb.shape[0]
    col_count = lax.axis_size("col")
    col_index = lax.axis_index("col")
    row_index = lax.axis_index("row")
    text_count = text_block.shape[0]
    factor = loss_grad[0] * logit_scale[0] / sample_count[0].astype(jnp.float32)
    valid_wire = image_valid.astype(jnp.bfloat16)
    parity = col_index % 2
    bit_count = col_count.bit_length() - 1
    text_wire = text_valid.astype(jnp.bfloat16)
    other_texts, other_valid = partner((text_block, text_wire), "col", 0)
    own_first = parity == 0
    texts = jnp.where(
        own_first,
        jnp.concatenate([text_block, other_texts], 0),
        jnp.concatenate([other_texts, text_block], 0),
    )
    text_weights = jnp.where(
        own_first,
        jnp.concatenate([text_wire, other_valid], 0),
        jnp.concatenate([other_valid, text_wire], 0),
    ).astype(jnp.float32)
    text_ids = (col_index - parity) * text_count + jnp.arange(2 * text_count, dtype=jnp.int32)
    image_rows, valid_rows = (image_emb, valid_wire)
    for bit in range(1, bit_count):
        other_rows, other_counts = partner((image_rows, valid_rows), "col", bit)
        lower = col_index >> bit & 1 == 0
        image_rows = jnp.where(
            lower,
            jnp.concatenate([image_rows, other_rows], 0),
            jnp.concatenate([other_rows, image_rows], 0),
        )
        valid_rows = jnp.where(
            lower,
            jnp.concatenate([valid_rows, other_counts], 0),
            jnp.concatenate([other_counts, valid_rows], 0),
        )
    positions = jnp.arange(image_rows.shape[0], dtype=jnp.int32)
    row_ids = (
        row_index * col_count + 2 * (positions // per_device) + parity
    ) * per_device + positions % per_device
    coefficient = coefficients(
        image_rows,
        valid_rows,
        row_ids,
        texts,
        text_weights,
        text_ids,
        factor,
        logit_scale,
        logit_bias,
    )
    partial_image = jnp.dot(coefficient, texts, preferred_element_type=jnp.float32)
    for bit in range(bit_count - 1, 0, -1):
        half = partial_image.shape[0] // 2
        upper = col_index >> bit & 1 == 1
        send = jnp.where(upper, partial_image[:half], partial_image[half:])
        keep = jnp.where(upper, partial_image[half:], partial_image[:half])
        partial_image = keep + partner(send, "col", bit)
    partial_text = text_part(coefficient, image_rows)
    odd = parity == 1
    send_text = jnp.where(odd, partial_text[:text_count], partial_text[text_count:])
    keep_text = jnp.where(odd, partial_text[text_count:], partial_text[:text_count])
    text_partial = keep_text + partner(send_text, "col", 0)
    text_grad = lax.psum_scatter(text_partial, "row", scatter_dimension=1, tiled=True)
    return (partial_image.astype(jnp.bfloat16), text_grad.astype(jnp.bfloat16))


def solution(mesh):
    in_specs = (
        P(("row", "col"), None),
        P("col", "row"),
        P(("row", "col")),
        P("col"),
        P(),
        P(),
        P(),
        P(),
    )
    out_specs = (P(("row", "col"), None), P("col", "row"))
    paired = mesh.shape["row"] == 2 and mesh.shape["col"] == 16
    run = pair_body if paired else body
    return jax.shard_map(run, mesh=mesh, in_specs=in_specs, out_specs=out_specs, check_vma=False)
```
